32 devices in a mesh: row: 8 (over y, x, core), col: 4 (over z).
Axes of the slice: x: 2, y: 2, z: 4, core: 2. Of those that a mesh axis runs over, the one named last changes fastest.
Arguments:
- diag_tiles: float32 [32, 256, 256], P('row'), as said below
- left_fac: bfloat16 [32, 32, 256, 128], P('row', 'col'), as said below
- right_fac: bfloat16 [32, 32, 256, 128], P('row', 'col'), as said below
- ranks: int32 [32, 32], replicated, may hold values from 16 to 128, as said below
Outputs:
- factored: float32 [32, 32, 256, 256], P('row', 'col')
The draws below stay inside these ranges and needn't reach their ends.
Inputs may be any that keep to these rules, and one draw needn't show every extreme that they name: `ranks`: every entry is a multiple of 16; in every draw some tile below the diagonal has rank 128, and the mean rank is about a third of 128. `diag_tiles`: every tile is symmetric; the first diagonal tile and the updated second diagonal tile M are positive definite. `left_fac`: entries have mean zero and deviation one. `right_fac`: entries have mean zero and deviation one over the square root of 128.
All inputs are finite; a program needn't handle non-finite values.
Results may differ from the reference program's by a relative error of at most 0.0003.
Values sent between devices are 32-bit elements; how exact they have to be, the bound alone decides.
No kernel may reach another device: no remote copies, remote signals or barrier semaphores. Data moves between devices by JAX's collectives and lax.ppermute only.
A program may use at most 64 MiB of HBM per device.

```python
import math
import jax
import jax.numpy as jnp
from jax import lax

NT = 32
B = 256
RMAX = 128
GRID_ROWS = 8
GRID_COLS = 4


def draw_diag_tiles(key, part):
    base_key = jax.random.fold_in(key, 3)
    key_levels, key_jitter, key_links = jax.random.split(base_key, 3)
    levels = math.sqrt(B) * jnp.exp(jax.random.uniform(key_levels, (NT, B), jnp.float32, math.log(3.5), math.log(7.0)))
    jitter = 0.5 * jax.random.normal(key_jitter, (NT, B, B), jnp.float32)
    symmetric = 0.5 * (jitter + jnp.swapaxes(jitter, 1, 2))
    link_count = max(B // 4, 1)
    links = jax.random.randint(key_links, (NT, B, link_count), -2, 3).astype(jnp.int32)
    stiffness = jnp.einsum('nbk,nck->nbc', links, links).astype(jnp.float32)
    coupling = stiffness
    identity = jnp.eye(B, dtype=jnp.float32)
    return symmetric + coupling + identity[None, :, :] * levels[:, :, None]


def draw_left_fac(key, part):
    base_key = jax.random.fold_in(key, 11)
    values = jnp.clip(jax.random.normal(base_key, (NT, NT, B, RMAX), jnp.float32), -6.0, 6.0)
    return values.astype(jnp.bfloat16)


def draw_right_fac(key, part):
    base_key = jax.random.fold_in(key, 13)
    spread = 1.0 / math.sqrt(RMAX)
    values = spread * jnp.clip(jax.random.normal(base_key, (NT, NT, B, RMAX), jnp.float32), -6.0, 6.0)
    return values.astype(jnp.bfloat16)


def draw_ranks(key, part):
    base_key = jax.random.fold_in(key, 7)
    key_first, key_second, key_third, key_row, key_col = jax.random.split(base_key, 5)
    first = jax.random.randint(key_first, (NT, NT), 1, 9)
    second = jax.random.randint(key_second, (NT, NT), 1, 9)
    third = jax.random.randint(key_third, (NT, NT), 1, 9)
    levels = jnp.minimum(jnp.minimum(first, second), third)
    heavy_row = jax.random.randint(key_row, (), 1, NT)
    heavy_col = jax.random.randint(key_col, (), 0, NT) % heavy_row
    row_ids = jnp.arange(NT, dtype=jnp.int32)[:, None]
    col_ids = jnp.arange(NT, dtype=jnp.int32)[None, :]
    levels = jnp.where((row_ids == heavy_row) & (col_ids == heavy_col), 8, levels)
    return (levels * (RMAX // 8)).astype(jnp.int32)


def setup_inputs(seed: int = 0) -> dict:
    arg_keys = jax.random.split(jax.random.key(seed), 5)
    diag_tiles = draw_diag_tiles(jax.random.fold_in(arg_keys[4], 71), 0)
    left_fac = draw_left_fac(jax.random.fold_in(arg_keys[4], 71), 0)
    right_fac = draw_right_fac(jax.random.fold_in(arg_keys[4], 71), 0)
    ranks = draw_ranks(jax.random.fold_in(arg_keys[4], 71), 0)
    return dict(diag_tiles=diag_tiles, left_fac=left_fac, right_fac=right_fac, ranks=ranks)


PRECISE = lax.Precision.HIGHEST

def lower_solve(factor, stacked):
    pieces, tile_width, rank_cap = stacked.shape
    flattened = jnp.transpose(stacked, (1, 0, 2)).reshape(tile_width, pieces * rank_cap)
    solved = lax.linalg.triangular_solve(factor, flattened, left_side=True, lower=True)
    return jnp.transpose(solved.reshape(tile_width, pieces, rank_cap), (1, 0, 2))

def expand(left_basis, weights):
    return jnp.einsum('nbr,ncr->nbc', left_basis, weights, precision=PRECISE)

def reference(diag_tiles, left_fac, right_fac, ranks):
    row_slots = NT // GRID_ROWS
    col_slots = NT // GRID_COLS
    tile_index = jnp.arange(NT, dtype=jnp.int32)
    row_place = tile_index % GRID_ROWS * row_slots + tile_index // GRID_ROWS
    col_place = tile_index % GRID_COLS * col_slots + tile_index // GRID_COLS
    columns_live = jnp.arange(RMAX, dtype=jnp.int32)[None, None, :] < ranks[:, :, None]
    left_bases = jnp.where(columns_live[:, :, None, :], left_fac[row_place][:, col_place].astype(jnp.float32), 0.0)
    right_coefs = right_fac[row_place][:, col_place].astype(jnp.float32)
    diagonals = diag_tiles[row_place]
    first_pivot = jnp.linalg.cholesky(diagonals[0])
    first_basis = left_bases[:, 0]
    first_solved = lower_solve(first_pivot, right_coefs[:, 0])
    crossing = jnp.einsum('nbr,bs->nrs', first_solved, first_solved[1], precision=PRECISE)
    partial_term = jnp.matmul(first_basis[1], crossing[1], precision=PRECISE)
    shifted = diagonals[1] - jnp.matmul(partial_term, first_basis[1].T, precision=PRECISE)
    second_pivot = jnp.linalg.cholesky(shifted)
    head_basis = lax.linalg.triangular_solve(second_pivot, first_basis[1], left_side=True, lower=True)
    second_solved = lower_solve(second_pivot, right_coefs[:, 1])
    minus_term = -jnp.einsum('bs,nrs->nbr', head_basis, crossing, precision=PRECISE)
    panel_first = expand(first_basis, first_solved)
    panel_second = expand(left_bases[:, 1], second_solved) + expand(first_basis, minus_term)
    both_panels = jnp.concatenate([panel_first, panel_second], axis=2)

    def one_row(row_id):
        dense_front = jnp.einsum('jbr,jcr->jbc', left_bases[row_id], right_coefs[row_id], precision=PRECISE)
        updates = jnp.einsum('bk,jck->jbc', both_panels[row_id], both_panels, precision=PRECISE)
        schur = dense_front - updates
        col_ids = tile_index[:, None, None]
        chosen = jnp.where(col_ids == 0, panel_first[row_id][None], jnp.where(col_ids == 1, panel_second[row_id][None], schur))
        return jnp.where(col_ids < row_id, chosen, 0.0)
    natural = lax.map(one_row, tile_index)
    storage = jnp.arange(NT, dtype=jnp.int32)
    row_back = storage % row_slots * GRID_ROWS + storage // row_slots
    col_back = storage % col_slots * GRID_COLS + storage // col_slots
    return natural[row_back][:, col_back]
```

```python
import functools

import jax
import jax.numpy as jnp
from jax import lax
from jax.experimental import pallas as pl
from jax.experimental.pallas import tpu as pltpu
from jax.sharding import PartitionSpec as P

PRECISE = lax.Precision.HIGHEST
AXES = ("row", "col")
BLOCK = 32
GROUP = 8
LANES = 128
NT = (((1,), (1,)), ((), ()))
TN = (((0,), (0,)), ((), ()))
NN = (((1,), (0,)), ((), ()))
ANYWHERE = pl.BlockSpec(memory_space=pl.ANY)
IN_VMEM = pl.BlockSpec(memory_space=pltpu.VMEM)
IN_SMEM = pl.BlockSpec(memory_space=pltpu.SMEM)
VMEM_LIMIT = 48 * 1024 * 1024


def dot32(lhs, rhs, dims):
    return lax.dot_general(lhs, rhs, dims, precision=PRECISE, preferred_element_type=jnp.float32)


def dot16(lhs, rhs, dims):
    return lax.dot_general(lhs, rhs, dims, preferred_element_type=jnp.float32)


def split2(value):
    high = value.astype(jnp.bfloat16)
    low = (value - high.astype(jnp.float32)).astype(jnp.bfloat16)
    return high, low


def split3(value):
    high = value.astype(jnp.bfloat16)
    rest = value - high.astype(jnp.float32)
    middle = rest.astype(jnp.bfloat16)
    low = (rest - middle.astype(jnp.float32)).astype(jnp.bfloat16)
    return high, middle, low


def params(**extra):
    return pltpu.CompilerParams(vmem_limit_bytes=VMEM_LIMIT, **extra)


def cost(flops, moved):
    return pl.CostEstimate(flops=int(flops), bytes_accessed=int(moved), transcendentals=0)


def eliminate(tiles):
    tiles, start = tiles
    rows = tiles[0].shape[0]
    done = []
    for first in range(0, rows, GROUP):
        height = rows - first
        row_ids = lax.broadcasted_iota(jnp.int32, (height, LANES), 0)
        heads = [
            jnp.broadcast_to(tiles[0][:, start + first + j : start + first + j + 1], (height, LANES))
            for j in range(GROUP)
        ]
        scale = jnp.zeros((GROUP, LANES), jnp.float32)
        for j in range(GROUP):
            pivot = heads[j][j : j + 1, :]
            factor = jnp.where(row_ids > j, heads[j] * (1.0 / pivot), 0.0)
            for other in range(j + 1, GROUP):
                heads[other] = heads[other] - factor * heads[other][j : j + 1, :]
            tiles = [tile - factor * tile[j : j + 1, :] for tile in tiles]
            root = lax.rsqrt(pivot)
            root = root * (1.5 - 0.5 * pivot * root * root)
            scale = jnp.where(row_ids[:GROUP] == j, root, scale)
        done.append([tile[:GROUP] * scale for tile in tiles])
        tiles = [tile[GROUP:] for tile in tiles]
    return [jnp.concatenate(parts, axis=0) for parts in zip(*done)]


def inverse_factor(source, work, result):
    order = source.shape[0]
    span = order // LANES
    for base in range(0, order, BLOCK):
        low = base // LANES
        row_ids = lax.broadcasted_iota(jnp.int32, (BLOCK, LANES), 0)
        lane_ids = lax.broadcasted_iota(jnp.int32, (BLOCK, LANES), 1)
        unit = jnp.where(lane_ids - base % LANES == row_ids, 1.0, 0.0)
        zero = jnp.zeros((BLOCK, LANES), jnp.float32)
        tiles = [source[base : base + BLOCK, s * LANES : (s + 1) * LANES] for s in range(low, span)]
        tiles += [zero] * low + [unit]
        if base:
            taken = dot32(
                work[0:base, base : base + BLOCK],
                work[0:base, low * LANES : order + (low + 1) * LANES],
                TN,
            )
            tiles = [tile - taken[:, s * LANES : (s + 1) * LANES] for s, tile in enumerate(tiles)]
        tiles = eliminate((tiles, base % LANES))
        for s, tile in enumerate(tiles):
            work[base : base + BLOCK, (low + s) * LANES : (low + s + 1) * LANES] = tile
        for s in range(low + 1, span):
            work[base : base + BLOCK, order + s * LANES : order + (s + 1) * LANES] = zero
    result[...] = work[:, order:]


def first_kernel(tile, result, work):
    inverse_factor(tile, work, result)


def first_inverse(tile):
    order = tile.shape[0]
    return pl.pallas_call(
        first_kernel,
        out_shape=jax.ShapeDtypeStruct((order, order), jnp.float32),
        in_specs=[IN_VMEM],
        out_specs=IN_VMEM,
        scratch_shapes=[pltpu.VMEM((order, 2 * order), jnp.float32)],
        compiler_params=params(),
        cost_estimate=cost(2**33, 2**20),
        name="first_inverse",
    )(tile)


def second_kernel(rank, head, inverse, result, mixing, shifted, work):
    order = inverse.shape[0]
    cap = (head.shape[0] - order) // 2
    live = lax.broadcasted_iota(jnp.int32, (cap, order), 0) < rank[0]
    left = jnp.where(live, head[order : order + cap, :], 0.0)
    right = jnp.where(live, head[order + cap :, :], 0.0)
    solved = dot32(right, inverse[...], NT)
    dense = dot32(left, solved, TN)
    shifted[...] = head[0:order, :] - dot32(dense, dense, NT)
    inverse_factor(shifted, work, result)
    mixing[...] = -dot32(dot32(result[...], dense, NN), inverse[...], NN)


def second_inverse(rank, head, inverse):
    order = inverse.shape[0]
    shape = jax.ShapeDtypeStruct((order, order), jnp.float32)
    return pl.pallas_call(
        second_kernel,
        out_shape=(shape, shape),
        in_specs=[IN_SMEM, IN_VMEM, IN_VMEM],
        out_specs=(IN_VMEM, IN_VMEM),
        scratch_shapes=[
            pltpu.VMEM((order, order), jnp.float32),
            pltpu.VMEM((order, 2 * order), jnp.float32),
        ],
        compiler_params=params(),
        cost_estimate=cost(2**33, 2**20),
        name="second_inverse",
    )(rank, head, inverse)


def pack_kernel(capacity, offsets, ranks, left, right, left_out, right_out):
    slots, _, order, cap = left.shape
    place = lax.broadcasted_iota(jnp.int32, (capacity, cap), 0)
    column = lax.broadcasted_iota(jnp.int32, (capacity, cap), 1)
    for source, target in ((left, left_out), (right, right_out)):
        total = jnp.zeros((capacity, order), jnp.float32)
        for slot in range(slots):
            hit = (place - offsets[slot] == column) & (column < ranks[slot])
            chosen = jnp.where(hit, 1.0, 0.0).astype(jnp.bfloat16)
            total = total + dot16(chosen, source[slot, 0], NT)
        target[...] = total


def pack(left_fac, right_fac, offsets, ranks, capacity):
    slots, _, order, cap = left_fac.shape
    shape = jax.ShapeDtypeStruct((capacity, order), jnp.float32)
    block = pl.BlockSpec((slots, 1, order, cap), lambda step: (0, 0, 0, 0))
    whole = pl.BlockSpec((capacity, order), lambda step: (0, 0))
    return pl.pallas_call(
        functools.partial(pack_kernel, capacity),
        grid=(1,),
        out_shape=(shape, shape),
        in_specs=[IN_SMEM, IN_SMEM, block, block],
        out_specs=(whole, whole),
        compiler_params=params(),
        cost_estimate=cost(2**28, 2**20),
        name="pack",
    )(offsets, ranks, left_fac, right_fac)


def panel_kernel(capacity, groups, factors, choice, offsets, ranks, *refs):
    total = sum(sum(counts) for counts in groups)
    sources, (first, second, mixing) = refs[:total], refs[total : total + 3]
    high_out, low_out = refs[total + 3 : total + 5]
    landed, weight_high, weight_low, sems = refs[total + 5 :]
    order = first.shape[0]
    cap = LANES
    slots = offsets.shape[1] // 2
    at = 0
    waits = []
    for g, counts in enumerate(groups):
        for k, count in enumerate(counts):
            candidates = sources[at : at + count]
            at += count
            spot = landed.at[4 * g + k, pl.ds(0, capacity)]
            for n, candidate in enumerate(candidates):
                copy = pltpu.make_async_copy(candidate, spot, sems.at[4 * g + k])
                if count == 1:
                    copy.start()
                else:
                    pl.when(choice[4 * g + k] == n)(copy.start)
            waits.append(pltpu.make_async_copy(candidates[0], spot, sems.at[4 * g + k]))
            landed[4 * g + k, capacity:, :] = jnp.zeros((cap, order), jnp.float32)
    base = jnp.concatenate([first[...], mixing[...]], axis=0)
    base_parts, second_parts = split3(base), split3(second[...])
    for wait in waits:
        wait.wait()
    for g in range(len(groups)):
        right0 = landed[4 * g + 1].astype(jnp.bfloat16)
        right1 = landed[4 * g + 3].astype(jnp.bfloat16)
        solved0 = sum(dot16(right0, part, NT) for part in base_parts)
        solved1 = sum(dot16(right1, part, NT) for part in second_parts)
        for column, value in ((0, solved0), (2 * order, solved1)):
            high, low = split2(value)
            weight_high[:, column : column + value.shape[1]] = high
            weight_low[:, column : column + value.shape[1]] = low
        live = lax.broadcasted_iota(jnp.int32, (cap, order), 0)
        for slot in range(slots):
            pieces = []
            for k in range(2):
                spot = pl.ds(pl.multiple_of(offsets[g, k * slots + slot], 16), cap)
                left = landed[4 * g + 2 * k, spot, :]
                left = jnp.where(live < ranks[g, k * slots + slot], left, 0.0).astype(jnp.bfloat16)
                columns = pl.ds(0, 2 * order) if k == 0 else pl.ds(2 * order, order)
                weights = jnp.concatenate([weight_high[spot, columns], weight_low[spot, columns]], axis=0)
                pieces.append(dot16(jnp.concatenate([left, left], axis=0), weights, TN))
            panel0 = pieces[0][:, :order]
            panel1 = pieces[0][:, order:] + pieces[1]
            where = slot if factors is None else slot * factors + choice[4 * len(groups) + g]
            for column, value in ((0, panel0), (order, panel1)):
                high, low = split2(value)
                high_out[where, :, column : column + order] = high
                low_out[where, :, column : column + order] = low


def panels(groups, choice, offsets, ranks, inverses, capacity, name):
    order = inverses[0].shape[0]
    count = len(groups)
    slots = offsets.shape[1] // 2
    flat = [array for group in groups for candidates in group for array in candidates]
    counts = tuple(tuple(len(candidates) for candidates in group) for group in groups)
    shape = jax.ShapeDtypeStruct((slots * count, order, 2 * order), jnp.bfloat16)
    return pl.pallas_call(
        functools.partial(panel_kernel, capacity, counts, count if count > 1 else None),
        out_shape=(shape, shape),
        in_specs=[IN_SMEM] * 3 + [ANYWHERE] * len(flat) + [IN_VMEM] * 3,
        out_specs=(IN_VMEM, IN_VMEM),
        scratch_shapes=[
            pltpu.VMEM((4 * count, capacity + LANES, order), jnp.float32),
            pltpu.VMEM((capacity + LANES, 3 * order), jnp.bfloat16),
            pltpu.VMEM((capacity + LANES, 3 * order), jnp.bfloat16),
            pltpu.SemaphoreType.DMA((4 * count,)),
        ],
        compiler_params=params(),
        cost_estimate=cost(2**31 * count, 2**22 * count),
        name=name,
    )(choice, offsets, ranks, *flat, *inverses)


def schur_kernel(place, ranks, left, right, row_high, row_low, col_high, col_low, out):
    row_slot, col_slot = pl.program_id(0), pl.program_id(1)
    tile_row = row_slot * place[2] + place[0]
    tile_col = col_slot * place[3] + place[1]
    order = out.shape[2]

    @pl.when(tile_row <= tile_col)
    def _():
        out[0, 0] = jnp.zeros((order, order), jnp.float32)

    @pl.when((tile_row > tile_col) & (tile_col == 0))
    def _():
        out[0, 0] = row_high[row_slot, :, :order].astype(jnp.float32) + row_low[row_slot, :, :order].astype(jnp.float32)

    @pl.when((tile_row > tile_col) & (tile_col == 1))
    def _():
        out[0, 0] = row_high[row_slot, :, order:].astype(jnp.float32) + row_low[row_slot, :, order:].astype(jnp.float32)

    @pl.when((tile_row > tile_col) & (tile_col > 1))
    def _():
        basis = left[0, 0]
        live = lax.broadcasted_iota(jnp.int32, basis.shape, 1) < ranks[row_slot, col_slot]
        basis = jnp.where(live, basis.astype(jnp.float32), 0.0).astype(jnp.bfloat16)
        front = dot16(basis, right[0, 0], NT)
        high, low = row_high[row_slot], row_low[row_slot]
        update = dot16(high, col_high[col_slot], NT)
        update = update + dot16(high, col_low[col_slot], NT)
        update = update + dot16(low, col_high[col_slot], NT)
        out[0, 0] = front - update


def schur(place, ranks, left_fac, right_fac, rows, cols):
    row_slots, col_slots, order, cap = left_fac.shape
    factor = pl.BlockSpec((1, 1, order, cap), lambda a, m: (a, m, 0, 0))
    return pl.pallas_call(
        schur_kernel,
        grid=(row_slots, col_slots),
        out_shape=jax.ShapeDtypeStruct((row_slots, col_slots, order, order), jnp.float32),
        in_specs=[IN_SMEM, IN_SMEM, factor, factor] + [IN_VMEM] * 4,
        out_specs=pl.BlockSpec((1, 1, order, order), lambda a, m: (a, m, 0, 0)),
        compiler_params=params(dimension_semantics=("arbitrary", "arbitrary")),
        cost_estimate=cost(2**33, 2**24),
        name="schur",
    )(place, ranks, left_fac, right_fac, *rows, *cols)


def shards(diag_tiles, left_fac, right_fac, ranks):
    grid_rows = lax.axis_size("row")
    grid_cols = lax.axis_size("col")
    row_here = lax.axis_index("row")
    col_here = lax.axis_index("col")
    row_slots, col_slots, order, cap = left_fac.shape
    assert cap == LANES and grid_rows % grid_cols == 0 and grid_cols >= 2
    spread = grid_rows // grid_cols
    row_bits = grid_rows.bit_length() - 1
    low_bits = grid_cols.bit_length() - 1
    assert 1 << row_bits == grid_rows and 1 << low_bits == grid_cols
    capacity = row_slots * cap

    def move(array, pairs):
        flat = [(r * grid_cols + c, s * grid_cols + d) for (r, c), (s, d) in pairs]
        return lax.ppermute(array, AXES, flat)

    every_row = range(grid_rows)
    every_col = range(grid_cols)

    tile_ids = jnp.arange(ranks.shape[0], dtype=jnp.int32)
    panel_ranks = jnp.stack([jnp.where(tile_ids > t, ranks[:, t], 0) for t in range(2)])
    panel_ranks = panel_ranks.reshape(2, row_slots, grid_rows)
    starts = jnp.broadcast_to(jnp.arange(row_slots, dtype=jnp.int32)[None, :, None] * cap, panel_ranks.shape)

    def of_group(table, group):
        return lax.dynamic_index_in_dim(table, group, 2, keepdims=False)

    my_ranks = of_group(panel_ranks, row_here)
    my_starts = of_group(starts, row_here)
    panel_here = jnp.minimum(col_here, 1)
    left_pack, right_pack = pack(
        left_fac,
        right_fac,
        lax.dynamic_index_in_dim(my_starts, panel_here, 0, keepdims=False),
        lax.dynamic_index_in_dim(my_ranks, panel_here, 0, keepdims=False),
        capacity,
    )

    tree_bits = list(range(1, row_bits)) + [0]

    def spread_rows(array, root):
        held = [root]
        for bit in tree_bits:
            step = 1 << bit
            got = move(array, [((r, c), (r ^ step, c)) for r in held for c in every_col])
            mask = sum(1 << b for b in range(row_bits) if all((h ^ root) >> b & 1 == 0 for h in held) and b != bit)
            arrived = (((row_here ^ root) & mask) == 0) & (((row_here ^ root) >> bit) & 1 == 1)
            array = jnp.where(arrived, got, array)
            held = held + [r ^ step for r in held]
        return array

    first_tile = spread_rows(diag_tiles[0], 0)

    pivot_bases = jnp.concatenate([left_pack[:cap], right_pack[:cap]], axis=0)
    received = [move(pivot_bases, [((1, 0), (1, c))]) for c in every_col if c]
    pivot_bases = jnp.where(col_here == 0, pivot_bases, sum(received))
    head = spread_rows(jnp.concatenate([diag_tiles[0], pivot_bases], axis=0), 1)

    chains = []
    for array in (left_pack, right_pack):
        back = move(array, [((r, 1), (r, 0)) for r in every_row])
        chain = [array]
        for s in range(1, grid_cols):
            pairs = [((r, c - 1), (r, c)) for c in (s, s + 1) if c < grid_cols for r in every_row]
            chain.append(move(chain[-1], pairs))
        chains.append((chain, back))

    def pick(index, arrays):
        out = arrays[0]
        for n in range(1, len(arrays)):
            out = jnp.where(index == n, arrays[n], out)
        return out

    row_arrays = []
    for t in range(2):
        for chain, back in chains:
            row_arrays.append(chain if t == 0 else [back] + chain[:-1])

    inverse0 = first_inverse(first_tile)
    inverse1, mixing = second_inverse(ranks[1, 0][None], head, inverse0)
    inverses = (inverse0, inverse1, mixing)

    col_arrays = []
    for candidates in row_arrays:
        have = pick(col_here, candidates)
        held = {c: [c] for c in every_col}
        for bit in range(1, low_bits):
            step = 1 << bit
            pairs = [((r + h * grid_cols, c), ((r ^ step) + h * grid_cols, c)) for c in every_col for r in held[c] for h in range(spread)]
            got = move(have, pairs)
            mask = (grid_cols - 1) - sum(1 << b for b in range(1, bit + 1))
            offset = (row_here ^ col_here) & (grid_cols - 1)
            arrived = ((offset & mask) == 0) & ((offset >> bit) & 1 == 1)
            have = jnp.where(arrived, got, have)
            held = {c: held[c] + [r ^ step for r in held[c]] for c in every_col}
        sets = [have]
        for bit in range(low_bits, row_bits):
            step = 1 << bit
            pairs = [((r + h * grid_cols, c), ((r + h * grid_cols) ^ step, c)) for c in every_col for r in held[c] for h in range(spread)]
            sets = sets + [move(array, pairs) for array in sets]
        pairs = [((r + h * grid_cols, c), ((r ^ 1) + h * grid_cols, c)) for c in every_col for r in held[c] for h in range(spread)]
        col_arrays.append([[array, move(array, pairs)] for array in sets])

    row_group = my_starts.reshape(1, -1), my_ranks.reshape(1, -1)
    rows = panels(
        [row_arrays],
        jnp.full((5,), col_here, jnp.int32),
        *row_group,
        inverses,
        capacity,
        "row_panels",
    )
    mine = row_here // grid_cols
    groups = [(mine ^ g) * grid_cols + col_here for g in range(spread)]
    col_starts = jnp.stack([of_group(starts, group).reshape(-1) for group in groups])
    col_ranks = jnp.stack([of_group(panel_ranks, group).reshape(-1) for group in groups])
    passed = (row_here ^ col_here) & 1
    choice = jnp.concatenate(
        [jnp.full((4 * spread,), passed, jnp.int32), jnp.stack([mine ^ g for g in range(spread)]).astype(jnp.int32)]
    )
    cols = panels(
        [[col_arrays[k][g] for k in range(4)] for g in range(spread)],
        choice,
        col_starts,
        col_ranks,
        inverses,
        capacity,
        "col_panels",
    )
    place = jnp.stack([row_here, col_here, jnp.int32(grid_rows), jnp.int32(grid_cols)]).astype(jnp.int32)
    tile_rows = jnp.arange(row_slots, dtype=jnp.int32) * grid_rows + row_here
    tile_cols = jnp.arange(col_slots, dtype=jnp.int32) * grid_cols + col_here
    local_ranks = jnp.take(jnp.take(ranks, tile_rows, axis=0), tile_cols, axis=1)
    return schur(place, local_ranks, left_fac, right_fac, rows, cols)


def solution(mesh):
    in_specs = (P("row", None, None), P("row", "col", None, None), P("row", "col", None, None), P())
    out_specs = P("row", "col", None, None)
    return jax.shard_map(shards, mesh=mesh, in_specs=in_specs, out_specs=out_specs, check_vma=False)
```

```python
import functools

import jax
import jax.numpy as jnp
from jax import lax
from jax.experimental import pallas as pl
from jax.experimental.pallas import tpu as pltpu
from jax.sharding import PartitionSpec as P

PRECISE = lax.Precision.HIGHEST
AXES = ("row", "col")
BLOCK = 32
GROUP = 8
LANES = 128
NT = (((1,), (1,)), ((), ()))
TN = (((0,), (0,)), ((), ()))
NN = (((1,), (0,)), ((), ()))
ANYWHERE = pl.BlockSpec(memory_space=pl.ANY)
IN_VMEM = pl.BlockSpec(memory_space=pltpu.VMEM)
IN_SMEM = pl.BlockSpec(memory_space=pltpu.SMEM)
IN_HBM = pl.BlockSpec(memory_space=pltpu.HBM)
VMEM_LIMIT = 48 * 1024 * 1024


def dot32(lhs, rhs, dims):
    return lax.dot_general(lhs, rhs, dims, precision=PRECISE, preferred_element_type=jnp.float32)


def dot16(lhs, rhs, dims):
    return lax.dot_general(lhs, rhs, dims, preferred_element_type=jnp.float32)


def split2(value):
    high = value.astype(jnp.bfloat16)
    low = (value - high.astype(jnp.float32)).astype(jnp.bfloat16)
    return high, low


def split3(value):
    high = value.astype(jnp.bfloat16)
    rest = value - high.astype(jnp.float32)
    middle = rest.astype(jnp.bfloat16)
    low = (rest - middle.astype(jnp.float32)).astype(jnp.bfloat16)
    return high, middle, low


def params(**extra):
    return pltpu.CompilerParams(vmem_limit_bytes=VMEM_LIMIT, **extra)


def cost(flops, moved):
    return pl.CostEstimate(flops=int(flops), bytes_accessed=int(moved), transcendentals=0)


def eliminate(tiles):
    tiles, start = tiles
    rows = tiles[0].shape[0]
    done = []
    for first in range(0, rows, GROUP):
        height = rows - first
        row_ids = lax.broadcasted_iota(jnp.int32, (height, LANES), 0)
        heads = [
            jnp.broadcast_to(tiles[0][:, start + first + j : start + first + j + 1], (height, LANES))
            for j in range(GROUP)
        ]
        scale = jnp.zeros((GROUP, LANES), jnp.float32)
        for j in range(GROUP):
            pivot = heads[j][j : j + 1, :]
            factor = jnp.where(row_ids > j, heads[j] * (1.0 / pivot), 0.0)
            for other in range(j + 1, GROUP):
                heads[other] = heads[other] - factor * heads[other][j : j + 1, :]
            tiles = [tile - factor * tile[j : j + 1, :] for tile in tiles]
            root = lax.rsqrt(pivot)
            root = root * (1.5 - 0.5 * pivot * root * root)
            scale = jnp.where(row_ids[:GROUP] == j, root, scale)
        done.append([tile[:GROUP] * scale for tile in tiles])
        tiles = [tile[GROUP:] for tile in tiles]
    return [jnp.concatenate(parts, axis=0) for parts in zip(*done)]


def inverse_factor(source, work, result):
    order = source.shape[0]
    span = order // LANES
    for base in range(0, order, BLOCK):
        low = base // LANES
        row_ids = lax.broadcasted_iota(jnp.int32, (BLOCK, LANES), 0)
        lane_ids = lax.broadcasted_iota(jnp.int32, (BLOCK, LANES), 1)
        unit = jnp.where(lane_ids - base % LANES == row_ids, 1.0, 0.0)
        zero = jnp.zeros((BLOCK, LANES), jnp.float32)
        tiles = [source[base : base + BLOCK, s * LANES : (s + 1) * LANES] for s in range(low, span)]
        tiles += [zero] * low + [unit]
        if base:
            taken = dot32(
                work[0:base, base : base + BLOCK],
                work[0:base, low * LANES : order + (low + 1) * LANES],
                TN,
            )
            tiles = [tile - taken[:, s * LANES : (s + 1) * LANES] for s, tile in enumerate(tiles)]
        tiles = eliminate((tiles, base % LANES))
        for s, tile in enumerate(tiles):
            work[base : base + BLOCK, (low + s) * LANES : (low + s + 1) * LANES] = tile
        for s in range(low + 1, span):
            work[base : base + BLOCK, order + s * LANES : order + (s + 1) * LANES] = zero
    result[...] = work[:, order:]


def fetch(choice, candidates, target, sem):
    for n, candidate in enumerate(candidates):
        copy = pltpu.make_async_copy(candidate, target, sem)
        pl.when(choice == n)(copy.start)
    return pltpu.make_async_copy(candidates[0], target, sem).wait


def first_kernel(place, own, got, result, tile, work, sem):
    order = tile.shape[0]
    mine, other = own.at[pl.ds(0, order)], got.at[pl.ds(0, order)]
    fetch(place[0] % 2, (mine, other), tile, sem)()
    inverse_factor(tile, work, result)


def first_inverse(place, own, got):
    order = own.shape[1]
    return pl.pallas_call(
        first_kernel,
        out_shape=jax.ShapeDtypeStruct((order, order), jnp.float32),
        in_specs=[IN_SMEM, ANYWHERE, ANYWHERE],
        out_specs=IN_VMEM,
        scratch_shapes=[
            pltpu.VMEM((order, order), jnp.float32),
            pltpu.VMEM((order, 2 * order), jnp.float32),
            pltpu.SemaphoreType.DMA,
        ],
        compiler_params=params(),
        cost_estimate=cost(2**33, 2**20),
        name="first_inverse",
    )(place, own, got)


def second_kernel(place, ranks, own, got, inverse, result, mixing, head, work, sem):
    order = inverse.shape[0]
    cap = (head.shape[0] - order) // 2
    fetch(1 - place[0] % 2, (own, got), head, sem)()
    live = lax.broadcasted_iota(jnp.int32, (cap, order), 0) < ranks[1, 0]
    left = jnp.where(live, head[order : order + cap, :], 0.0)
    right = jnp.where(live, head[order + cap :, :], 0.0)
    solved = dot32(right, inverse[...], NT)
    dense = dot32(left, solved, TN)
    shifted = head.at[pl.ds(0, order)]
    shifted[...] = shifted[...] - dot32(dense, dense, NT)
    inverse_factor(shifted, work, result)
    mixing[...] = -dot32(dot32(result[...], dense, NN), inverse[...], NN)


def second_inverse(place, ranks, own, got, inverse):
    order = inverse.shape[0]
    shape = jax.ShapeDtypeStruct((order, order), jnp.float32)
    return pl.pallas_call(
        second_kernel,
        out_shape=(shape, shape),
        in_specs=[IN_SMEM, IN_SMEM, ANYWHERE, ANYWHERE, IN_VMEM],
        out_specs=(IN_VMEM, IN_VMEM),
        scratch_shapes=[
            pltpu.VMEM(own.shape, jnp.float32),
            pltpu.VMEM((order, 2 * order), jnp.float32),
            pltpu.SemaphoreType.DMA,
        ],
        compiler_params=params(),
        cost_estimate=cost(2**33, 2**20),
        name="second_inverse",
    )(place, ranks, own, got, inverse)


def segment(ranks, panel, group, slot, slots, grid_rows):
    start, count = jnp.int32(0), jnp.int32(0)
    for s in range(slots):
        tile_row = s * grid_rows + group
        rank = jnp.where(tile_row > panel, ranks[tile_row, panel], 0)
        start = start + jnp.where(s < slot, rank, 0)
        count = count + jnp.where(s == slot, rank, 0)
    return start, count


def pack_kernel(capacity, grid_rows, place, ranks, left, right, packed, pivot, held, sem):
    slots, order, cap = held.shape[1:]
    copies = [
        pltpu.make_async_copy(source.at[:, 0], held.at[k], sem.at[k]) for k, source in enumerate((left, right))
    ]
    for copy in copies:
        copy.start()
    panel = jnp.minimum(place[1], 1)
    spot = lax.broadcasted_iota(jnp.int32, (capacity, cap), 0)
    column = lax.broadcasted_iota(jnp.int32, (capacity, cap), 1)
    chosen = []
    for slot in range(slots):
        start, count = segment(ranks, panel, place[0], slot, slots, grid_rows)
        hit = (spot - start == column) & (column < count)
        chosen.append(jnp.where(hit, 1.0, 0.0).astype(jnp.bfloat16))
    for k, copy in enumerate(copies):
        copy.wait()
        total = sum(dot16(chosen[slot], held[k, slot], NT) for slot in range(slots))
        packed[k * capacity : (k + 1) * capacity, :] = total
        pivot[k * cap : (k + 1) * cap, :] = total[:cap]


def pack(place, ranks, left_fac, right_fac, capacity, grid_rows):
    slots, _, order, cap = left_fac.shape
    return pl.pallas_call(
        functools.partial(pack_kernel, capacity, grid_rows),
        out_shape=(
            jax.ShapeDtypeStruct((2 * capacity, order), jnp.float32),
            jax.ShapeDtypeStruct((2 * cap, order), jnp.float32),
        ),
        in_specs=[IN_SMEM, IN_SMEM, IN_HBM, IN_HBM],
        out_specs=(IN_VMEM, IN_VMEM),
        scratch_shapes=[pltpu.VMEM((2, slots, order, cap), jnp.bfloat16), pltpu.SemaphoreType.DMA((2,))],
        compiler_params=params(),
        cost_estimate=cost(2**28, 2**20),
        name="pack",
    )(place, ranks, left_fac, right_fac)


def pick_kernel(count, index, *refs):
    candidates, target, sem = refs[:count], refs[count], refs[count + 1]
    wait = fetch(index[0], candidates, target, sem)
    pl.when(index[0] >= 0)(wait)


def pick(index, candidates):
    return pl.pallas_call(
        functools.partial(pick_kernel, len(candidates)),
        out_shape=jax.ShapeDtypeStruct(candidates[0].shape, candidates[0].dtype),
        in_specs=[IN_SMEM] + [ANYWHERE] * len(candidates),
        out_specs=ANYWHERE,
        scratch_shapes=[pltpu.SemaphoreType.DMA],
        compiler_params=params(),
        cost_estimate=cost(0, 2 * candidates[0].size * 4),
        name="pick",
    )(jnp.reshape(index, (1,)).astype(jnp.int32), *candidates)


def rows_kernel(capacity, grid_rows, count, place, ranks, *refs):
    sources, (first, second, mixing), stacked = refs[: 2 * count], refs[2 * count : 2 * count + 3], refs[2 * count + 3]
    landed, weight_high, weight_low, sems = refs[2 * count + 4 :]
    order = first.shape[0]
    slots = stacked.shape[0]
    cap = LANES
    waits = []
    for t in range(2):
        for k in range(2):
            part = [source.at[pl.ds(k * capacity, capacity)] for source in sources[t * count : (t + 1) * count]]
            waits.append(fetch(place[1], part, landed.at[2 * t + k, pl.ds(0, capacity)], sems.at[2 * t + k]))
            landed[2 * t + k, capacity:, :] = jnp.zeros((cap, order), jnp.float32)
    base = jnp.concatenate([first[...], mixing[...]], axis=0)
    base_parts, second_parts = split3(base), split3(second[...])
    for wait in waits:
        wait()
    solved0 = sum(dot16(landed[1].astype(jnp.bfloat16), part, NT) for part in base_parts)
    solved1 = sum(dot16(landed[3].astype(jnp.bfloat16), part, NT) for part in second_parts)
    for column, value in ((0, solved0), (2 * order, solved1)):
        high, low = split2(value)
        weight_high[:, column : column + value.shape[1]] = high
        weight_low[:, column : column + value.shape[1]] = low
    live = lax.broadcasted_iota(jnp.int32, (cap, order), 0)
    for slot in range(slots):
        pieces = []
        for t in range(2):
            start, rank = segment(ranks, t, place[0], slot, slots, grid_rows)
            spot = pl.ds(pl.multiple_of(start, 16), cap)
            left = jnp.where(live < rank, landed[2 * t, spot, :], 0.0).astype(jnp.bfloat16)
            columns = pl.ds(0, 2 * order) if t == 0 else pl.ds(2 * order, order)
            weights = jnp.concatenate([weight_high[spot, columns], weight_low[spot, columns]], axis=0)
            pieces.append(dot16(jnp.concatenate([left, left], axis=0), weights, TN))
        for column, value in ((0, pieces[0][:, :order]), (order, pieces[0][:, order:] + pieces[1])):
            high, low = split2(value)
            stacked[slot, :order, column : column + order] = high
            stacked[slot, order:, column : column + order] = low


def row_panels(place, ranks, firsts, seconds, inverses, capacity, slots, grid_rows):
    order = inverses[0].shape[0]
    count = len(firsts)
    return pl.pallas_call(
        functools.partial(rows_kernel, capacity, grid_rows, count),
        out_shape=jax.ShapeDtypeStruct((slots, 2 * order, 2 * order), jnp.bfloat16),
        in_specs=[IN_SMEM] * 2 + [ANYWHERE] * (2 * count) + [IN_VMEM] * 3,
        out_specs=IN_VMEM,
        scratch_shapes=[
            pltpu.VMEM((4, capacity + LANES, order), jnp.float32),
            pltpu.VMEM((capacity + LANES, 3 * order), jnp.bfloat16),
            pltpu.VMEM((capacity + LANES, 3 * order), jnp.bfloat16),
            pltpu.SemaphoreType.DMA((4,)),
        ],
        compiler_params=params(),
        cost_estimate=cost(2**32, 2**22),
        name="row_panels",
    )(place, ranks, *firsts, *seconds, *inverses)


def schur_kernel(capacity, grid_rows, grid_cols, place, ranks, *refs):
    spread = grid_rows // grid_cols
    sources = refs[: 4 * spread]
    first, second, mixing, rows, left, right, out = refs[4 * spread : 4 * spread + 7]
    landed, weight0, weight1, panel_high, panel_low, sems = refs[4 * spread + 7 :]
    slots, order, cap = out.shape[0], out.shape[2], left.shape[3]
    padded = landed.shape[1]
    step = pl.program_id(0)
    row_here, col_here = place[0], place[1]
    mine = row_here // grid_cols

    @pl.when(step == 0)
    def _():
        passed = (row_here ^ col_here) & 1
        waits = []
        for n in range(2 * spread):
            for k in range(2):
                part = [source.at[pl.ds(k * capacity, capacity)] for source in sources[2 * n : 2 * n + 2]]
                waits.append(fetch(passed, part, landed.at[2 * n + k, pl.ds(0, capacity)], sems.at[2 * n + k]))
                if padded > capacity:
                    landed[2 * n + k, capacity:, :] = jnp.zeros((padded - capacity, order), jnp.float32)
        base_parts = split3(jnp.concatenate([first[...], mixing[...]], axis=0))
        second_parts = split3(second[...])
        for wait in waits:
            wait()
        for g in range(spread):
            for target, at, parts in ((weight0, 4 * g + 1, base_parts), (weight1, 4 * g + 3, second_parts)):
                right_panel = landed[at].astype(jnp.bfloat16)
                high, low = split2(sum(dot16(part, right_panel, NT) for part in parts))
                height = high.shape[0]
                target[g, :height, :] = high
                target[g, height:, :] = low

    tile_col = step * grid_cols + col_here
    last_row = (slots - 1) * grid_rows + row_here

    @pl.when((tile_col > 1) & (last_row > tile_col))
    def _():
        part = step % spread
        g = part ^ mine
        group = part * grid_cols + col_here
        ids = lax.broadcasted_iota(jnp.int32, (padded, order), 0)
        masked = []
        for t in range(2):
            start, count = segment(ranks, t, group, step // spread, slots, grid_rows)
            value = landed[4 * g + 2 * t]
            masked.append(jnp.where((ids >= start) & (ids < start + count), value, 0.0).astype(jnp.bfloat16))
        part0 = dot16(weight0[g], masked[0], NN)
        part1 = dot16(weight1[g], masked[1], NN)
        panel0 = part0[:order] + part0[2 * order : 3 * order]
        panel1 = part0[order : 2 * order] + part0[3 * order :] + part1[:order] + part1[order:]
        for at, value in ((0, panel0), (order, panel1)):
            high, low = split2(value)
            panel_high[at : at + order, :] = high
            panel_low[at : at + order, :] = low

    for slot in range(slots):
        tile_row = slot * grid_rows + row_here
        below = tile_row > tile_col

        @pl.when(jnp.logical_not(below))
        def _():
            out[slot, 0] = jnp.zeros((order, order), jnp.float32)

        for t in range(2):

            @pl.when(below & (tile_col == t))
            def _():
                both = rows[slot, :, t * order : (t + 1) * order].astype(jnp.float32)
                out[slot, 0] = both[:order] + both[order:]

        @pl.when(below & (tile_col > 1))
        def _():
            basis = left[slot, 0].astype(jnp.float32)
            live = lax.broadcasted_iota(jnp.int32, basis.shape, 1) < ranks[tile_row, tile_col]
            front = dot16(jnp.where(live, basis, 0.0).astype(jnp.bfloat16), right[slot, 0], NT)
            both = dot16(rows[slot], panel_high[...], NN)
            rest = dot16(rows[slot, :order], panel_low[...], NN)
            out[slot, 0] = front - (both[:order] + (both[order:] + rest))


def schur(place, ranks, col_arrays, inverses, rows, left_fac, right_fac, capacity, grid_rows, grid_cols):
    slots, steps, order, cap = left_fac.shape
    spread = grid_rows // grid_cols
    padded = -(-capacity // LANES) * LANES
    flat = [array for pair in col_arrays for array in pair]
    factor = pl.BlockSpec((slots, 1, order, cap), lambda m: (0, m, 0, 0))
    return pl.pallas_call(
        functools.partial(schur_kernel, capacity, grid_rows, grid_cols),
        grid=(steps,),
        out_shape=jax.ShapeDtypeStruct((slots, steps, order, order), jnp.float32),
        in_specs=[IN_SMEM] * 2 + [ANYWHERE] * len(flat) + [IN_VMEM] * 4 + [factor, factor],
        out_specs=pl.BlockSpec((slots, 1, order, order), lambda m: (0, m, 0, 0)),
        scratch_shapes=[
            pltpu.VMEM((4 * spread, padded, order), jnp.float32),
            pltpu.VMEM((spread, 4 * order, padded), jnp.bfloat16),
            pltpu.VMEM((spread, 2 * order, padded), jnp.bfloat16),
            pltpu.VMEM((2 * order, order), jnp.bfloat16),
            pltpu.VMEM((2 * order, order), jnp.bfloat16),
            pltpu.SemaphoreType.DMA((4 * spread,)),
        ],
        compiler_params=params(dimension_semantics=("arbitrary",)),
        cost_estimate=cost(2**33, 2**24),
        name="schur",
    )(place, ranks, *flat, *inverses, rows, left_fac, right_fac)


def after(array, *others):
    return lax.optimization_barrier((array, *others))[0]


def device_program(capacity, diag_tiles, left_fac, right_fac, ranks):
    grid_rows = lax.axis_size("row")
    grid_cols = lax.axis_size("col")
    row_here = lax.axis_index("row")
    col_here = lax.axis_index("col")
    row_slots, _, order, cap = left_fac.shape
    assert cap == LANES and grid_rows % grid_cols == 0 and grid_cols >= 2
    spread = grid_rows // grid_cols
    row_bits = grid_rows.bit_length() - 1
    low_bits = grid_cols.bit_length() - 1
    assert 1 << row_bits == grid_rows and 1 << low_bits == grid_cols
    every_row = range(grid_rows)
    every_col = range(grid_cols)
    place = jnp.stack([row_here, col_here]).astype(jnp.int32)

    def move(array, pairs):
        flat = [(r * grid_cols + c, s * grid_cols + d) for (r, c), (s, d) in pairs]
        return lax.ppermute(array, AXES, flat)

    packed, pivot_bases = pack(place, ranks, left_fac, right_fac, capacity, grid_rows)

    received = [move(pivot_bases, [((1, 0), (1, c))]) for c in every_col if c]

    def chain_step(array, s):
        return move(array, [((r, c - 1), (r, c)) for c in (s, s + 1) if c < grid_cols for r in every_row])

    chain = [packed, chain_step(packed, 1)]
    back = move(packed, [((r, 1), (r, 0)) for r in every_row])

    pivot_bases = jnp.where(col_here == 0, pivot_bases, sum(received))
    own = jnp.concatenate([diag_tiles[0], pivot_bases], axis=0)
    held = [0, 1]
    for bit in range(1, row_bits):
        step = 1 << bit
        got = move(own, [((r, c), (r ^ step, c)) for r in held for c in every_col])
        arrived = (row_here >> bit) == 1
        own = jnp.where(arrived, got, own)
        held = held + [r ^ step for r in held]
    got = move(own, [((r, c), (r ^ 1, c)) for r in every_row for c in every_col])

    chain.append(chain_step(chain[1], 2))
    inverse0 = first_inverse(place, own, got)
    for s in range(3, grid_cols):
        chain.append(chain_step(after(chain[s - 1], inverse0) if s == 3 else chain[s - 1], s))

    firsts = chain
    seconds = [back] + chain[:-1]
    offset = (row_here ^ col_here) & (grid_cols - 1)
    held = {c: [c] for c in every_col}

    def hop(array, bit, held):
        step = 1 << bit
        return move(
            array,
            [
                ((r + h * grid_cols, c), ((r + h * grid_cols) ^ step, c))
                for c in every_col
                for r in held[c]
                for h in range(spread)
            ],
        )

    def along_column(candidates, fence):
        have = pick(jnp.where(offset == 0, col_here, -1), candidates)
        held = {c: [c] for c in every_col}
        for bit in range(1, low_bits):
            got = hop(have, bit, held)
            arrived = (offset >> bit == 1) & (offset & 1 == 0)
            stays = (offset >> bit == 0) & (offset & 1 == 0)
            have = pick(jnp.where(arrived, 1, jnp.where(stays, 0, -1)), [have, got])
            held = {c: held[c] + [r ^ (1 << bit) for r in held[c]] for c in every_col}
        have = after(have, fence)
        sets = [have]
        for bit in range(low_bits, row_bits):
            sets = sets + [hop(array, bit, held) for array in sets]
        return [[array, hop(array, 0, held)] for array in sets]

    inverse1, mixing = second_inverse(place, ranks, own, got, inverse0)
    inverses = (inverse0, inverse1, mixing)
    second_sets = along_column([after(array, inverse0) for array in seconds], inverse1)
    first_sets = along_column(firsts, inverse1)
    rows = row_panels(place, ranks, firsts, seconds, inverses, capacity, row_slots, grid_rows)
    col_arrays = [sets[g] for g in range(spread) for sets in (first_sets, second_sets)]
    return schur(place, ranks, col_arrays, inverses, rows, left_fac, right_fac, capacity, grid_rows, grid_cols)


def shards(diag_tiles, left_fac, right_fac, ranks):
    row_slots, cap = left_fac.shape[0], left_fac.shape[3]
    grid_rows = lax.axis_size("row")
    full = row_slots * cap
    packed = max(cap, full * 5 // 8)
    args = (diag_tiles, left_fac, right_fac, ranks)
    if packed == full:
        return device_program(full, *args)
    tile_ids = jnp.arange(ranks.shape[0], dtype=jnp.int32)[:, None]
    live = jnp.where(tile_ids > jnp.arange(2, dtype=jnp.int32)[None, :], ranks[:, :2], 0)
    widest = jnp.max(jnp.sum(live.reshape(row_slots, grid_rows, 2), axis=0))
    return lax.cond(
        widest <= packed,
        functools.partial(device_program, packed),
        functools.partial(device_program, full),
        *args,
    )


def solution(mesh):
    in_specs = (P("row", None, None), P("row", "col", None, None), P("row", "col", None, None), P())
    out_specs = P("row", "col", None, None)
    return jax.shard_map(shards, mesh=mesh, in_specs=in_specs, out_specs=out_specs, check_vma=False)
```

```python
import functools

import jax
import jax.numpy as jnp
from jax import lax
from jax.experimental import pallas as pl
from jax.experimental.pallas import tpu as pltpu
from jax.sharding import PartitionSpec as P

PRECISE = lax.Precision.HIGHEST
AXES = ("row", "col")
BLOCK = 32
GROUP = 8
LANES = 128
NT = (((1,), (1,)), ((), ()))
TN = (((0,), (0,)), ((), ()))
NN = (((1,), (0,)), ((), ()))
ANYWHERE = pl.BlockSpec(memory_space=pl.ANY)
IN_VMEM = pl.BlockSpec(memory_space=pltpu.VMEM)
IN_SMEM = pl.BlockSpec(memory_space=pltpu.SMEM)
IN_HBM = pl.BlockSpec(memory_space=pltpu.HBM)
VMEM_LIMIT = 48 * 1024 * 1024


def dot32(lhs, rhs, dims):
    return lax.dot_general(lhs, rhs, dims, precision=PRECISE, preferred_element_type=jnp.float32)


def dot16(lhs, rhs, dims):
    return lax.dot_general(lhs, rhs, dims, preferred_element_type=jnp.float32)


def split2(value):
    high = value.astype(jnp.bfloat16)
    low = (value - high.astype(jnp.float32)).astype(jnp.bfloat16)
    return high, low


def split3(value):
    high = value.astype(jnp.bfloat16)
    rest = value - high.astype(jnp.float32)
    middle = rest.astype(jnp.bfloat16)
    low = (rest - middle.astype(jnp.float32)).astype(jnp.bfloat16)
    return high, middle, low


def params(**extra):
    return pltpu.CompilerParams(vmem_limit_bytes=VMEM_LIMIT, **extra)


def cost(flops, moved):
    return pl.CostEstimate(flops=int(flops), bytes_accessed=int(moved), transcendentals=0)


def eliminate(tiles):
    tiles, start = tiles
    rows = tiles[0].shape[0]
    done = []
    for first in range(0, rows, GROUP):
        height = rows - first
        row_ids = lax.broadcasted_iota(jnp.int32, (height, LANES), 0)
        heads = [
            jnp.broadcast_to(tiles[0][:, start + first + j : start + first + j + 1], (height, LANES))
            for j in range(GROUP)
        ]
        scale = jnp.zeros((GROUP, LANES), jnp.float32)
        for j in range(GROUP):
            pivot = heads[j][j : j + 1, :]
            factor = jnp.where(row_ids > j, heads[j] * (1.0 / pivot), 0.0)
            for other in range(j + 1, GROUP):
                heads[other] = heads[other] - factor * heads[other][j : j + 1, :]
            tiles = [tile - factor * tile[j : j + 1, :] for tile in tiles]
            root = lax.rsqrt(pivot)
            root = root * (1.5 - 0.5 * pivot * root * root)
            scale = jnp.where(row_ids[:GROUP] == j, root, scale)
        done.append([tile[:GROUP] * scale for tile in tiles])
        tiles = [tile[GROUP:] for tile in tiles]
    return [jnp.concatenate(parts, axis=0) for parts in zip(*done)]


def inverse_factor(source, work, result):
    order = source.shape[0]
    span = order // LANES
    for base in range(0, order, BLOCK):
        low = base // LANES
        row_ids = lax.broadcasted_iota(jnp.int32, (BLOCK, LANES), 0)
        lane_ids = lax.broadcasted_iota(jnp.int32, (BLOCK, LANES), 1)
        unit = jnp.where(lane_ids - base % LANES == row_ids, 1.0, 0.0)
        zero = jnp.zeros((BLOCK, LANES), jnp.float32)
        tiles = [source[base : base + BLOCK, s * LANES : (s + 1) * LANES] for s in range(low, span)]
        tiles += [zero] * low + [unit]
        if base:
            taken = dot32(
                work[0:base, base : base + BLOCK],
                work[0:base, low * LANES : order + (low + 1) * LANES],
                TN,
            )
            tiles = [tile - taken[:, s * LANES : (s + 1) * LANES] for s, tile in enumerate(tiles)]
        tiles = eliminate((tiles, base % LANES))
        for s, tile in enumerate(tiles):
            work[base : base + BLOCK, (low + s) * LANES : (low + s + 1) * LANES] = tile
        for s in range(low + 1, span):
            work[base : base + BLOCK, order + s * LANES : order + (s + 1) * LANES] = zero
    result[...] = work[:, order:]


def fetch(choice, candidates, target, sem):
    for n, candidate in enumerate(candidates):
        copy = pltpu.make_async_copy(candidate, target, sem)
        pl.when(choice == n)(copy.start)
    return pltpu.make_async_copy(candidates[0], target, sem).wait


def first_kernel(place, own, got, result, tile, work, sem):
    fetch(place[0] % 2, (own, got), tile, sem)()
    inverse_factor(tile, work, result)


def first_inverse(place, own, got):
    order = own.shape[1]
    return pl.pallas_call(
        first_kernel,
        out_shape=jax.ShapeDtypeStruct((order, order), jnp.float32),
        in_specs=[IN_SMEM, ANYWHERE, ANYWHERE],
        out_specs=IN_VMEM,
        scratch_shapes=[
            pltpu.VMEM((order, order), jnp.float32),
            pltpu.VMEM((order, 2 * order), jnp.float32),
            pltpu.SemaphoreType.DMA,
        ],
        compiler_params=params(),
        cost_estimate=cost(2**30, 2**20),
        name="first_inverse",
    )(place, own, got)


def second_kernel(place, ranks, own, got, inverse, result, mixing, head, work, sem):
    order = inverse.shape[0]
    cap = (head.shape[0] - order) // 2
    fetch(1 - place[0] % 2, (own, got), head, sem)()
    live = lax.broadcasted_iota(jnp.int32, (cap, order), 0) < ranks[1, 0]
    left = jnp.where(live, head[order : order + cap, :], 0.0)
    right = jnp.where(live, head[order + cap :, :], 0.0)
    solved = dot32(right, inverse[...], NT)
    dense = dot32(left, solved, TN)
    shifted = head.at[pl.ds(0, order)]
    shifted[...] = shifted[...] - dot32(dense, dense, NT)
    inverse_factor(shifted, work, result)
    mixing[...] = -dot32(dot32(result[...], dense, NN), inverse[...], NN)


def second_inverse(place, ranks, own, got, inverse):
    order = inverse.shape[0]
    shape = jax.ShapeDtypeStruct((order, order), jnp.float32)
    return pl.pallas_call(
        second_kernel,
        out_shape=(shape, shape),
        in_specs=[IN_SMEM, IN_SMEM, ANYWHERE, ANYWHERE, IN_VMEM],
        out_specs=(IN_VMEM, IN_VMEM),
        scratch_shapes=[
            pltpu.VMEM(own.shape, jnp.float32),
            pltpu.VMEM((order, 2 * order), jnp.float32),
            pltpu.SemaphoreType.DMA,
        ],
        compiler_params=params(),
        cost_estimate=cost(2**30, 2**20),
        name="second_inverse",
    )(place, ranks, own, got, inverse)


def segment(ranks, panel, group, slot, slots, grid_rows):
    start, count = jnp.int32(0), jnp.int32(0)
    for s in range(slots):
        tile_row = s * grid_rows + group
        rank = jnp.where(tile_row > panel, ranks[tile_row, panel], 0)
        start = start + jnp.where(s < slot, rank, 0)
        count = count + jnp.where(s == slot, rank, 0)
    return start, count


def pack_kernel(capacity, grid_rows, place, ranks, left, right, packed, pivot, held, sem):
    slots, order, cap = held.shape[1:]
    copies = [
        pltpu.make_async_copy(source.at[:, 0], held.at[k], sem.at[k]) for k, source in enumerate((left, right))
    ]
    for copy in copies:
        copy.start()
    panel = jnp.minimum(place[1], 1)
    spot = lax.broadcasted_iota(jnp.int32, (capacity, cap), 0)
    column = lax.broadcasted_iota(jnp.int32, (capacity, cap), 1)
    chosen = []
    for slot in range(slots):
        start, count = segment(ranks, panel, place[0], slot, slots, grid_rows)
        hit = (spot - start == column) & (column < count)
        chosen.append(jnp.where(hit, 1.0, 0.0).astype(jnp.bfloat16))
    for k, copy in enumerate(copies):
        copy.wait()
        total = sum(dot16(chosen[slot], held[k, slot], NT) for slot in range(slots))
        packed[k * capacity : (k + 1) * capacity, :] = total
        pivot[k * cap : (k + 1) * cap, :] = total[:cap]


def pack(place, ranks, left_fac, right_fac, capacity, grid_rows):
    slots, _, order, cap = left_fac.shape
    return pl.pallas_call(
        functools.partial(pack_kernel, capacity, grid_rows),
        out_shape=(
            jax.ShapeDtypeStruct((2 * capacity, order), jnp.float32),
            jax.ShapeDtypeStruct((2 * cap, order), jnp.float32),
        ),
        in_specs=[IN_SMEM, IN_SMEM, IN_HBM, IN_HBM],
        out_specs=(IN_VMEM, IN_VMEM),
        scratch_shapes=[pltpu.VMEM((2, slots, order, cap), jnp.bfloat16), pltpu.SemaphoreType.DMA((2,))],
        compiler_params=params(),
        cost_estimate=cost(2**28, 2**20),
        name="pack",
    )(place, ranks, left_fac, right_fac)


def pick_kernel(count, index, *refs):
    candidates, target, sem = refs[:count], refs[count], refs[count + 1]
    wait = fetch(index[0], candidates, target, sem)
    pl.when(index[0] >= 0)(wait)


def pick(index, candidates):
    return pl.pallas_call(
        functools.partial(pick_kernel, len(candidates)),
        out_shape=jax.ShapeDtypeStruct(candidates[0].shape, candidates[0].dtype),
        in_specs=[IN_SMEM] + [ANYWHERE] * len(candidates),
        out_specs=ANYWHERE,
        scratch_shapes=[pltpu.SemaphoreType.DMA],
        compiler_params=params(),
        cost_estimate=cost(0, 2 * candidates[0].size * 4),
        name="pick",
    )(jnp.reshape(index, (1,)).astype(jnp.int32), *candidates)


def rows_kernel(capacity, grid_rows, count, place, ranks, *refs):
    sources, (first, second, mixing), stacked = refs[: 2 * count], refs[2 * count : 2 * count + 3], refs[2 * count + 3]
    landed, weight_high, weight_low, sems = refs[2 * count + 4 :]
    order = first.shape[0]
    slots = stacked.shape[0]
    cap = LANES
    waits = []
    for t in range(2):
        for k in range(2):
            part = [source.at[pl.ds(k * capacity, capacity)] for source in sources[t * count : (t + 1) * count]]
            waits.append(fetch(place[1], part, landed.at[2 * t + k, pl.ds(0, capacity)], sems.at[2 * t + k]))
            landed[2 * t + k, capacity:, :] = jnp.zeros((cap, order), jnp.float32)
    base = jnp.concatenate([first[...], mixing[...]], axis=0)
    base_parts, second_parts = split3(base), split3(second[...])
    for wait in waits:
        wait()
    solved0 = sum(dot16(landed[1].astype(jnp.bfloat16), part, NT) for part in base_parts)
    solved1 = sum(dot16(landed[3].astype(jnp.bfloat16), part, NT) for part in second_parts)
    for column, value in ((0, solved0), (2 * order, solved1)):
        high, low = split2(value)
        weight_high[:, column : column + value.shape[1]] = high
        weight_low[:, column : column + value.shape[1]] = low
    live = lax.broadcasted_iota(jnp.int32, (cap, order), 0)
    for slot in range(slots):
        pieces = []
        for t in range(2):
            start, rank = segment(ranks, t, place[0], slot, slots, grid_rows)
            spot = pl.ds(pl.multiple_of(start, 16), cap)
            left = jnp.where(live < rank, landed[2 * t, spot, :], 0.0).astype(jnp.bfloat16)
            columns = pl.ds(0, 2 * order) if t == 0 else pl.ds(2 * order, order)
            weights = jnp.concatenate([weight_high[spot, columns], weight_low[spot, columns]], axis=0)
            pieces.append(dot16(jnp.concatenate([left, left], axis=0), weights, TN))
        for column, value in ((0, pieces[0][:, :order]), (order, pieces[0][:, order:] + pieces[1])):
            high, low = split2(value)
            stacked[slot, :, column : column + order] = high
            stacked[slot, :, 2 * order + column : 2 * order + column + order] = low
            stacked[slot, :, 4 * order + column : 4 * order + column + order] = high


def row_panels(place, ranks, firsts, seconds, inverses, capacity, slots, grid_rows):
    order = inverses[0].shape[0]
    count = len(firsts)
    return pl.pallas_call(
        functools.partial(rows_kernel, capacity, grid_rows, count),
        out_shape=jax.ShapeDtypeStruct((slots, order, 6 * order), jnp.bfloat16),
        in_specs=[IN_SMEM] * 2 + [ANYWHERE] * (2 * count) + [IN_VMEM] * 3,
        out_specs=IN_VMEM,
        scratch_shapes=[
            pltpu.VMEM((4, capacity + LANES, order), jnp.float32),
            pltpu.VMEM((capacity + LANES, 3 * order), jnp.bfloat16),
            pltpu.VMEM((capacity + LANES, 3 * order), jnp.bfloat16),
            pltpu.SemaphoreType.DMA((4,)),
        ],
        compiler_params=params(),
        cost_estimate=cost(2**32, 2**22),
        name="row_panels",
    )(place, ranks, *firsts, *seconds, *inverses)


def schur_kernel(capacity, grid_rows, grid_cols, place, ranks, *refs):
    spread = grid_rows // grid_cols
    sources = refs[: 4 * spread]
    first, second, mixing, rows, left, right, out = refs[4 * spread : 4 * spread + 7]
    landed, weight0, weight1, bases, panel, sems = refs[4 * spread + 7 :]
    slots, order, cap = out.shape[0], out.shape[2], left.shape[3]
    padded = landed.shape[1]
    step = pl.program_id(0)
    row_here, col_here = place[0], place[1]
    mine = row_here // grid_cols

    @pl.when(step == 0)
    def _():
        passed = (row_here ^ col_here) & 1
        waits = []
        for n in range(2 * spread):
            for k in range(2):
                part = [source.at[pl.ds(k * capacity, capacity)] for source in sources[2 * n : 2 * n + 2]]
                waits.append(fetch(passed, part, landed.at[2 * n + k, pl.ds(0, capacity)], sems.at[2 * n + k]))
                if padded > capacity:
                    landed[2 * n + k, capacity:, :] = jnp.zeros((padded - capacity, order), jnp.float32)
        base_parts = split3(jnp.concatenate([first[...], mixing[...]], axis=0))
        second_parts = split3(second[...])
        for wait in waits:
            wait()
        for g in range(spread):
            right0 = landed[4 * g + 1].astype(jnp.bfloat16)
            right1 = landed[4 * g + 3].astype(jnp.bfloat16)
            solved0 = sum(dot16(part, right0, NT) for part in base_parts)
            solved1 = sum(dot16(part, right1, NT) for part in second_parts)
            for target, at, value in (
                (weight0, 0, solved0[:order]),
                (weight1, 0, solved0[order:]),
                (weight1, 2, solved1),
            ):
                for n, piece in enumerate(split2(value)):
                    target[g, :, (at + n) * padded : (at + n + 1) * padded] = piece

    tile_col = step * grid_cols + col_here
    last_row = (slots - 1) * grid_rows + row_here

    @pl.when((tile_col > 1) & (last_row > tile_col))
    def _():
        part = step % spread
        g = part ^ mine
        group = part * grid_cols + col_here
        ids = lax.broadcasted_iota(jnp.int32, (padded, order), 0)
        for t in range(2):
            start, count = segment(ranks, t, group, step // spread, slots, grid_rows)
            value = landed[4 * g + 2 * t]
            value = jnp.where((ids >= start) & (ids < start + count), value, 0.0).astype(jnp.bfloat16)
            for n in range(2):
                bases[(2 * t + n) * padded : (2 * t + n + 1) * padded, :] = value
        panel0 = dot16(weight0[g], bases[: 2 * padded], NN)
        panel1 = dot16(weight1[g], bases[...], NN)
        for at, value in ((0, panel0), (order, panel1)):
            high, low = split2(value)
            panel[at : at + order, :] = high
            panel[2 * order + at : 3 * order + at, :] = high
            panel[4 * order + at : 5 * order + at, :] = low

    for slot in range(slots):
        tile_row = slot * grid_rows + row_here
        below = tile_row > tile_col

        @pl.when(jnp.logical_not(below))
        def _():
            out[slot, 0] = jnp.zeros((order, order), jnp.float32)

        for t in range(2):

            @pl.when(below & (tile_col == t))
            def _():
                high = rows[slot, :, t * order : (t + 1) * order].astype(jnp.float32)
                low = rows[slot, :, (t + 2) * order : (t + 3) * order].astype(jnp.float32)
                out[slot, 0] = high + low

        @pl.when(below & (tile_col > 1))
        def _():
            basis = left[slot, 0].astype(jnp.float32)
            live = lax.broadcasted_iota(jnp.int32, basis.shape, 1) < ranks[tile_row, tile_col]
            front = dot16(jnp.where(live, basis, 0.0).astype(jnp.bfloat16), right[slot, 0], NT)
            out[slot, 0] = front - dot16(rows[slot], panel[...], NN)


def schur(place, ranks, col_arrays, inverses, rows, left_fac, right_fac, capacity, grid_rows, grid_cols):
    slots, steps, order, cap = left_fac.shape
    spread = grid_rows // grid_cols
    padded = -(-capacity // LANES) * LANES
    flat = [array for pair in col_arrays for array in pair]
    factor = pl.BlockSpec((slots, 1, order, cap), lambda m: (0, m, 0, 0))
    return pl.pallas_call(
        functools.partial(schur_kernel, capacity, grid_rows, grid_cols),
        grid=(steps,),
        out_shape=jax.ShapeDtypeStruct((slots, steps, order, order), jnp.float32),
        in_specs=[IN_SMEM] * 2 + [ANYWHERE] * len(flat) + [IN_VMEM] * 4 + [factor, factor],
        out_specs=pl.BlockSpec((slots, 1, order, order), lambda m: (0, m, 0, 0)),
        scratch_shapes=[
            pltpu.VMEM((4 * spread, padded, order), jnp.float32),
            pltpu.VMEM((spread, order, 2 * padded), jnp.bfloat16),
            pltpu.VMEM((spread, order, 4 * padded), jnp.bfloat16),
            pltpu.VMEM((4 * padded, order), jnp.bfloat16),
            pltpu.VMEM((6 * order, order), jnp.bfloat16),
            pltpu.SemaphoreType.DMA((4 * spread,)),
        ],
        compiler_params=params(dimension_semantics=("arbitrary",)),
        cost_estimate=cost(2**33, 2**24),
        name="schur",
    )(place, ranks, *flat, *inverses, rows, left_fac, right_fac)


def after(array, *others):
    return lax.optimization_barrier((array, *others))[0]


def device_program(capacity, diag_tiles, left_fac, right_fac, ranks):
    grid_rows = lax.axis_size("row")
    grid_cols = lax.axis_size("col")
    row_here = lax.axis_index("row")
    col_here = lax.axis_index("col")
    row_slots, _, order, cap = left_fac.shape
    assert cap == LANES and grid_rows % grid_cols == 0 and grid_cols >= 2
    spread = grid_rows // grid_cols
    row_bits = grid_rows.bit_length() - 1
    low_bits = grid_cols.bit_length() - 1
    assert 1 << row_bits == grid_rows and 1 << low_bits == grid_cols
    every_row = range(grid_rows)
    every_col = range(grid_cols)
    place = jnp.stack([row_here, col_here]).astype(jnp.int32)

    def move(array, pairs):
        flat = [(r * grid_cols + c, s * grid_cols + d) for (r, c), (s, d) in pairs]
        return lax.ppermute(array, AXES, flat)

    def down_column(array, root):
        held = [root]
        for bit in range(1, row_bits):
            step = 1 << bit
            got = move(array, [((r, c), (r ^ step, c)) for r in held for c in every_col])
            array = jnp.where(row_here >> bit == 1, got, array)
            held = held + [r ^ step for r in held]
        return array, move(array, [((r, c), (r ^ 1, c)) for r in held for c in every_col])

    tile = down_column(diag_tiles[0], 0)

    packed, pivot_bases = pack(place, ranks, left_fac, right_fac, capacity, grid_rows)

    def chain_step(array, s):
        return move(array, [((r, c - 1), (r, c)) for c in (s, s + 1) if c < grid_cols for r in every_row])

    chain = [packed, chain_step(packed, 1)]
    back = move(packed, [((r, 1), (r, 0)) for r in every_row])

    received = [move(pivot_bases, [((1, 0), (1, c))]) for c in every_col if c]
    pivot_bases = jnp.where(col_here == 0, pivot_bases, sum(received))
    head = down_column(jnp.concatenate([diag_tiles[0], pivot_bases], axis=0), 1)

    inverse0 = first_inverse(place, *tile)
    for s in range(2, grid_cols):
        chain.append(chain_step(after(chain[s - 1], inverse0) if s == 2 else chain[s - 1], s))

    firsts = chain
    seconds = [back] + chain[:-1]
    offset = (row_here ^ col_here) & (grid_cols - 1)
    held = {c: [c] for c in every_col}

    def hop(array, bit, held):
        step = 1 << bit
        return move(
            array,
            [
                ((r + h * grid_cols, c), ((r + h * grid_cols) ^ step, c))
                for c in every_col
                for r in held[c]
                for h in range(spread)
            ],
        )

    def along_column(candidates, fence):
        have = pick(jnp.where(offset == 0, col_here, -1), candidates)
        held = {c: [c] for c in every_col}
        for bit in range(1, low_bits):
            got = hop(have, bit, held)
            arrived = (offset >> bit == 1) & (offset & 1 == 0)
            stays = (offset >> bit == 0) & (offset & 1 == 0)
            have = pick(jnp.where(arrived, 1, jnp.where(stays, 0, -1)), [have, got])
            held = {c: held[c] + [r ^ (1 << bit) for r in held[c]] for c in every_col}
        have = after(have, fence)
        sets = [have]
        for bit in range(low_bits, row_bits):
            sets = sets + [hop(array, bit, held) for array in sets]
        return [[array, hop(array, 0, held)] for array in sets]

    head = [after(array, chain[min(2, grid_cols - 1)]) for array in head]
    inverse1, mixing = second_inverse(place, ranks, *head, inverse0)
    inverses = (inverse0, inverse1, mixing)
    rows = row_panels(place, ranks, firsts, seconds, inverses, capacity, row_slots, grid_rows)
    second_sets = along_column(seconds, inverse1)
    first_sets = along_column([firsts[0], *[after(array, inverse1) for array in firsts[1:]]], rows)
    col_arrays = [sets[g] for g in range(spread) for sets in (first_sets, second_sets)]
    return schur(place, ranks, col_arrays, inverses, rows, left_fac, right_fac, capacity, grid_rows, grid_cols)


def shards(diag_tiles, left_fac, right_fac, ranks):
    row_slots, cap = left_fac.shape[0], left_fac.shape[3]
    grid_rows = lax.axis_size("row")
    full = row_slots * cap
    packed = max(cap, full * 5 // 8)
    args = (diag_tiles, left_fac, right_fac, ranks)
    if packed == full:
        return device_program(full, *args)
    tile_ids = jnp.arange(ranks.shape[0], dtype=jnp.int32)[:, None]
    live = jnp.where(tile_ids > jnp.arange(2, dtype=jnp.int32)[None, :], ranks[:, :2], 0)
    widest = jnp.max(sum(live[s * grid_rows : (s + 1) * grid_rows] for s in range(row_slots)))
    return lax.cond(
        widest <= packed,
        functools.partial(device_program, packed),
        functools.partial(device_program, full),
        *args,
    )


def solution(mesh):
    in_specs = (P("row", None, None), P("row", "col", None, None), P("row", "col", None, None), P())
    out_specs = P("row", "col", None, None)
    return jax.shard_map(shards, mesh=mesh, in_specs=in_specs, out_specs=out_specs, check_vma=False)
```

```python
import functools

import jax
import jax.numpy as jnp
from jax import lax
from jax.experimental import pallas as pl
from jax.experimental.pallas import tpu as pltpu
from jax.sharding import PartitionSpec as P

PRECISE = lax.Precision.HIGHEST
AXES = ("row", "col")
BLOCK = 32
GROUP = 8
LANES = 128
NT = (((1,), (1,)), ((), ()))
TN = (((0,), (0,)), ((), ()))
NN = (((1,), (0,)), ((), ()))
ANYWHERE = pl.BlockSpec(memory_space=pl.ANY)
IN_VMEM = pl.BlockSpec(memory_space=pltpu.VMEM)
IN_SMEM = pl.BlockSpec(memory_space=pltpu.SMEM)
IN_HBM = pl.BlockSpec(memory_space=pltpu.HBM)
MEBI = 1024 * 1024


def dot32(lhs, rhs, dims):
    return lax.dot_general(lhs, rhs, dims, precision=PRECISE, preferred_element_type=jnp.float32)


def dot16(lhs, rhs, dims):
    return lax.dot_general(lhs, rhs, dims, preferred_element_type=jnp.float32)


def split2(value):
    high = value.astype(jnp.bfloat16)
    low = (value - high.astype(jnp.float32)).astype(jnp.bfloat16)
    return high, low


def params(mebibytes, **extra):
    return pltpu.CompilerParams(vmem_limit_bytes=mebibytes * MEBI, **extra)


def cost(flops, moved):
    return pl.CostEstimate(flops=int(flops), bytes_accessed=int(moved), transcendentals=0)


def eliminate(tiles):
    tiles, start = tiles
    rows = tiles[0].shape[0]
    done = []
    for first in range(0, rows, GROUP):
        height = rows - first
        row_ids = lax.broadcasted_iota(jnp.int32, (height, LANES), 0)
        heads = [
            jnp.broadcast_to(tiles[0][:, start + first + j : start + first + j + 1], (height, LANES))
            for j in range(GROUP)
        ]
        scale = jnp.zeros((GROUP, LANES), jnp.float32)
        for j in range(GROUP):
            pivot = heads[j][j : j + 1, :]
            factor = jnp.where(row_ids > j, heads[j] * (1.0 / pivot), 0.0)
            for other in range(j + 1, GROUP):
                heads[other] = heads[other] - factor * heads[other][j : j + 1, :]
            tiles = [tile - factor * tile[j : j + 1, :] for tile in tiles]
            root = lax.rsqrt(pivot)
            root = root * (1.5 - 0.5 * pivot * root * root)
            scale = jnp.where(row_ids[:GROUP] == j, root, scale)
        done.append([tile[:GROUP] * scale for tile in tiles])
        tiles = [tile[GROUP:] for tile in tiles]
    return [jnp.concatenate(parts, axis=0) for parts in zip(*done)]


def inverse_factor(source, work, result):
    order = source.shape[0]
    span = order // LANES
    for base in range(0, order, BLOCK):
        low = base // LANES
        row_ids = lax.broadcasted_iota(jnp.int32, (BLOCK, LANES), 0)
        lane_ids = lax.broadcasted_iota(jnp.int32, (BLOCK, LANES), 1)
        unit = jnp.where(lane_ids - base % LANES == row_ids, 1.0, 0.0)
        zero = jnp.zeros((BLOCK, LANES), jnp.float32)
        tiles = [source[base : base + BLOCK, s * LANES : (s + 1) * LANES] for s in range(low, span)]
        tiles += [zero] * low + [unit]
        if base:
            taken = dot32(
                work[0:base, base : base + BLOCK],
                work[0:base, low * LANES : order + (low + 1) * LANES],
                TN,
            )
            tiles = [tile - taken[:, s * LANES : (s + 1) * LANES] for s, tile in enumerate(tiles)]
        tiles = eliminate((tiles, base % LANES))
        for s, tile in enumerate(tiles):
            work[base : base + BLOCK, (low + s) * LANES : (low + s + 1) * LANES] = tile
        for s in range(low + 1, span):
            work[base : base + BLOCK, order + s * LANES : order + (s + 1) * LANES] = zero
    result[...] = work[:, order:]


def fetch(choice, candidates, target, sem):
    for n, candidate in enumerate(candidates):
        copy = pltpu.make_async_copy(candidate, target, sem)
        pl.when(choice == n)(copy.start)
    return pltpu.make_async_copy(candidates[0], target, sem).wait


def first_kernel(place, own, got, result, tile, work, sem):
    fetch(place[0] % 2, (own, got), tile, sem)()
    inverse_factor(tile, work, result)


def first_inverse(place, own, got):
    order = own.shape[1]
    return pl.pallas_call(
        first_kernel,
        out_shape=jax.ShapeDtypeStruct((order, order), jnp.float32),
        in_specs=[IN_SMEM, ANYWHERE, ANYWHERE],
        out_specs=IN_VMEM,
        scratch_shapes=[
            pltpu.VMEM((order, order), jnp.float32),
            pltpu.VMEM((order, 2 * order), jnp.float32),
            pltpu.SemaphoreType.DMA,
        ],
        compiler_params=params(8),
        cost_estimate=cost(2**30, 2**20),
        name="first_inverse",
    )(place, own, got)


def second_kernel(place, ranks, own, got, inverse, result, mixing, head, work, sem):
    order = inverse.shape[0]
    cap = (head.shape[0] - order) // 2
    fetch(1 - place[0] % 2, (own, got), head, sem)()
    live = lax.broadcasted_iota(jnp.int32, (cap, order), 0) < ranks[1, 0]
    left = jnp.where(live, head[order : order + cap, :], 0.0)
    right = jnp.where(live, head[order + cap :, :], 0.0)
    solved = dot32(right, inverse[...], NT)
    dense = dot32(left, solved, TN)
    shifted = head.at[pl.ds(0, order)]
    shifted[...] = shifted[...] - dot32(dense, dense, NT)
    inverse_factor(shifted, work, result)
    mixing[...] = -dot32(dot32(result[...], dense, NN), inverse[...], NN)


def second_inverse(place, ranks, own, got, inverse):
    order = inverse.shape[0]
    shape = jax.ShapeDtypeStruct((order, order), jnp.float32)
    return pl.pallas_call(
        second_kernel,
        out_shape=(shape, shape),
        in_specs=[IN_SMEM, IN_SMEM, ANYWHERE, ANYWHERE, IN_VMEM],
        out_specs=(IN_VMEM, IN_VMEM),
        scratch_shapes=[
            pltpu.VMEM(own.shape, jnp.float32),
            pltpu.VMEM((order, 2 * order), jnp.float32),
            pltpu.SemaphoreType.DMA,
        ],
        compiler_params=params(8),
        cost_estimate=cost(2**30, 2**20),
        name="second_inverse",
    )(place, ranks, own, got, inverse)


def segment(ranks, panel, group, slot, slots, grid_rows):
    start, count = jnp.int32(0), jnp.int32(0)
    for s in range(slots):
        tile_row = s * grid_rows + group
        rank = jnp.where(tile_row > panel, ranks[tile_row, panel], 0)
        start = start + jnp.where(s < slot, rank, 0)
        count = count + jnp.where(s == slot, rank, 0)
    return start, count


def pack_kernel(capacity, grid_rows, place, ranks, left, right, packed, pivot, held, sem):
    slots, order, cap = held.shape[1:]
    copies = [
        pltpu.make_async_copy(source.at[:, 0], held.at[k], sem.at[k]) for k, source in enumerate((left, right))
    ]
    for copy in copies:
        copy.start()
    panel = jnp.minimum(place[1], 1)
    spot = lax.broadcasted_iota(jnp.int32, (capacity, cap), 0)
    column = lax.broadcasted_iota(jnp.int32, (capacity, cap), 1)
    chosen = []
    for slot in range(slots):
        start, count = segment(ranks, panel, place[0], slot, slots, grid_rows)
        hit = (spot - start == column) & (column < count)
        chosen.append(jnp.where(hit, 1.0, 0.0).astype(jnp.bfloat16))
    for k, copy in enumerate(copies):
        copy.wait()
        total = sum(dot16(chosen[slot], held[k, slot], NT) for slot in range(slots))
        packed[k * capacity : (k + 1) * capacity, :] = total
        pivot[k * cap : (k + 1) * cap, :] = total[:cap]


def pack(place, ranks, left_fac, right_fac, capacity, grid_rows):
    slots, _, order, cap = left_fac.shape
    return pl.pallas_call(
        functools.partial(pack_kernel, capacity, grid_rows),
        out_shape=(
            jax.ShapeDtypeStruct((2 * capacity, order), jnp.float32),
            jax.ShapeDtypeStruct((2 * cap, order), jnp.float32),
        ),
        in_specs=[IN_SMEM, IN_SMEM, IN_HBM, IN_HBM],
        out_specs=(IN_VMEM, IN_VMEM),
        scratch_shapes=[pltpu.VMEM((2, slots, order, cap), jnp.bfloat16), pltpu.SemaphoreType.DMA((2,))],
        compiler_params=params(16),
        cost_estimate=cost(2**28, 2**20),
        name="pack",
    )(place, ranks, left_fac, right_fac)


def pick_kernel(count, index, *refs):
    candidates, target, sem = refs[:count], refs[count], refs[count + 1]
    wait = fetch(index[0], candidates, target, sem)
    pl.when(index[0] >= 0)(wait)


def pick(index, candidates):
    return pl.pallas_call(
        functools.partial(pick_kernel, len(candidates)),
        out_shape=jax.ShapeDtypeStruct(candidates[0].shape, candidates[0].dtype),
        in_specs=[IN_SMEM] + [ANYWHERE] * len(candidates),
        out_specs=ANYWHERE,
        scratch_shapes=[pltpu.SemaphoreType.DMA],
        compiler_params=params(4),
        cost_estimate=cost(0, 2 * candidates[0].size * 4),
        name="pick",
    )(jnp.reshape(index, (1,)).astype(jnp.int32), *candidates)


def rows_kernel(capacity, grid_rows, count, place, ranks, *refs):
    sources, (first, second, mixing), stacked = refs[: 2 * count], refs[2 * count : 2 * count + 3], refs[2 * count + 3]
    landed, weight_high, weight_low, sems = refs[2 * count + 4 :]
    order = first.shape[0]
    slots = stacked.shape[0]
    cap = LANES
    waits = []
    for t in range(2):
        for k in range(2):
            part = [source.at[pl.ds(k * capacity, capacity)] for source in sources[t * count : (t + 1) * count]]
            waits.append(fetch(place[1], part, landed.at[2 * t + k, pl.ds(0, capacity)], sems.at[2 * t + k]))
            landed[2 * t + k, capacity:, :] = jnp.zeros((cap, order), jnp.float32)
    base = jnp.concatenate([first[...], mixing[...]], axis=0)
    base_parts, second_parts = split2(base), split2(second[...])
    for wait in waits:
        wait()
    solved0 = sum(dot16(landed[1].astype(jnp.bfloat16), part, NT) for part in base_parts)
    solved1 = sum(dot16(landed[3].astype(jnp.bfloat16), part, NT) for part in second_parts)
    for column, value in ((0, solved0), (2 * order, solved1)):
        high, low = split2(value)
        weight_high[:, column : column + value.shape[1]] = high
        weight_low[:, column : column + value.shape[1]] = low
    live = lax.broadcasted_iota(jnp.int32, (cap, order), 0)
    for slot in range(slots):
        pieces = []
        for t in range(2):
            start, rank = segment(ranks, t, place[0], slot, slots, grid_rows)
            spot = pl.ds(pl.multiple_of(start, 16), cap)
            left = jnp.where(live < rank, landed[2 * t, spot, :], 0.0).astype(jnp.bfloat16)
            columns = pl.ds(0, 2 * order) if t == 0 else pl.ds(2 * order, order)
            weights = jnp.concatenate([weight_high[spot, columns], weight_low[spot, columns]], axis=0)
            pieces.append(dot16(jnp.concatenate([left, left], axis=0), weights, TN))
        for column, value in ((0, pieces[0][:, :order]), (order, pieces[0][:, order:] + pieces[1])):
            high, low = split2(value)
            stacked[slot, :, column : column + order] = high
            stacked[slot, :, 2 * order + column : 2 * order + column + order] = low
            stacked[slot, :, 4 * order + column : 4 * order + column + order] = high


def row_panels(place, ranks, firsts, seconds, inverses, capacity, slots, grid_rows):
    order = inverses[0].shape[0]
    count = len(firsts)
    return pl.pallas_call(
        functools.partial(rows_kernel, capacity, grid_rows, count),
        out_shape=jax.ShapeDtypeStruct((slots, order, 6 * order), jnp.bfloat16),
        in_specs=[IN_SMEM] * 2 + [ANYWHERE] * (2 * count) + [IN_VMEM] * 3,
        out_specs=IN_VMEM,
        scratch_shapes=[
            pltpu.VMEM((4, capacity + LANES, order), jnp.float32),
            pltpu.VMEM((capacity + LANES, 3 * order), jnp.bfloat16),
            pltpu.VMEM((capacity + LANES, 3 * order), jnp.bfloat16),
            pltpu.SemaphoreType.DMA((4,)),
        ],
        compiler_params=params(20),
        cost_estimate=cost(2**32, 2**22),
        name="row_panels",
    )(place, ranks, *firsts, *seconds, *inverses)


def schur_kernel(capacity, grid_rows, grid_cols, place, ranks, *refs):
    spread = grid_rows // grid_cols
    sources = refs[: 4 * spread]
    first, second, mixing, rows, left, right, out = refs[4 * spread : 4 * spread + 7]
    landed, weight0, weight1, bases, panel, sems = refs[4 * spread + 7 :]
    slots, order, cap = out.shape[0], out.shape[2], left.shape[3]
    padded = landed.shape[1]
    step = pl.program_id(0)
    row_here, col_here = place[0], place[1]
    mine = row_here // grid_cols

    @pl.when(step == 0)
    def _():
        passed = (row_here ^ col_here) & 1
        waits = []
        for n in range(2 * spread):
            for k in range(2):
                part = [source.at[pl.ds(k * capacity, capacity)] for source in sources[2 * n : 2 * n + 2]]
                waits.append(fetch(passed, part, landed.at[2 * n + k, pl.ds(0, capacity)], sems.at[2 * n + k]))
                if padded > capacity:
                    landed[2 * n + k, capacity:, :] = jnp.zeros((padded - capacity, order), jnp.float32)
        base_parts = split2(jnp.concatenate([first[...], mixing[...]], axis=0))
        second_parts = split2(second[...])
        for wait in waits:
            wait()
        for g in range(spread):
            right0 = landed[4 * g + 1].astype(jnp.bfloat16)
            right1 = landed[4 * g + 3].astype(jnp.bfloat16)
            solved0 = sum(dot16(part, right0, NT) for part in base_parts)
            solved1 = sum(dot16(part, right1, NT) for part in second_parts)
            for target, at, value in (
                (weight0, 2 * g, solved0[:order]),
                (weight1, 4 * g, solved0[order:]),
                (weight1, 4 * g + 2, solved1),
            ):
                for n, piece in enumerate(split2(value)):
                    target[at + n] = piece

    tile_col = step * grid_cols + col_here
    last_row = (slots - 1) * grid_rows + row_here

    @pl.when((tile_col > 1) & (last_row > tile_col))
    def _():
        part = step % spread
        g = part ^ mine
        group = part * grid_cols + col_here
        span = 2 * LANES
        ids = lax.broadcasted_iota(jnp.int32, (span, order), 0)
        windows = []
        for t in range(2):
            start, count = segment(ranks, t, group, step // spread, slots, grid_rows)
            first_lane = start // LANES * LANES
            window = pl.ds(pl.multiple_of(first_lane, LANES), span)
            value = landed[4 * g + 2 * t, window, :]
            live = (ids >= start - first_lane) & (ids < start - first_lane + count)
            value = jnp.where(live, value, 0.0).astype(jnp.bfloat16)
            for n in range(2):
                bases[(2 * t + n) * span : (2 * t + n + 1) * span, :] = value
            windows.append(window)
        left0 = [weight0[2 * g + n, :, windows[0]] for n in range(2)]
        left1 = [weight1[4 * g + n, :, windows[n // 2]] for n in range(4)]
        panel0 = dot16(jnp.concatenate(left0, axis=1), bases[: 2 * span], NN)
        panel1 = dot16(jnp.concatenate(left1, axis=1), bases[...], NN)
        for at, value in ((0, panel0), (order, panel1)):
            high, low = split2(value)
            panel[at : at + order, :] = high
            panel[2 * order + at : 3 * order + at, :] = high
            panel[4 * order + at : 5 * order + at, :] = low

    for slot in range(slots):
        tile_row = slot * grid_rows + row_here
        below = tile_row > tile_col

        @pl.when(jnp.logical_not(below))
        def _():
            out[slot, 0] = jnp.zeros((order, order), jnp.float32)

        for t in range(2):

            @pl.when(below & (tile_col == t))
            def _():
                high = rows[slot, :, t * order : (t + 1) * order].astype(jnp.float32)
                low = rows[slot, :, (t + 2) * order : (t + 3) * order].astype(jnp.float32)
                out[slot, 0] = high + low

        @pl.when(below & (tile_col > 1))
        def _():
            basis = left[slot, 0].astype(jnp.float32)
            live = lax.broadcasted_iota(jnp.int32, basis.shape, 1) < ranks[tile_row, tile_col]
            front = dot16(jnp.where(live, basis, 0.0).astype(jnp.bfloat16), right[slot, 0], NT)
            out[slot, 0] = front - dot16(rows[slot], panel[...], NN)


def schur(place, ranks, col_arrays, inverses, rows, left_fac, right_fac, capacity, grid_rows, grid_cols):
    slots, steps, order, cap = left_fac.shape
    spread = grid_rows // grid_cols
    padded = (-(-capacity // LANES) + 1) * LANES
    flat = [array for pair in col_arrays for array in pair]
    factor = pl.BlockSpec((slots, 1, order, cap), lambda m: (0, m, 0, 0))
    return pl.pallas_call(
        functools.partial(schur_kernel, capacity, grid_rows, grid_cols),
        grid=(steps,),
        out_shape=pltpu.HBM((slots, steps, order, order), jnp.float32),
        in_specs=[IN_SMEM] * 2 + [ANYWHERE] * len(flat) + [IN_VMEM] * 4 + [factor, factor],
        out_specs=pl.BlockSpec((slots, 1, order, order), lambda m: (0, m, 0, 0)),
        scratch_shapes=[
            pltpu.VMEM((4 * spread, padded, order), jnp.float32),
            pltpu.VMEM((2 * spread, order, padded), jnp.bfloat16),
            pltpu.VMEM((4 * spread, order, padded), jnp.bfloat16),
            pltpu.VMEM((8 * LANES, order), jnp.bfloat16),
            pltpu.VMEM((6 * order, order), jnp.bfloat16),
            pltpu.SemaphoreType.DMA((4 * spread,)),
        ],
        compiler_params=params(40, dimension_semantics=("arbitrary",)),
        cost_estimate=cost(2**33, 2**24),
        name="schur",
    )(place, ranks, *flat, *inverses, rows, left_fac, right_fac)


def after(array, *others):
    return lax.optimization_barrier((array, *others))[0]


def device_program(capacity, diag_tiles, left_fac, right_fac, ranks):
    grid_rows = lax.axis_size("row")
    grid_cols = lax.axis_size("col")
    row_here = lax.axis_index("row")
    col_here = lax.axis_index("col")
    row_slots, _, order, cap = left_fac.shape
    assert cap == LANES and grid_rows % grid_cols == 0 and grid_cols >= 2
    spread = grid_rows // grid_cols
    row_bits = grid_rows.bit_length() - 1
    low_bits = grid_cols.bit_length() - 1
    assert 1 << row_bits == grid_rows and 1 << low_bits == grid_cols
    every_row = range(grid_rows)
    every_col = range(grid_cols)
    place = jnp.stack([row_here, col_here]).astype(jnp.int32)

    def move(array, pairs):
        flat = [(r * grid_cols + c, s * grid_cols + d) for (r, c), (s, d) in pairs]
        return lax.ppermute(array, AXES, flat)

    def down_column(array, root, fence):
        held = [root]
        for bit in range(1, row_bits):
            step = 1 << bit
            got = move(array, [((r, c), (r ^ step, c)) for r in held for c in every_col])
            array = after(jnp.where(row_here >> bit == 1, got, array), fence)
            held = held + [r ^ step for r in held]
        return array, move(array, [((r, c), (r ^ 1, c)) for r in held for c in every_col])

    packed, pivot_bases = pack(place, ranks, left_fac, right_fac, capacity, grid_rows)

    tile = down_column(diag_tiles[0], 0, packed)

    def chain_step(array, s):
        return move(array, [((r, c - 1), (r, c)) for c in (s, s + 1) if c < grid_cols for r in every_row])

    chain = [packed, chain_step(packed, 1)]
    back = move(packed, [((r, 1), (r, 0)) for r in every_row])

    pivot_bases = after(pivot_bases, tile[0])
    received = [move(pivot_bases, [((1, 0), (1, c))]) for c in every_col if c]
    pivot_bases = jnp.where(col_here == 0, pivot_bases, sum(received))
    head = down_column(jnp.concatenate([diag_tiles[0], pivot_bases], axis=0), 1, chain[1])

    inverse0 = first_inverse(place, *[after(array, chain[1]) for array in tile])
    for s in range(2, grid_cols):
        chain.append(chain_step(after(chain[s - 1], inverse0) if s == 3 else chain[s - 1], s))

    firsts = chain
    seconds = [back] + chain[:-1]
    offset = (row_here ^ col_here) & (grid_cols - 1)
    held = {c: [c] for c in every_col}

    def hop(array, bit, held):
        step = 1 << bit
        return move(
            array,
            [
                ((r + h * grid_cols, c), ((r + h * grid_cols) ^ step, c))
                for c in every_col
                for r in held[c]
                for h in range(spread)
            ],
        )

    def along_column(candidates, fence):
        have = pick(jnp.where(offset == 0, col_here, -1), candidates)
        held = {c: [c] for c in every_col}
        for bit in range(1, low_bits):
            got = hop(have, bit, held)
            arrived = (offset >> bit == 1) & (offset & 1 == 0)
            stays = (offset >> bit == 0) & (offset & 1 == 0)
            have = pick(jnp.where(arrived, 1, jnp.where(stays, 0, -1)), [have, got])
            held = {c: held[c] + [r ^ (1 << bit) for r in held[c]] for c in every_col}
        have = after(have, fence)
        sets = [have]
        for bit in range(low_bits, row_bits):
            sets = sets + [hop(array, bit, held) for array in sets]
        return [[array, hop(array, 0, held)] for array in sets]

    head = [after(array, chain[min(2, grid_cols - 1)]) for array in head]
    inverse1, mixing = second_inverse(place, ranks, *head, inverse0)
    inverses = (inverse0, inverse1, mixing)
    rows = row_panels(place, ranks, firsts, seconds, inverses, capacity, row_slots, grid_rows)
    second_sets = along_column(seconds, inverse1)
    first_sets = along_column([firsts[0], *[after(array, inverse1) for array in firsts[1:]]], rows)
    col_arrays = [sets[g] for g in range(spread) for sets in (first_sets, second_sets)]
    return schur(place, ranks, col_arrays, inverses, rows, left_fac, right_fac, capacity, grid_rows, grid_cols)


def shards(diag_tiles, left_fac, right_fac, ranks):
    row_slots, cap = left_fac.shape[0], left_fac.shape[3]
    grid_rows = lax.axis_size("row")
    full = row_slots * cap
    packed = max(cap, full * 5 // 8)
    args = (diag_tiles, left_fac, right_fac, ranks)
    if packed == full:
        return device_program(full, *args)
    tile_ids = jnp.arange(ranks.shape[0], dtype=jnp.int32)[:, None]
    live = jnp.where(tile_ids > jnp.arange(2, dtype=jnp.int32)[None, :], ranks[:, :2], 0)
    widest = jnp.max(sum(live[s * grid_rows : (s + 1) * grid_rows] for s in range(row_slots)))
    return lax.cond(
        widest <= packed,
        functools.partial(device_program, packed),
        functools.partial(device_program, full),
        *args,
    )


def solution(mesh):
    in_specs = (P("row", None, None), P("row", "col", None, None), P("row", "col", None, None), P())
    out_specs = P("row", "col", None, None)
    return jax.shard_map(shards, mesh=mesh, in_specs=in_specs, out_specs=out_specs, check_vma=False)
```

```python
import functools

import jax
import jax.numpy as jnp
from jax import lax
from jax.experimental import pallas as pl
from jax.experimental.pallas import tpu as pltpu
from jax.sharding import PartitionSpec as P

PRECISE = lax.Precision.HIGHEST
AXES = ("row", "col")
BLOCK = 32
GROUP = 8
LANES = 128
NT = (((1,), (1,)), ((), ()))
TN = (((0,), (0,)), ((), ()))
NN = (((1,), (0,)), ((), ()))
ANYWHERE = pl.BlockSpec(memory_space=pl.ANY)
IN_VMEM = pl.BlockSpec(memory_space=pltpu.VMEM)
IN_SMEM = pl.BlockSpec(memory_space=pltpu.SMEM)
IN_HBM = pl.BlockSpec(memory_space=pltpu.HBM)
MEBI = 1024 * 1024


def dot32(lhs, rhs, dims):
    return lax.dot_general(lhs, rhs, dims, precision=PRECISE, preferred_element_type=jnp.float32)


def dot16(lhs, rhs, dims):
    return lax.dot_general(lhs, rhs, dims, preferred_element_type=jnp.float32)


def split2(value):
    high = value.astype(jnp.bfloat16)
    low = (value - high.astype(jnp.float32)).astype(jnp.bfloat16)
    return high, low


def params(mebibytes, **extra):
    return pltpu.CompilerParams(vmem_limit_bytes=mebibytes * MEBI, **extra)


def cost(flops, moved):
    return pl.CostEstimate(flops=int(flops), bytes_accessed=int(moved), transcendentals=0)


def eliminate(tiles):
    tiles, start = tiles
    rows = tiles[0].shape[0]
    done = []
    for first in range(0, rows, GROUP):
        height = rows - first
        row_ids = lax.broadcasted_iota(jnp.int32, (height, LANES), 0)
        heads = [
            jnp.broadcast_to(tiles[0][:, start + first + j : start + first + j + 1], (height, LANES))
            for j in range(GROUP)
        ]
        scale = jnp.zeros((GROUP, LANES), jnp.float32)
        for j in range(GROUP):
            pivot = heads[j][j : j + 1, :]
            factor = jnp.where(row_ids > j, heads[j] * (1.0 / pivot), 0.0)
            for other in range(j + 1, GROUP):
                heads[other] = heads[other] - factor * heads[other][j : j + 1, :]
            tiles = [tile - factor * tile[j : j + 1, :] for tile in tiles]
            root = lax.rsqrt(pivot)
            root = root * (1.5 - 0.5 * pivot * root * root)
            scale = jnp.where(row_ids[:GROUP] == j, root, scale)
        done.append([tile[:GROUP] * scale for tile in tiles])
        tiles = [tile[GROUP:] for tile in tiles]
    return [jnp.concatenate(parts, axis=0) for parts in zip(*done)]


def inverse_factor(source, work, result):
    order = source.shape[0]
    span = order // LANES
    for base in range(0, order, BLOCK):
        low = base // LANES
        row_ids = lax.broadcasted_iota(jnp.int32, (BLOCK, LANES), 0)
        lane_ids = lax.broadcasted_iota(jnp.int32, (BLOCK, LANES), 1)
        unit = jnp.where(lane_ids - base % LANES == row_ids, 1.0, 0.0)
        zero = jnp.zeros((BLOCK, LANES), jnp.float32)
        tiles = [source[base : base + BLOCK, s * LANES : (s + 1) * LANES] for s in range(low, span)]
        tiles += [zero] * low + [unit]
        if base:
            taken = dot32(
                work[0:base, base : base + BLOCK],
                work[0:base, low * LANES : order + (low + 1) * LANES],
                TN,
            )
            tiles = [tile - taken[:, s * LANES : (s + 1) * LANES] for s, tile in enumerate(tiles)]
        tiles = eliminate((tiles, base % LANES))
        for s, tile in enumerate(tiles):
            work[base : base + BLOCK, (low + s) * LANES : (low + s + 1) * LANES] = tile
        for s in range(low + 1, span):
            work[base : base + BLOCK, order + s * LANES : order + (s + 1) * LANES] = zero
    result[...] = work[:, order:]


def fetch(choice, candidates, target, sem):
    for n, candidate in enumerate(candidates):
        copy = pltpu.make_async_copy(candidate, target, sem)
        pl.when(choice == n)(copy.start)
    return pltpu.make_async_copy(candidates[0], target, sem).wait


def first_kernel(place, own, got, result, tile, work, sem):
    fetch(place[0] % 2, (own, got), tile, sem)()
    inverse_factor(tile, work, result)


def first_inverse(place, own, got):
    order = own.shape[1]
    return pl.pallas_call(
        first_kernel,
        out_shape=jax.ShapeDtypeStruct((order, order), jnp.float32),
        in_specs=[IN_SMEM, ANYWHERE, ANYWHERE],
        out_specs=IN_VMEM,
        scratch_shapes=[
            pltpu.VMEM((order, order), jnp.float32),
            pltpu.VMEM((order, 2 * order), jnp.float32),
            pltpu.SemaphoreType.DMA,
        ],
        compiler_params=params(8),
        cost_estimate=cost(2**10, 2**10),
        name="first_inverse",
    )(place, own, got)


def second_kernel(place, ranks, own, got, inverse, weights, head, work, held, sems):
    order = inverse.shape[0]
    cap = (head.shape[0] - order) // 2
    fetch(1 - place[0] % 2, (own, got), head, sems.at[0])()
    held[:order, :] = inverse[...]
    live = lax.broadcasted_iota(jnp.int32, (cap, order), 0) < ranks[1, 0]
    left = jnp.where(live, head[order : order + cap, :], 0.0)
    right = jnp.where(live, head[order + cap :, :], 0.0)
    solved = dot32(right, inverse[...], NT)
    dense = dot32(left, solved, TN)
    shifted = head.at[pl.ds(0, order)]
    shifted[...] = shifted[...] - dot32(dense, dense, NT)
    inverse_factor(shifted, work, held.at[pl.ds(2 * order, order)])
    held[order : 2 * order, :] = -dot32(dot32(held[2 * order :, :], dense, NN), inverse[...], NN)
    copy = pltpu.make_async_copy(held, weights, sems.at[1])
    copy.start()
    copy.wait()


def second_inverse(place, ranks, own, got, inverse):
    order = inverse.shape[0]
    return pl.pallas_call(
        second_kernel,
        out_shape=pltpu.HBM((3 * order, order), jnp.float32),
        in_specs=[IN_SMEM, IN_SMEM, ANYWHERE, ANYWHERE, IN_VMEM],
        out_specs=IN_HBM,
        scratch_shapes=[
            pltpu.VMEM(own.shape, jnp.float32),
            pltpu.VMEM((order, 2 * order), jnp.float32),
            pltpu.VMEM((3 * order, order), jnp.float32),
            pltpu.SemaphoreType.DMA((2,)),
        ],
        compiler_params=params(8),
        cost_estimate=cost(2**10, 2**10),
        name="second_inverse",
    )(place, ranks, own, got, inverse)


def segment(ranks, panel, group, slot, slots, grid_rows):
    start, count = jnp.int32(0), jnp.int32(0)
    for s in range(slots):
        tile_row = s * grid_rows + group
        rank = jnp.where(tile_row > panel, ranks[tile_row, panel], 0)
        start = start + jnp.where(s < slot, rank, 0)
        count = count + jnp.where(s == slot, rank, 0)
    return start, count


def pack_kernel(capacity, grid_rows, place, ranks, left, right, packed, pivot, held, sem):
    slots, order, cap = held.shape[1:]
    copies = [
        pltpu.make_async_copy(source.at[:, 0], held.at[k], sem.at[k]) for k, source in enumerate((left, right))
    ]
    for copy in copies:
        copy.start()
    panel = jnp.minimum(place[1], 1)
    spot = lax.broadcasted_iota(jnp.int32, (capacity, cap), 0)
    column = lax.broadcasted_iota(jnp.int32, (capacity, cap), 1)
    chosen = []
    for slot in range(slots):
        start, count = segment(ranks, panel, place[0], slot, slots, grid_rows)
        hit = (spot - start == column) & (column < count)
        chosen.append(jnp.where(hit, 1.0, 0.0).astype(jnp.bfloat16))
    for k, copy in enumerate(copies):
        copy.wait()
        total = sum(dot16(chosen[slot], held[k, slot], NT) for slot in range(slots))
        packed[k * capacity : (k + 1) * capacity, :] = total
        pivot[k * cap : (k + 1) * cap, :] = total[:cap]


def pack(place, ranks, left_fac, right_fac, capacity, grid_rows):
    slots, _, order, cap = left_fac.shape
    return pl.pallas_call(
        functools.partial(pack_kernel, capacity, grid_rows),
        out_shape=(
            jax.ShapeDtypeStruct((2 * capacity, order), jnp.float32),
            jax.ShapeDtypeStruct((2 * cap, order), jnp.float32),
        ),
        in_specs=[IN_SMEM, IN_SMEM, IN_HBM, IN_HBM],
        out_specs=(IN_VMEM, IN_VMEM),
        scratch_shapes=[pltpu.VMEM((2, slots, order, cap), jnp.bfloat16), pltpu.SemaphoreType.DMA((2,))],
        compiler_params=params(16),
        cost_estimate=cost(2**10, 2**10),
        name="pack",
    )(place, ranks, left_fac, right_fac)


def pick_kernel(count, index, *refs):
    candidates, target, sem = refs[:count], refs[count], refs[count + 1]
    wait = fetch(index[0], candidates, target, sem)
    pl.when(index[0] >= 0)(wait)


def pick(index, candidates):
    return pl.pallas_call(
        functools.partial(pick_kernel, len(candidates)),
        out_shape=jax.ShapeDtypeStruct(candidates[0].shape, candidates[0].dtype),
        in_specs=[IN_SMEM] + [ANYWHERE] * len(candidates),
        out_specs=ANYWHERE,
        scratch_shapes=[pltpu.SemaphoreType.DMA],
        compiler_params=params(4),
        cost_estimate=cost(0, 2 * candidates[0].size * 4),
        name="pick",
    )(jnp.reshape(index, (1,)).astype(jnp.int32), *candidates)


def rows_kernel(capacity, grid_rows, count, place, ranks, *refs):
    sources, weights, stacked = refs[: 2 * count], refs[2 * count], refs[2 * count + 1]
    landed, inverses, weight_high, weight_low, sems = refs[2 * count + 2 :]
    order = inverses.shape[1]
    inverses_in = pltpu.make_async_copy(weights, inverses, sems.at[4])
    inverses_in.start()
    slots = stacked.shape[0]
    cap = LANES
    waits = []
    for t in range(2):
        for k in range(2):
            part = [source.at[pl.ds(k * capacity, capacity)] for source in sources[t * count : (t + 1) * count]]
            waits.append(fetch(place[1], part, landed.at[2 * t + k, pl.ds(0, capacity)], sems.at[2 * t + k]))
            landed[2 * t + k, capacity:, :] = jnp.zeros((cap, order), jnp.float32)
    inverses_in.wait()
    base_parts, second_parts = split2(inverses[: 2 * order, :]), split2(inverses[2 * order :, :])
    for wait in waits:
        wait()
    solved0 = sum(dot16(landed[1].astype(jnp.bfloat16), part, NT) for part in base_parts)
    solved1 = sum(dot16(landed[3].astype(jnp.bfloat16), part, NT) for part in second_parts)
    for column, value in ((0, solved0), (2 * order, solved1)):
        high, low = split2(value)
        weight_high[:, column : column + value.shape[1]] = high
        weight_low[:, column : column + value.shape[1]] = low
    live = lax.broadcasted_iota(jnp.int32, (cap, order), 0)
    for slot in range(slots):
        pieces = []
        for t in range(2):
            start, rank = segment(ranks, t, place[0], slot, slots, grid_rows)
            spot = pl.ds(pl.multiple_of(start, 16), cap)
            left = jnp.where(live < rank, landed[2 * t, spot, :], 0.0).astype(jnp.bfloat16)
            columns = pl.ds(0, 2 * order) if t == 0 else pl.ds(2 * order, order)
            weights = jnp.concatenate([weight_high[spot, columns], weight_low[spot, columns]], axis=0)
            pieces.append(dot16(jnp.concatenate([left, left], axis=0), weights, TN))
        for column, value in ((0, pieces[0][:, :order]), (order, pieces[0][:, order:] + pieces[1])):
            high, low = split2(value)
            stacked[slot, :, column : column + order] = high
            stacked[slot, :, 2 * order + column : 2 * order + column + order] = low
            stacked[slot, :, 4 * order + column : 4 * order + column + order] = high


def row_panels(place, ranks, firsts, seconds, inverses, capacity, slots, grid_rows):
    order = inverses.shape[1]
    count = len(firsts)
    spaces = [ANYWHERE] * count + [IN_HBM] + [ANYWHERE] * (count - 1)
    return pl.pallas_call(
        functools.partial(rows_kernel, capacity, grid_rows, count),
        out_shape=jax.ShapeDtypeStruct((slots, order, 6 * order), jnp.bfloat16),
        in_specs=[IN_SMEM] * 2 + spaces + [IN_HBM],
        out_specs=IN_VMEM,
        scratch_shapes=[
            pltpu.VMEM((4, capacity + LANES, order), jnp.float32),
            pltpu.VMEM((3 * order, order), jnp.float32),
            pltpu.VMEM((capacity + LANES, 3 * order), jnp.bfloat16),
            pltpu.VMEM((capacity + LANES, 3 * order), jnp.bfloat16),
            pltpu.SemaphoreType.DMA((5,)),
        ],
        compiler_params=params(20),
        cost_estimate=cost(2**32, 2**22),
        name="row_panels",
    )(place, ranks, *firsts, *seconds, inverses)


def schur_kernel(capacity, grid_rows, grid_cols, place, ranks, *refs):
    spread = grid_rows // grid_cols
    sources = refs[: 4 * spread]
    weights, rows, left, right, out = refs[4 * spread : 4 * spread + 5]
    landed, inverses, weight0, weight1, bases, panel, sems = refs[4 * spread + 5 :]
    slots, order, cap = out.shape[0], out.shape[2], left.shape[3]
    padded = landed.shape[1]
    step = pl.program_id(0)
    row_here, col_here = place[0], place[1]
    mine = row_here // grid_cols

    @pl.when(step == 0)
    def _():
        inverses_in = pltpu.make_async_copy(weights, inverses, sems.at[4 * spread])
        inverses_in.start()
        passed = (row_here ^ col_here) & 1
        waits = []
        for n in range(2 * spread):
            for k in range(2):
                part = [source.at[pl.ds(k * capacity, capacity)] for source in sources[2 * n : 2 * n + 2]]
                waits.append(fetch(passed, part, landed.at[2 * n + k, pl.ds(0, capacity)], sems.at[2 * n + k]))
                if padded > capacity:
                    landed[2 * n + k, capacity:, :] = jnp.zeros((padded - capacity, order), jnp.float32)
        inverses_in.wait()
        base_parts, second_parts = split2(inverses[: 2 * order, :]), split2(inverses[2 * order :, :])
        for wait in waits:
            wait()
        for g in range(spread):
            right0 = landed[4 * g + 1].astype(jnp.bfloat16)
            right1 = landed[4 * g + 3].astype(jnp.bfloat16)
            solved0 = sum(dot16(part, right0, NT) for part in base_parts)
            solved1 = sum(dot16(part, right1, NT) for part in second_parts)
            for target, at, value in (
                (weight0, 2 * g, solved0[:order]),
                (weight1, 4 * g, solved0[order:]),
                (weight1, 4 * g + 2, solved1),
            ):
                for n, piece in enumerate(split2(value)):
                    target[at + n] = piece

    tile_col = step * grid_cols + col_here
    last_row = (slots - 1) * grid_rows + row_here

    @pl.when((tile_col > 1) & (last_row > tile_col))
    def _():
        part = step % spread
        g = part ^ mine
        group = part * grid_cols + col_here
        span = 2 * LANES
        ids = lax.broadcasted_iota(jnp.int32, (span, order), 0)
        windows = []
        for t in range(2):
            start, count = segment(ranks, t, group, step // spread, slots, grid_rows)
            first_lane = start // LANES * LANES
            window = pl.ds(pl.multiple_of(first_lane, LANES), span)
            value = landed[4 * g + 2 * t, window, :]
            live = (ids >= start - first_lane) & (ids < start - first_lane + count)
            value = jnp.where(live, value, 0.0).astype(jnp.bfloat16)
            for n in range(2):
                bases[(2 * t + n) * span : (2 * t + n + 1) * span, :] = value
            windows.append(window)
        left0 = [weight0[2 * g + n, :, windows[0]] for n in range(2)]
        left1 = [weight1[4 * g + n, :, windows[n // 2]] for n in range(4)]
        panel0 = dot16(jnp.concatenate(left0, axis=1), bases[: 2 * span], NN)
        panel1 = dot16(jnp.concatenate(left1, axis=1), bases[...], NN)
        for at, value in ((0, panel0), (order, panel1)):
            high, low = split2(value)
            panel[at : at + order, :] = high
            panel[2 * order + at : 3 * order + at, :] = high
            panel[4 * order + at : 5 * order + at, :] = low

    for slot in range(slots):
        tile_row = slot * grid_rows + row_here
        below = tile_row > tile_col

        @pl.when(jnp.logical_not(below))
        def _():
            out[slot, 0] = jnp.zeros((order, order), jnp.float32)

        for t in range(2):

            @pl.when(below & (tile_col == t))
            def _():
                high = rows[slot, :, t * order : (t + 1) * order].astype(jnp.float32)
                low = rows[slot, :, (t + 2) * order : (t + 3) * order].astype(jnp.float32)
                out[slot, 0] = high + low

        @pl.when(below & (tile_col > 1))
        def _():
            basis = left[slot, 0].astype(jnp.float32)
            live = lax.broadcasted_iota(jnp.int32, basis.shape, 1) < ranks[tile_row, tile_col]
            front = dot16(jnp.where(live, basis, 0.0).astype(jnp.bfloat16), right[slot, 0], NT)
            out[slot, 0] = front - dot16(rows[slot], panel[...], NN)


def schur(place, ranks, col_arrays, inverses, rows, left_fac, right_fac, capacity, grid_rows, grid_cols):
    slots, steps, order, cap = left_fac.shape
    spread = grid_rows // grid_cols
    padded = (-(-capacity // LANES) + 1) * LANES
    flat = [array for pair in col_arrays for array in pair]
    factor = pl.BlockSpec((slots, 1, order, cap), lambda m: (0, m, 0, 0))
    return pl.pallas_call(
        functools.partial(schur_kernel, capacity, grid_rows, grid_cols),
        grid=(steps,),
        out_shape=pltpu.HBM((slots, steps, order, order), jnp.float32),
        in_specs=[IN_SMEM] * 2 + [ANYWHERE] * len(flat) + [IN_HBM, IN_VMEM, factor, factor],
        out_specs=pl.BlockSpec((slots, 1, order, order), lambda m: (0, m, 0, 0)),
        scratch_shapes=[
            pltpu.VMEM((4 * spread, padded, order), jnp.float32),
            pltpu.VMEM((3 * order, order), jnp.float32),
            pltpu.VMEM((2 * spread, order, padded), jnp.bfloat16),
            pltpu.VMEM((4 * spread, order, padded), jnp.bfloat16),
            pltpu.VMEM((8 * LANES, order), jnp.bfloat16),
            pltpu.VMEM((6 * order, order), jnp.bfloat16),
            pltpu.SemaphoreType.DMA((4 * spread + 1,)),
        ],
        compiler_params=params(40, dimension_semantics=("arbitrary",)),
        cost_estimate=cost(2**33, 2**24),
        name="schur",
    )(place, ranks, *flat, inverses, rows, left_fac, right_fac)


def after(array, *others):
    return lax.optimization_barrier((array, *others))[0]


def device_program(capacity, diag_tiles, left_fac, right_fac, ranks):
    grid_rows = lax.axis_size("row")
    grid_cols = lax.axis_size("col")
    row_here = lax.axis_index("row")
    col_here = lax.axis_index("col")
    row_slots, _, order, cap = left_fac.shape
    assert cap == LANES and grid_rows % grid_cols == 0 and grid_cols >= 2
    spread = grid_rows // grid_cols
    row_bits = grid_rows.bit_length() - 1
    low_bits = grid_cols.bit_length() - 1
    assert 1 << row_bits == grid_rows and 1 << low_bits == grid_cols
    every_row = range(grid_rows)
    every_col = range(grid_cols)
    place = jnp.stack([row_here, col_here]).astype(jnp.int32)

    def move(array, pairs):
        flat = [(r * grid_cols + c, s * grid_cols + d) for (r, c), (s, d) in pairs]
        return lax.ppermute(array, AXES, flat)

    def down_column(array, root, *fence):
        held = [root]
        for bit in range(1, row_bits):
            step = 1 << bit
            got = move(array, [((r, c), (r ^ step, c)) for r in held for c in every_col])
            array = after(jnp.where(row_here >> bit == 1, got, array), *fence)
            held = held + [r ^ step for r in held]
        return array

    def to_other_parity(array, root):
        return move(array, [((r, c), (r ^ 1, c)) for r in every_row if r % 2 == root for c in every_col])

    def chain_step(array, s):
        return move(array, [((r, c - 1), (r, c)) for c in (s, s + 1) if c < grid_cols for r in every_row])

    packed, pivot_bases = pack(place, ranks, left_fac, right_fac, capacity, grid_rows)
    chain = [packed, chain_step(packed, 1)]
    back = move(packed, [((r, 1), (r, 0)) for r in every_row])

    tile = after(down_column(diag_tiles[0], 0), chain[1])
    tile = [tile, to_other_parity(tile, 0)]

    pivot_bases = after(pivot_bases, tile[0])
    received = [move(pivot_bases, [((1, 0), (1, c))]) for c in every_col if c]
    pivot_bases = jnp.where(col_here == 0, pivot_bases, sum(received))
    head = down_column(jnp.concatenate([diag_tiles[0], pivot_bases], axis=0), 1, chain[1])
    head = [head, to_other_parity(head, 1)]

    inverse0 = first_inverse(place, *tile)
    for s in range(2, grid_cols):
        chain.append(chain_step(after(chain[s - 1], inverse0) if s == 3 else chain[s - 1], s))

    firsts = chain
    seconds = [back] + chain[:-1]
    offset = (row_here ^ col_here) & (grid_cols - 1)
    held = {c: [c] for c in every_col}

    def hop(array, bit, held):
        step = 1 << bit
        return move(
            array,
            [
                ((r + h * grid_cols, c), ((r + h * grid_cols) ^ step, c))
                for c in every_col
                for r in held[c]
                for h in range(spread)
            ],
        )

    def along_column(candidates, fence):
        have = pick(jnp.where(offset == 0, col_here, -1), candidates)
        held = {c: [c] for c in every_col}
        for bit in range(1, low_bits):
            got = hop(have, bit, held)
            arrived = (offset >> bit == 1) & (offset & 1 == 0)
            stays = (offset >> bit == 0) & (offset & 1 == 0)
            have = pick(jnp.where(arrived, 1, jnp.where(stays, 0, -1)), [have, got])
            held = {c: held[c] + [r ^ (1 << bit) for r in held[c]] for c in every_col}
        have = after(have, fence)
        sets = [have]
        for bit in range(low_bits, row_bits):
            sets = sets + [hop(array, bit, held) for array in sets]
        return [[array, hop(array, 0, held)] for array in sets]

    head = [after(array, chain[min(2, grid_cols - 1)]) for array in head]
    inverses = second_inverse(place, ranks, *head, inverse0)
    rows = row_panels(place, ranks, firsts, seconds, inverses, capacity, row_slots, grid_rows)
    second_sets = along_column(seconds, inverses)
    first_sets = along_column([firsts[0], *[after(array, inverses) for array in firsts[1:]]], rows)
    col_arrays = [sets[g] for g in range(spread) for sets in (first_sets, second_sets)]
    return schur(place, ranks, col_arrays, inverses, rows, left_fac, right_fac, capacity, grid_rows, grid_cols)


def shards(diag_tiles, left_fac, right_fac, ranks):
    row_slots, cap = left_fac.shape[0], left_fac.shape[3]
    grid_rows = lax.axis_size("row")
    full = row_slots * cap
    packed = max(cap, full * 5 // 8)
    args = (diag_tiles, left_fac, right_fac, ranks)
    if packed == full:
        return device_program(full, *args)
    tile_ids = jnp.arange(ranks.shape[0], dtype=jnp.int32)[:, None]
    live = jnp.where(tile_ids > jnp.arange(2, dtype=jnp.int32)[None, :], ranks[:, :2], 0)
    widest = jnp.max(sum(live[s * grid_rows : (s + 1) * grid_rows] for s in range(row_slots)))
    return lax.cond(
        widest <= packed,
        functools.partial(device_program, packed),
        functools.partial(device_program, full),
        *args,
    )


def solution(mesh):
    in_specs = (P("row", None, None), P("row", "col", None, None), P("row", "col", None, None), P())
    out_specs = P("row", "col", None, None)
    return jax.shard_map(shards, mesh=mesh, in_specs=in_specs, out_specs=out_specs, check_vma=False)
```

```python
import functools

import jax
import jax.numpy as jnp
from jax import lax
from jax.experimental import pallas as pl
from jax.experimental.pallas import tpu as pltpu
from jax.sharding import PartitionSpec as P

PRECISE = lax.Precision.HIGHEST
AXES = ("row", "col")
BLOCK = 32
GROUP = 8
LANES = 128
NT = (((1,), (1,)), ((), ()))
TN = (((0,), (0,)), ((), ()))
NN = (((1,), (0,)), ((), ()))
ANYWHERE = pl.BlockSpec(memory_space=pl.ANY)
IN_VMEM = pl.BlockSpec(memory_space=pltpu.VMEM)
IN_SMEM = pl.BlockSpec(memory_space=pltpu.SMEM)
IN_HBM = pl.BlockSpec(memory_space=pltpu.HBM)
MEBI = 1024 * 1024


def dot32(lhs, rhs, dims):
    return lax.dot_general(lhs, rhs, dims, precision=PRECISE, preferred_element_type=jnp.float32)


def dot16(lhs, rhs, dims):
    return lax.dot_general(lhs, rhs, dims, preferred_element_type=jnp.float32)


def split2(value):
    high = value.astype(jnp.bfloat16)
    low = (value - high.astype(jnp.float32)).astype(jnp.bfloat16)
    return high, low


def params(mebibytes, **extra):
    return pltpu.CompilerParams(vmem_limit_bytes=mebibytes * MEBI, **extra)


def cost(flops, moved):
    return pl.CostEstimate(flops=int(flops), bytes_accessed=int(moved), transcendentals=0)


def eliminate(tiles):
    tiles, start = tiles
    rows = tiles[0].shape[0]
    done = []
    for first in range(0, rows, GROUP):
        height = rows - first
        row_ids = lax.broadcasted_iota(jnp.int32, (height, LANES), 0)
        heads = [
            jnp.broadcast_to(tiles[0][:, start + first + j : start + first + j + 1], (height, LANES))
            for j in range(GROUP)
        ]
        scale = jnp.zeros((GROUP, LANES), jnp.float32)
        for j in range(GROUP):
            pivot = heads[j][j : j + 1, :]
            factor = jnp.where(row_ids > j, heads[j] * (1.0 / pivot), 0.0)
            for other in range(j + 1, GROUP):
                heads[other] = heads[other] - factor * heads[other][j : j + 1, :]
            tiles = [tile - factor * tile[j : j + 1, :] for tile in tiles]
            root = lax.rsqrt(pivot)
            root = root * (1.5 - 0.5 * pivot * root * root)
            scale = jnp.where(row_ids[:GROUP] == j, root, scale)
        done.append([tile[:GROUP] * scale for tile in tiles])
        tiles = [tile[GROUP:] for tile in tiles]
    return [jnp.concatenate(parts, axis=0) for parts in zip(*done)]


def inverse_factor(source, work, result):
    order = source.shape[0]
    span = order // LANES
    for base in range(0, order, BLOCK):
        low = base // LANES
        row_ids = lax.broadcasted_iota(jnp.int32, (BLOCK, LANES), 0)
        lane_ids = lax.broadcasted_iota(jnp.int32, (BLOCK, LANES), 1)
        unit = jnp.where(lane_ids - base % LANES == row_ids, 1.0, 0.0)
        zero = jnp.zeros((BLOCK, LANES), jnp.float32)
        tiles = [source[base : base + BLOCK, s * LANES : (s + 1) * LANES] for s in range(low, span)]
        tiles += [zero] * low + [unit]
        if base:
            taken = dot32(
                work[0:base, base : base + BLOCK],
                work[0:base, low * LANES : order + (low + 1) * LANES],
                TN,
            )
            tiles = [tile - taken[:, s * LANES : (s + 1) * LANES] for s, tile in enumerate(tiles)]
        tiles = eliminate((tiles, base % LANES))
        for s, tile in enumerate(tiles):
            work[base : base + BLOCK, (low + s) * LANES : (low + s + 1) * LANES] = tile
        for s in range(low + 1, span):
            work[base : base + BLOCK, order + s * LANES : order + (s + 1) * LANES] = zero
    result[...] = work[:, order:]


def fetch(choice, candidates, target, sem):
    for n, candidate in enumerate(candidates):
        copy = pltpu.make_async_copy(candidate, target, sem)
        pl.when(choice == n)(copy.start)
    return pltpu.make_async_copy(candidates[0], target, sem).wait


def first_kernel(tile, result, work):
    inverse_factor(tile, work, result)


def first_inverse(tile):
    order = tile.shape[1]
    return pl.pallas_call(
        first_kernel,
        out_shape=jax.ShapeDtypeStruct((order, order), jnp.float32),
        in_specs=[IN_VMEM],
        out_specs=IN_VMEM,
        scratch_shapes=[pltpu.VMEM((order, 2 * order), jnp.float32)],
        compiler_params=params(8),
        cost_estimate=cost(2**10, 2**10),
        name="first_inverse",
    )(tile)


def second_kernel(ranks, tile, bases, inverse, weights, shifted, work, held, sem):
    order = inverse.shape[0]
    cap = bases.shape[0] // 2
    held[:order, :] = inverse[...]
    live = lax.broadcasted_iota(jnp.int32, (cap, order), 0) < ranks[1, 0]
    left = jnp.where(live, bases[:cap, :], 0.0)
    right = jnp.where(live, bases[cap:, :], 0.0)
    solved = dot32(right, inverse[...], NT)
    dense = dot32(left, solved, TN)
    shifted[...] = tile[...] - dot32(dense, dense, NT)
    inverse_factor(shifted, work, held.at[pl.ds(2 * order, order)])
    held[order : 2 * order, :] = -dot32(dot32(held[2 * order :, :], dense, NN), inverse[...], NN)
    copy = pltpu.make_async_copy(held, weights, sem)
    copy.start()
    copy.wait()


def second_inverse(ranks, tile, bases, inverse):
    order = inverse.shape[0]
    return pl.pallas_call(
        second_kernel,
        out_shape=pltpu.HBM((3 * order, order), jnp.float32),
        in_specs=[IN_SMEM, IN_VMEM, IN_VMEM, IN_VMEM],
        out_specs=IN_HBM,
        scratch_shapes=[
            pltpu.VMEM((order, order), jnp.float32),
            pltpu.VMEM((order, 2 * order), jnp.float32),
            pltpu.VMEM((3 * order, order), jnp.float32),
            pltpu.SemaphoreType.DMA,
        ],
        compiler_params=params(8),
        cost_estimate=cost(2**10, 2**10),
        name="second_inverse",
    )(ranks, tile, bases, inverse)


def segment(ranks, panel, group, slot, slots, grid_rows):
    start, count = jnp.int32(0), jnp.int32(0)
    for s in range(slots):
        tile_row = s * grid_rows + group
        rank = jnp.where(tile_row > panel, ranks[tile_row, panel], 0)
        start = start + jnp.where(s < slot, rank, 0)
        count = count + jnp.where(s == slot, rank, 0)
    return start, count


def pack_kernel(capacity, grid_rows, place, ranks, left, right, packed, pivot, held, sem):
    slots, order, cap = held.shape[1:]
    copies = [
        pltpu.make_async_copy(source.at[:, 0], held.at[k], sem.at[k]) for k, source in enumerate((left, right))
    ]
    for copy in copies:
        copy.start()
    panel = jnp.minimum(place[1], 1)
    spot = lax.broadcasted_iota(jnp.int32, (capacity, cap), 0)
    column = lax.broadcasted_iota(jnp.int32, (capacity, cap), 1)
    chosen = []
    for slot in range(slots):
        start, count = segment(ranks, panel, place[0], slot, slots, grid_rows)
        hit = (spot - start == column) & (column < count)
        chosen.append(jnp.where(hit, 1.0, 0.0).astype(jnp.bfloat16))
    for k, copy in enumerate(copies):
        copy.wait()
        total = sum(dot16(chosen[slot], held[k, slot], NT) for slot in range(slots))
        packed[k * capacity : (k + 1) * capacity, :] = total
        pivot[k * cap : (k + 1) * cap, :] = total[:cap]


def pack(place, ranks, left_fac, right_fac, capacity, grid_rows):
    slots, _, order, cap = left_fac.shape
    return pl.pallas_call(
        functools.partial(pack_kernel, capacity, grid_rows),
        out_shape=(
            jax.ShapeDtypeStruct((2 * capacity, order), jnp.float32),
            jax.ShapeDtypeStruct((2 * cap, order), jnp.float32),
        ),
        in_specs=[IN_SMEM, IN_SMEM, IN_HBM, IN_HBM],
        out_specs=(IN_VMEM, IN_VMEM),
        scratch_shapes=[pltpu.VMEM((2, slots, order, cap), jnp.bfloat16), pltpu.SemaphoreType.DMA((2,))],
        compiler_params=params(16),
        cost_estimate=cost(2**10, 2**10),
        name="pack",
    )(place, ranks, left_fac, right_fac)


def pick_kernel(count, index, *refs):
    candidates, target, sem = refs[:count], refs[count], refs[count + 1]
    wait = fetch(index[0], candidates, target, sem)
    pl.when(index[0] >= 0)(wait)


def pick(index, candidates):
    return pl.pallas_call(
        functools.partial(pick_kernel, len(candidates)),
        out_shape=jax.ShapeDtypeStruct(candidates[0].shape, candidates[0].dtype),
        in_specs=[IN_SMEM] + [ANYWHERE] * len(candidates),
        out_specs=ANYWHERE,
        scratch_shapes=[pltpu.SemaphoreType.DMA],
        compiler_params=params(4),
        cost_estimate=cost(0, 2 * candidates[0].size * 4),
        name="pick",
    )(jnp.reshape(index, (1,)).astype(jnp.int32), *candidates)


def rows_kernel(capacity, grid_rows, count, place, ranks, *refs):
    sources, weights, stacked = refs[: 2 * count], refs[2 * count], refs[2 * count + 1]
    landed, inverses, weight_high, weight_low, sems = refs[2 * count + 2 :]
    order = inverses.shape[1]
    inverses_in = pltpu.make_async_copy(weights, inverses, sems.at[4])
    inverses_in.start()
    slots = stacked.shape[0]
    cap = LANES
    waits = []
    for t in range(2):
        for k in range(2):
            part = [source.at[pl.ds(k * capacity, capacity)] for source in sources[t * count : (t + 1) * count]]
            waits.append(fetch(place[1], part, landed.at[2 * t + k, pl.ds(0, capacity)], sems.at[2 * t + k]))
            landed[2 * t + k, capacity:, :] = jnp.zeros((cap, order), jnp.float32)
    inverses_in.wait()
    base_parts, second_parts = split2(inverses[: 2 * order, :]), split2(inverses[2 * order :, :])
    for wait in waits:
        wait()
    solved0 = sum(dot16(landed[1].astype(jnp.bfloat16), part, NT) for part in base_parts)
    solved1 = sum(dot16(landed[3].astype(jnp.bfloat16), part, NT) for part in second_parts)
    for column, value in ((0, solved0), (2 * order, solved1)):
        high, low = split2(value)
        weight_high[:, column : column + value.shape[1]] = high
        weight_low[:, column : column + value.shape[1]] = low
    live = lax.broadcasted_iota(jnp.int32, (cap, order), 0)
    for slot in range(slots):
        pieces = []
        for t in range(2):
            start, rank = segment(ranks, t, place[0], slot, slots, grid_rows)
            spot = pl.ds(pl.multiple_of(start, 16), cap)
            left = jnp.where(live < rank, landed[2 * t, spot, :], 0.0).astype(jnp.bfloat16)
            columns = pl.ds(0, 2 * order) if t == 0 else pl.ds(2 * order, order)
            weights = jnp.concatenate([weight_high[spot, columns], weight_low[spot, columns]], axis=0)
            pieces.append(dot16(jnp.concatenate([left, left], axis=0), weights, TN))
        for column, value in ((0, pieces[0][:, :order]), (order, pieces[0][:, order:] + pieces[1])):
            high, low = split2(value)
            stacked[slot, :, column : column + order] = high
            stacked[slot, :, 2 * order + column : 2 * order + column + order] = low
            stacked[slot, :, 4 * order + column : 4 * order + column + order] = high


def row_panels(place, ranks, firsts, seconds, inverses, capacity, slots, grid_rows):
    order = inverses.shape[1]
    count = len(firsts)
    spaces = [ANYWHERE] * count + [IN_HBM] + [ANYWHERE] * (count - 1)
    return pl.pallas_call(
        functools.partial(rows_kernel, capacity, grid_rows, count),
        out_shape=jax.ShapeDtypeStruct((slots, order, 6 * order), jnp.bfloat16),
        in_specs=[IN_SMEM] * 2 + spaces + [IN_HBM],
        out_specs=IN_VMEM,
        scratch_shapes=[
            pltpu.VMEM((4, capacity + LANES, order), jnp.float32),
            pltpu.VMEM((3 * order, order), jnp.float32),
            pltpu.VMEM((capacity + LANES, 3 * order), jnp.bfloat16),
            pltpu.VMEM((capacity + LANES, 3 * order), jnp.bfloat16),
            pltpu.SemaphoreType.DMA((5,)),
        ],
        compiler_params=params(20),
        cost_estimate=cost(2**32, 2**22),
        name="row_panels",
    )(place, ranks, *firsts, *seconds, inverses)


def schur_kernel(capacity, grid_rows, grid_cols, place, ranks, *refs):
    spread = grid_rows // grid_cols
    sources = refs[: 4 * spread]
    weights, rows, left, right, out = refs[4 * spread : 4 * spread + 5]
    landed, inverses, weight0, weight1, bases, panel, sems = refs[4 * spread + 5 :]
    slots, order, cap = out.shape[0], out.shape[2], left.shape[3]
    padded = landed.shape[1]
    step = pl.program_id(0)
    row_here, col_here = place[0], place[1]
    mine = row_here // grid_cols

    @pl.when(step == 0)
    def _():
        inverses_in = pltpu.make_async_copy(weights, inverses, sems.at[4 * spread])
        inverses_in.start()
        passed = (row_here ^ col_here) & 1
        waits = []
        for n in range(2 * spread):
            for k in range(2):
                part = [source.at[pl.ds(k * capacity, capacity)] for source in sources[2 * n : 2 * n + 2]]
                waits.append(fetch(passed, part, landed.at[2 * n + k, pl.ds(0, capacity)], sems.at[2 * n + k]))
                if padded > capacity:
                    landed[2 * n + k, capacity:, :] = jnp.zeros((padded - capacity, order), jnp.float32)
        inverses_in.wait()
        base_parts, second_parts = split2(inverses[: 2 * order, :]), split2(inverses[2 * order :, :])
        for wait in waits:
            wait()
        for g in range(spread):
            right0 = landed[4 * g + 1].astype(jnp.bfloat16)
            right1 = landed[4 * g + 3].astype(jnp.bfloat16)
            solved0 = sum(dot16(part, right0, NT) for part in base_parts)
            solved1 = sum(dot16(part, right1, NT) for part in second_parts)
            for target, at, value in (
                (weight0, 2 * g, solved0[:order]),
                (weight1, 4 * g, solved0[order:]),
                (weight1, 4 * g + 2, solved1),
            ):
                for n, piece in enumerate(split2(value)):
                    target[at + n] = piece

    tile_col = step * grid_cols + col_here
    last_row = (slots - 1) * grid_rows + row_here

    @pl.when((tile_col > 1) & (last_row > tile_col))
    def _():
        part = step % spread
        g = part ^ mine
        group = part * grid_cols + col_here
        span = 2 * LANES
        ids = lax.broadcasted_iota(jnp.int32, (span, order), 0)
        windows = []
        for t in range(2):
            start, count = segment(ranks, t, group, step // spread, slots, grid_rows)
            first_lane = start // LANES * LANES
            window = pl.ds(pl.multiple_of(first_lane, LANES), span)
            value = landed[4 * g + 2 * t, window, :]
            live = (ids >= start - first_lane) & (ids < start - first_lane + count)
            value = jnp.where(live, value, 0.0).astype(jnp.bfloat16)
            for n in range(2):
                bases[(2 * t + n) * span : (2 * t + n + 1) * span, :] = value
            windows.append(window)
        left0 = [weight0[2 * g + n, :, windows[0]] for n in range(2)]
        left1 = [weight1[4 * g + n, :, windows[n // 2]] for n in range(4)]
        panel0 = dot16(jnp.concatenate(left0, axis=1), bases[: 2 * span], NN)
        panel1 = dot16(jnp.concatenate(left1, axis=1), bases[...], NN)
        for at, value in ((0, panel0), (order, panel1)):
            high, low = split2(value)
            panel[at : at + order, :] = high
            panel[2 * order + at : 3 * order + at, :] = high
            panel[4 * order + at : 5 * order + at, :] = low

    for slot in range(slots):
        tile_row = slot * grid_rows + row_here
        below = tile_row > tile_col

        @pl.when(jnp.logical_not(below))
        def _():
            out[slot, 0] = jnp.zeros((order, order), jnp.float32)

        for t in range(2):

            @pl.when(below & (tile_col == t))
            def _():
                high = rows[slot, :, t * order : (t + 1) * order].astype(jnp.float32)
                low = rows[slot, :, (t + 2) * order : (t + 3) * order].astype(jnp.float32)
                out[slot, 0] = high + low

        @pl.when(below & (tile_col > 1))
        def _():
            basis = left[slot, 0].astype(jnp.float32)
            live = lax.broadcasted_iota(jnp.int32, basis.shape, 1) < ranks[tile_row, tile_col]
            front = dot16(jnp.where(live, basis, 0.0).astype(jnp.bfloat16), right[slot, 0], NT)
            out[slot, 0] = front - dot16(rows[slot], panel[...], NN)


def schur(place, ranks, col_arrays, inverses, rows, left_fac, right_fac, capacity, grid_rows, grid_cols):
    slots, steps, order, cap = left_fac.shape
    spread = grid_rows // grid_cols
    padded = (-(-capacity // LANES) + 1) * LANES
    flat = [array for pair in col_arrays for array in pair]
    factor = pl.BlockSpec((slots, 1, order, cap), lambda m: (0, m, 0, 0))
    return pl.pallas_call(
        functools.partial(schur_kernel, capacity, grid_rows, grid_cols),
        grid=(steps,),
        out_shape=pltpu.HBM((slots, steps, order, order), jnp.float32),
        in_specs=[IN_SMEM] * 2 + [ANYWHERE] * len(flat) + [IN_HBM, IN_VMEM, factor, factor],
        out_specs=pl.BlockSpec((slots, 1, order, order), lambda m: (0, m, 0, 0)),
        scratch_shapes=[
            pltpu.VMEM((4 * spread, padded, order), jnp.float32),
            pltpu.VMEM((3 * order, order), jnp.float32),
            pltpu.VMEM((2 * spread, order, padded), jnp.bfloat16),
            pltpu.VMEM((4 * spread, order, padded), jnp.bfloat16),
            pltpu.VMEM((8 * LANES, order), jnp.bfloat16),
            pltpu.VMEM((6 * order, order), jnp.bfloat16),
            pltpu.SemaphoreType.DMA((4 * spread + 1,)),
        ],
        compiler_params=params(40, dimension_semantics=("arbitrary",)),
        cost_estimate=cost(2**33, 2**24),
        name="schur",
    )(place, ranks, *flat, inverses, rows, left_fac, right_fac)


def after(array, *others):
    return lax.optimization_barrier((array, *others))[0]


def device_program(capacity, diag_tiles, left_fac, right_fac, ranks):
    grid_rows = lax.axis_size("row")
    grid_cols = lax.axis_size("col")
    row_here = lax.axis_index("row")
    col_here = lax.axis_index("col")
    row_slots, _, order, cap = left_fac.shape
    assert cap == LANES and grid_rows % grid_cols == 0 and grid_cols >= 2
    spread = grid_rows // grid_cols
    row_bits = grid_rows.bit_length() - 1
    low_bits = grid_cols.bit_length() - 1
    assert 1 << row_bits == grid_rows and 1 << low_bits == grid_cols
    every_row = range(grid_rows)
    every_col = range(grid_cols)
    place = jnp.stack([row_here, col_here]).astype(jnp.int32)

    def move(array, pairs):
        flat = [(r * grid_cols + c, s * grid_cols + d) for (r, c), (s, d) in pairs]
        return lax.ppermute(array, AXES, flat)

    def when(mine, array):
        return jnp.where(mine, array, 0.0)

    tile = diag_tiles[0]
    tiles = lax.psum(jnp.stack([when(row_here == 0, tile), when(row_here == 1, tile)]), "row")

    def chain_step(array, s):
        return move(array, [((r, c - 1), (r, c)) for c in (s, s + 1) if c < grid_cols for r in every_row])

    packed, pivot_bases = pack(place, ranks, left_fac, right_fac, capacity, grid_rows)
    chain = [packed, chain_step(packed, 1)]
    back = move(packed, [((r, 1), (r, 0)) for r in every_row])

    pivot_bases = lax.psum(when((row_here == 1) & (col_here == 0), pivot_bases), AXES)

    inverse0 = first_inverse(tiles[0])
    for s in range(2, grid_cols):
        fence = {2: (tiles,), 3: (inverse0, pivot_bases)}.get(s, ())
        chain.append(chain_step(after(chain[s - 1], *fence) if fence else chain[s - 1], s))

    firsts = chain
    seconds = [back] + chain[:-1]
    offset = (row_here ^ col_here) & (grid_cols - 1)
    held = {c: [c] for c in every_col}

    def hop(array, bit, held):
        step = 1 << bit
        return move(
            array,
            [
                ((r + h * grid_cols, c), ((r + h * grid_cols) ^ step, c))
                for c in every_col
                for r in held[c]
                for h in range(spread)
            ],
        )

    def along_column(candidates, fence):
        have = pick(jnp.where(offset == 0, col_here, -1), candidates)
        held = {c: [c] for c in every_col}
        for bit in range(1, low_bits):
            got = hop(have, bit, held)
            arrived = (offset >> bit == 1) & (offset & 1 == 0)
            stays = (offset >> bit == 0) & (offset & 1 == 0)
            have = pick(jnp.where(arrived, 1, jnp.where(stays, 0, -1)), [have, got])
            held = {c: held[c] + [r ^ (1 << bit) for r in held[c]] for c in every_col}
        have = after(have, fence)
        sets = [have]
        for bit in range(low_bits, row_bits):
            sets = sets + [hop(array, bit, held) for array in sets]
        return [[array, hop(array, 0, held)] for array in sets]

    second_tile = after(tiles[1], chain[min(2, grid_cols - 1)])
    inverses = second_inverse(ranks, second_tile, pivot_bases, inverse0)
    rows = row_panels(place, ranks, firsts, seconds, inverses, capacity, row_slots, grid_rows)
    second_sets = along_column(seconds, inverses)
    first_sets = along_column([firsts[0], *[after(array, inverses) for array in firsts[1:]]], rows)
    col_arrays = [sets[g] for g in range(spread) for sets in (first_sets, second_sets)]
    return schur(place, ranks, col_arrays, inverses, rows, left_fac, right_fac, capacity, grid_rows, grid_cols)


def shards(diag_tiles, left_fac, right_fac, ranks):
    row_slots, cap = left_fac.shape[0], left_fac.shape[3]
    grid_rows = lax.axis_size("row")
    full = row_slots * cap
    packed = max(cap, full * 5 // 8)
    args = (diag_tiles, left_fac, right_fac, ranks)
    if packed == full:
        return device_program(full, *args)
    tile_ids = jnp.arange(ranks.shape[0], dtype=jnp.int32)[:, None]
    live = jnp.where(tile_ids > jnp.arange(2, dtype=jnp.int32)[None, :], ranks[:, :2], 0)
    widest = jnp.max(sum(live[s * grid_rows : (s + 1) * grid_rows] for s in range(row_slots)))
    return lax.cond(
        widest <= packed,
        functools.partial(device_program, packed),
        functools.partial(device_program, full),
        *args,
    )


def solution(mesh):
    in_specs = (P("row", None, None), P("row", "col", None, None), P("row", "col", None, None), P())
    out_specs = P("row", "col", None, None)
    return jax.shard_map(shards, mesh=mesh, in_specs=in_specs, out_specs=out_specs, check_vma=False)
```

```python
import functools

import jax
import jax.numpy as jnp
from jax import lax
from jax.experimental import pallas as pl
from jax.experimental.pallas import tpu as pltpu
from jax.sharding import PartitionSpec as P

PRECISE = lax.Precision.HIGHEST
AXES = ("row", "col")
BLOCK = 32
GROUP = 8
LANES = 128
NT = (((1,), (1,)), ((), ()))
TN = (((0,), (0,)), ((), ()))
NN = (((1,), (0,)), ((), ()))
ANYWHERE = pl.BlockSpec(memory_space=pl.ANY)
IN_VMEM = pl.BlockSpec(memory_space=pltpu.VMEM)
IN_SMEM = pl.BlockSpec(memory_space=pltpu.SMEM)
IN_HBM = pl.BlockSpec(memory_space=pltpu.HBM)
MEBI = 1024 * 1024


def dot32(lhs, rhs, dims):
    return lax.dot_general(lhs, rhs, dims, precision=PRECISE, preferred_element_type=jnp.float32)


def dot16(lhs, rhs, dims):
    return lax.dot_general(lhs, rhs, dims, preferred_element_type=jnp.float32)


def split2(value):
    high = value.astype(jnp.bfloat16)
    low = (value - high.astype(jnp.float32)).astype(jnp.bfloat16)
    return high, low


def params(mebibytes, **extra):
    return pltpu.CompilerParams(vmem_limit_bytes=mebibytes * MEBI, **extra)


def cost(flops, moved):
    return pl.CostEstimate(flops=int(flops), bytes_accessed=int(moved), transcendentals=0)


def eliminate(tiles):
    tiles, start = tiles
    rows = tiles[0].shape[0]
    done = []
    for first in range(0, rows, GROUP):
        height = rows - first
        row_ids = lax.broadcasted_iota(jnp.int32, (height, LANES), 0)
        heads = [
            jnp.broadcast_to(tiles[0][:, start + first + j : start + first + j + 1], (height, LANES))
            for j in range(GROUP)
        ]
        scale = jnp.zeros((GROUP, LANES), jnp.float32)
        for j in range(GROUP):
            pivot = heads[j][j : j + 1, :]
            factor = jnp.where(row_ids > j, heads[j] * (1.0 / pivot), 0.0)
            for other in range(j + 1, GROUP):
                heads[other] = heads[other] - factor * heads[other][j : j + 1, :]
            tiles = [tile - factor * tile[j : j + 1, :] for tile in tiles]
            root = lax.rsqrt(pivot)
            root = root * (1.5 - 0.5 * pivot * root * root)
            scale = jnp.where(row_ids[:GROUP] == j, root, scale)
        done.append([tile[:GROUP] * scale for tile in tiles])
        tiles = [tile[GROUP:] for tile in tiles]
    return [jnp.concatenate(parts, axis=0) for parts in zip(*done)]


def inverse_factor(source, work, result):
    order = source.shape[0]
    span = order // LANES
    for base in range(0, order, BLOCK):
        low = base // LANES
        row_ids = lax.broadcasted_iota(jnp.int32, (BLOCK, LANES), 0)
        lane_ids = lax.broadcasted_iota(jnp.int32, (BLOCK, LANES), 1)
        unit = jnp.where(lane_ids - base % LANES == row_ids, 1.0, 0.0)
        zero = jnp.zeros((BLOCK, LANES), jnp.float32)
        tiles = [source[base : base + BLOCK, s * LANES : (s + 1) * LANES] for s in range(low, span)]
        tiles += [zero] * low + [unit]
        if base:
            taken = dot32(
                work[0:base, base : base + BLOCK],
                work[0:base, low * LANES : order + (low + 1) * LANES],
                TN,
            )
            tiles = [tile - taken[:, s * LANES : (s + 1) * LANES] for s, tile in enumerate(tiles)]
        tiles = eliminate((tiles, base % LANES))
        for s, tile in enumerate(tiles):
            work[base : base + BLOCK, (low + s) * LANES : (low + s + 1) * LANES] = tile
        for s in range(low + 1, span):
            work[base : base + BLOCK, order + s * LANES : order + (s + 1) * LANES] = zero
    result[...] = work[:, order:]


def fetch(choice, candidates, target, sem):
    for n, candidate in enumerate(candidates):
        copy = pltpu.make_async_copy(candidate, target, sem)
        pl.when(choice == n)(copy.start)
    return pltpu.make_async_copy(candidates[0], target, sem).wait


def first_kernel(place, own, got, result, tile, work, sem):
    fetch(place[0] % 2, (own, got), tile, sem)()
    inverse_factor(tile, work, result)


def first_inverse(place, own, got):
    order = own.shape[1]
    return pl.pallas_call(
        first_kernel,
        out_shape=jax.ShapeDtypeStruct((order, order), jnp.float32),
        in_specs=[IN_SMEM, ANYWHERE, ANYWHERE],
        out_specs=IN_VMEM,
        scratch_shapes=[
            pltpu.VMEM((order, order), jnp.float32),
            pltpu.VMEM((order, 2 * order), jnp.float32),
            pltpu.SemaphoreType.DMA,
        ],
        compiler_params=params(8),
        cost_estimate=cost(2**10, 2**10),
        name="first_inverse",
    )(place, own, got)


def second_kernel(place, ranks, own, got, inverse, weights, head, work, held, sems):
    order = inverse.shape[0]
    cap = (head.shape[0] - order) // 2
    fetch(1 - place[0] % 2, (own, got), head, sems.at[0])()
    held[:order, :] = inverse[...]
    live = lax.broadcasted_iota(jnp.int32, (cap, order), 0) < ranks[1, 0]
    left = jnp.where(live, head[order : order + cap, :], 0.0)
    right = jnp.where(live, head[order + cap :, :], 0.0)
    solved = dot32(right, inverse[...], NT)
    dense = dot32(left, solved, TN)
    shifted = head.at[pl.ds(0, order)]
    shifted[...] = shifted[...] - dot32(dense, dense, NT)
    inverse_factor(shifted, work, held.at[pl.ds(2 * order, order)])
    held[order : 2 * order, :] = -dot32(dot32(held[2 * order :, :], dense, NN), inverse[...], NN)
    copy = pltpu.make_async_copy(held, weights, sems.at[1])
    copy.start()
    copy.wait()


def second_inverse(place, ranks, own, got, inverse):
    order = inverse.shape[0]
    return pl.pallas_call(
        second_kernel,
        out_shape=pltpu.HBM((3 * order, order), jnp.float32),
        in_specs=[IN_SMEM, IN_SMEM, ANYWHERE, ANYWHERE, IN_VMEM],
        out_specs=IN_HBM,
        scratch_shapes=[
            pltpu.VMEM(own.shape, jnp.float32),
            pltpu.VMEM((order, 2 * order), jnp.float32),
            pltpu.VMEM((3 * order, order), jnp.float32),
            pltpu.SemaphoreType.DMA((2,)),
        ],
        compiler_params=params(8),
        cost_estimate=cost(2**10, 2**10),
        name="second_inverse",
    )(place, ranks, own, got, inverse)


def segment(ranks, panel, group, slot, slots, grid_rows):
    start, count = jnp.int32(0), jnp.int32(0)
    for s in range(slots):
        tile_row = s * grid_rows + group
        rank = jnp.where(tile_row > panel, ranks[tile_row, panel], 0)
        start = start + jnp.where(s < slot, rank, 0)
        count = count + jnp.where(s == slot, rank, 0)
    return start, count


def pack_kernel(capacity, grid_rows, place, ranks, left, right, packed, pivot, held, sem):
    slots, order, cap = held.shape[1:]
    copies = [
        pltpu.make_async_copy(source.at[:, 0], held.at[k], sem.at[k]) for k, source in enumerate((left, right))
    ]
    for copy in copies:
        copy.start()
    panel = jnp.minimum(place[1], 1)
    spot = lax.broadcasted_iota(jnp.int32, (capacity, cap), 0)
    column = lax.broadcasted_iota(jnp.int32, (capacity, cap), 1)
    chosen = []
    for slot in range(slots):
        start, count = segment(ranks, panel, place[0], slot, slots, grid_rows)
        hit = (spot - start == column) & (column < count)
        chosen.append(jnp.where(hit, 1.0, 0.0).astype(jnp.bfloat16))
    for k, copy in enumerate(copies):
        copy.wait()
        total = sum(dot16(chosen[slot], held[k, slot], NT) for slot in range(slots))
        packed[k * capacity : (k + 1) * capacity, :] = total
        pivot[k * cap : (k + 1) * cap, :] = total[:cap]


def pack(place, ranks, left_fac, right_fac, capacity, grid_rows):
    slots, _, order, cap = left_fac.shape
    return pl.pallas_call(
        functools.partial(pack_kernel, capacity, grid_rows),
        out_shape=(
            jax.ShapeDtypeStruct((2 * capacity, order), jnp.float32),
            jax.ShapeDtypeStruct((2 * cap, order), jnp.float32),
        ),
        in_specs=[IN_SMEM, IN_SMEM, IN_HBM, IN_HBM],
        out_specs=(IN_VMEM, IN_VMEM),
        scratch_shapes=[pltpu.VMEM((2, slots, order, cap), jnp.bfloat16), pltpu.SemaphoreType.DMA((2,))],
        compiler_params=params(16),
        cost_estimate=cost(2**10, 2**10),
        name="pack",
    )(place, ranks, left_fac, right_fac)


def pick_kernel(count, index, *refs):
    candidates, target, sem = refs[:count], refs[count], refs[count + 1]
    wait = fetch(index[0], candidates, target, sem)
    pl.when(index[0] >= 0)(wait)


def pick(index, candidates):
    return pl.pallas_call(
        functools.partial(pick_kernel, len(candidates)),
        out_shape=jax.ShapeDtypeStruct(candidates[0].shape, candidates[0].dtype),
        in_specs=[IN_SMEM] + [ANYWHERE] * len(candidates),
        out_specs=ANYWHERE,
        scratch_shapes=[pltpu.SemaphoreType.DMA],
        compiler_params=params(4),
        cost_estimate=cost(0, 2 * candidates[0].size * 4),
        name="pick",
    )(jnp.reshape(index, (1,)).astype(jnp.int32), *candidates)


def rows_kernel(capacity, grid_rows, count, place, ranks, *refs):
    sources, weights, stacked = refs[: 2 * count], refs[2 * count], refs[2 * count + 1]
    landed, inverses, weight_high, weight_low, sems = refs[2 * count + 2 :]
    order = inverses.shape[1]
    inverses_in = pltpu.make_async_copy(weights, inverses, sems.at[4])
    inverses_in.start()
    slots = stacked.shape[0]
    cap = LANES
    waits = []
    for t in range(2):
        for k in range(2):
            part = [source.at[pl.ds(k * capacity, capacity)] for source in sources[t * count : (t + 1) * count]]
            waits.append(fetch(place[1], part, landed.at[2 * t + k, pl.ds(0, capacity)], sems.at[2 * t + k]))
            landed[2 * t + k, capacity:, :] = jnp.zeros((cap, order), jnp.float32)
    inverses_in.wait()
    base_parts, second_parts = split2(inverses[: 2 * order, :]), split2(inverses[2 * order :, :])
    for wait in waits:
        wait()
    solved0 = sum(dot16(landed[1].astype(jnp.bfloat16), part, NT) for part in base_parts)
    solved1 = sum(dot16(landed[3].astype(jnp.bfloat16), part, NT) for part in second_parts)
    for column, value in ((0, solved0), (2 * order, solved1)):
        high, low = split2(value)
        weight_high[:, column : column + value.shape[1]] = high
        weight_low[:, column : column + value.shape[1]] = low
    live = lax.broadcasted_iota(jnp.int32, (cap, order), 0)
    for slot in range(slots):
        pieces = []
        for t in range(2):
            start, rank = segment(ranks, t, place[0], slot, slots, grid_rows)
            spot = pl.ds(pl.multiple_of(start, 16), cap)
            left = jnp.where(live < rank, landed[2 * t, spot, :], 0.0).astype(jnp.bfloat16)
            columns = pl.ds(0, 2 * order) if t == 0 else pl.ds(2 * order, order)
            weights = jnp.concatenate([weight_high[spot, columns], weight_low[spot, columns]], axis=0)
            pieces.append(dot16(jnp.concatenate([left, left], axis=0), weights, TN))
        for column, value in ((0, pieces[0][:, :order]), (order, pieces[0][:, order:] + pieces[1])):
            high, low = split2(value)
            stacked[slot, :, column : column + order] = high
            stacked[slot, :, 2 * order + column : 2 * order + column + order] = low
            stacked[slot, :, 4 * order + column : 4 * order + column + order] = high


def row_panels(place, ranks, firsts, seconds, inverses, capacity, slots, grid_rows):
    order = inverses.shape[1]
    count = len(firsts)
    spaces = [ANYWHERE] * count + [IN_HBM] + [ANYWHERE] * (count - 1)
    return pl.pallas_call(
        functools.partial(rows_kernel, capacity, grid_rows, count),
        out_shape=jax.ShapeDtypeStruct((slots, order, 6 * order), jnp.bfloat16),
        in_specs=[IN_SMEM] * 2 + spaces + [IN_HBM],
        out_specs=IN_VMEM,
        scratch_shapes=[
            pltpu.VMEM((4, capacity + LANES, order), jnp.float32),
            pltpu.VMEM((3 * order, order), jnp.float32),
            pltpu.VMEM((capacity + LANES, 3 * order), jnp.bfloat16),
            pltpu.VMEM((capacity + LANES, 3 * order), jnp.bfloat16),
            pltpu.SemaphoreType.DMA((5,)),
        ],
        compiler_params=params(20),
        cost_estimate=cost(2**32, 2**22),
        name="row_panels",
    )(place, ranks, *firsts, *seconds, inverses)


def schur_kernel(capacity, grid_rows, grid_cols, place, ranks, *refs):
    spread = grid_rows // grid_cols
    sources = refs[: 4 * spread]
    weights, rows, left, right, out = refs[4 * spread : 4 * spread + 5]
    landed, inverses, weight0, weight1, bases, panel, sems = refs[4 * spread + 5 :]
    slots, order, cap = out.shape[0], out.shape[2], left.shape[3]
    padded = landed.shape[1]
    used = padded - LANES
    step = pl.program_id(0)
    row_here, col_here = place[0], place[1]
    mine = row_here // grid_cols

    @pl.when(step == 0)
    def _():
        inverses_in = pltpu.make_async_copy(weights, inverses, sems.at[4 * spread])
        inverses_in.start()
        passed = (row_here ^ col_here) & 1
        waits = []
        for n in range(2 * spread):
            for k in range(2):
                part = [source.at[pl.ds(k * capacity, capacity)] for source in sources[2 * n : 2 * n + 2]]
                waits.append(fetch(passed, part, landed.at[2 * n + k, pl.ds(0, capacity)], sems.at[2 * n + k]))
                if padded > capacity:
                    landed[2 * n + k, capacity:, :] = jnp.zeros((padded - capacity, order), jnp.float32)
        inverses_in.wait()
        base_parts, second_parts = split2(inverses[: 2 * order, :]), split2(inverses[2 * order :, :])
        for wait in waits:
            wait()
        for g in range(spread):
            right0 = landed[4 * g + 1, :used, :].astype(jnp.bfloat16)
            right1 = landed[4 * g + 3, :used, :].astype(jnp.bfloat16)
            solved0 = sum(dot16(part, right0, NT) for part in base_parts)
            solved1 = sum(dot16(part, right1, NT) for part in second_parts)
            for target, at, value in (
                (weight0, 2 * g, solved0[:order]),
                (weight1, 4 * g, solved0[order:]),
                (weight1, 4 * g + 2, solved1),
            ):
                for n, piece in enumerate(split2(value)):
                    target[at + n, :, :used] = piece
                    target[at + n, :, used:] = jnp.zeros((order, padded - used), jnp.bfloat16)

    tile_col = step * grid_cols + col_here
    last_row = (slots - 1) * grid_rows + row_here

    @pl.when((tile_col > 1) & (last_row > tile_col))
    def _():
        part = step % spread
        g = part ^ mine
        group = part * grid_cols + col_here
        span = 2 * LANES
        ids = lax.broadcasted_iota(jnp.int32, (span, order), 0)
        windows = []
        for t in range(2):
            start, count = segment(ranks, t, group, step // spread, slots, grid_rows)
            first_lane = start // LANES * LANES
            window = pl.ds(pl.multiple_of(first_lane, LANES), span)
            value = landed[4 * g + 2 * t, window, :]
            live = (ids >= start - first_lane) & (ids < start - first_lane + count)
            value = jnp.where(live, value, 0.0).astype(jnp.bfloat16)
            bases[t * span : (t + 1) * span, :] = value
            windows.append(window)
        panel0 = sum(dot16(weight0[2 * g + n, :, windows[0]], bases[:span], NN) for n in range(2))
        panel1 = sum(
            dot16(weight1[4 * g + n, :, windows[n // 2]], bases[n // 2 * span : (n // 2 + 1) * span], NN)
            for n in range(4)
        )
        for at, value in ((0, panel0), (order, panel1)):
            high, low = split2(value)
            panel[at : at + order, :] = high
            panel[2 * order + at : 3 * order + at, :] = high
            panel[4 * order + at : 5 * order + at, :] = low

    for slot in range(slots):
        tile_row = slot * grid_rows + row_here
        below = tile_row > tile_col

        @pl.when(jnp.logical_not(below))
        def _():
            out[slot, 0] = jnp.zeros((order, order), jnp.float32)

        for t in range(2):

            @pl.when(below & (tile_col == t))
            def _():
                high = rows[slot, :, t * order : (t + 1) * order].astype(jnp.float32)
                low = rows[slot, :, (t + 2) * order : (t + 3) * order].astype(jnp.float32)
                out[slot, 0] = high + low

        @pl.when(below & (tile_col > 1))
        def _():
            basis = left[slot, 0].astype(jnp.float32)
            live = lax.broadcasted_iota(jnp.int32, basis.shape, 1) < ranks[tile_row, tile_col]
            front = dot16(jnp.where(live, basis, 0.0).astype(jnp.bfloat16), right[slot, 0], NT)
            out[slot, 0] = front - dot16(rows[slot], panel[...], NN)


def schur(place, ranks, col_arrays, inverses, rows, left_fac, right_fac, capacity, grid_rows, grid_cols):
    slots, steps, order, cap = left_fac.shape
    spread = grid_rows // grid_cols
    padded = (-(-capacity // LANES) + 1) * LANES
    flat = [array for pair in col_arrays for array in pair]
    factor = pl.BlockSpec((slots, 1, order, cap), lambda m: (0, m, 0, 0))
    return pl.pallas_call(
        functools.partial(schur_kernel, capacity, grid_rows, grid_cols),
        grid=(steps,),
        out_shape=pltpu.HBM((slots, steps, order, order), jnp.float32),
        in_specs=[IN_SMEM] * 2 + [ANYWHERE] * len(flat) + [IN_HBM, IN_VMEM, factor, factor],
        out_specs=pl.BlockSpec((slots, 1, order, order), lambda m: (0, m, 0, 0)),
        scratch_shapes=[
            pltpu.VMEM((4 * spread, padded, order), jnp.float32),
            pltpu.VMEM((3 * order, order), jnp.float32),
            pltpu.VMEM((2 * spread, order, padded), jnp.bfloat16),
            pltpu.VMEM((4 * spread, order, padded), jnp.bfloat16),
            pltpu.VMEM((4 * LANES, order), jnp.bfloat16),
            pltpu.VMEM((6 * order, order), jnp.bfloat16),
            pltpu.SemaphoreType.DMA((4 * spread + 1,)),
        ],
        compiler_params=params(40, dimension_semantics=("arbitrary",)),
        cost_estimate=cost(2**33, 2**24),
        name="schur",
    )(place, ranks, *flat, inverses, rows, left_fac, right_fac)


def after(array, *others):
    return lax.optimization_barrier((array, *others))[0]


def device_program(capacity, diag_tiles, left_fac, right_fac, ranks):
    grid_rows = lax.axis_size("row")
    grid_cols = lax.axis_size("col")
    row_here = lax.axis_index("row")
    col_here = lax.axis_index("col")
    row_slots, _, order, cap = left_fac.shape
    assert cap == LANES and grid_rows % grid_cols == 0 and grid_cols >= 2
    spread = grid_rows // grid_cols
    row_bits = grid_rows.bit_length() - 1
    low_bits = grid_cols.bit_length() - 1
    assert 1 << row_bits == grid_rows and 1 << low_bits == grid_cols
    every_row = range(grid_rows)
    every_col = range(grid_cols)
    place = jnp.stack([row_here, col_here]).astype(jnp.int32)

    def move(array, pairs):
        flat = [(r * grid_cols + c, s * grid_cols + d) for (r, c), (s, d) in pairs]
        return lax.ppermute(array, AXES, flat)

    def down_column(array, root):
        held = [root]
        stages = []
        for bit in range(1, row_bits):
            step = 1 << bit
            got = move(array, [((r, c), (r ^ step, c)) for r in held for c in every_col])
            array = jnp.where(row_here >> bit == 1, got, array)
            held = held + [r ^ step for r in held]
            stages.append(array)
        return stages

    def to_other_parity(array, root):
        return move(array, [((r, c), (r ^ 1, c)) for r in every_row if r % 2 == root for c in every_col])

    def chain_step(array, s):
        return move(array, [((r, c - 1), (r, c)) for c in (s, s + 1) if c < grid_cols for r in every_row])

    packed, pivot_bases = pack(place, ranks, left_fac, right_fac, capacity, grid_rows)
    chain = [packed, chain_step(packed, 1)]
    back = move(packed, [((r, 1), (r, 0)) for r in every_row])

    hops = down_column(diag_tiles[0], 0)
    tile = [hops[-1], to_other_parity(hops[-1], 0)]

    pivot_bases = after(pivot_bases, hops[0])
    received = [move(pivot_bases, [((1, 0), (1, c))]) for c in every_col if c]
    pivot_bases = jnp.where(col_here == 0, pivot_bases, sum(received))
    chain[1] = after(chain[1], pivot_bases, *tile)
    hops = down_column(jnp.concatenate([diag_tiles[0], pivot_bases], axis=0), 1)
    head = hops[-1]

    inverse0 = first_inverse(place, *[after(array, hops[0], chain[1]) for array in tile])
    for s in range(2, grid_cols):
        chain.append(chain_step(after(chain[s - 1], inverse0) if s == 3 else chain[s - 1], s))
    head = [head, to_other_parity(after(head, chain[min(2, grid_cols - 1)]), 1)]

    firsts = chain
    seconds = [back] + chain[:-1]
    offset = (row_here ^ col_here) & (grid_cols - 1)
    held = {c: [c] for c in every_col}

    def hop(array, bit, held):
        step = 1 << bit
        return move(
            array,
            [
                ((r + h * grid_cols, c), ((r + h * grid_cols) ^ step, c))
                for c in every_col
                for r in held[c]
                for h in range(spread)
            ],
        )

    def along_column(candidates, fence):
        have = pick(jnp.where(offset == 0, col_here, -1), candidates)
        held = {c: [c] for c in every_col}
        for bit in range(1, low_bits):
            got = hop(have, bit, held)
            arrived = (offset >> bit == 1) & (offset & 1 == 0)
            stays = (offset >> bit == 0) & (offset & 1 == 0)
            have = pick(jnp.where(arrived, 1, jnp.where(stays, 0, -1)), [have, got])
            held = {c: held[c] + [r ^ (1 << bit) for r in held[c]] for c in every_col}
        have = after(have, fence)
        sets = [have]
        for bit in range(low_bits, row_bits):
            sets = sets + [hop(array, bit, held) for array in sets]
        return [[array, hop(array, 0, held)] for array in sets]

    inverses = second_inverse(place, ranks, *head, inverse0)
    rows = row_panels(place, ranks, firsts, seconds, inverses, capacity, row_slots, grid_rows)
    second_sets = along_column(seconds, inverses)
    first_sets = along_column([firsts[0], *[after(array, inverses) for array in firsts[1:]]], rows)
    col_arrays = [sets[g] for g in range(spread) for sets in (first_sets, second_sets)]
    return schur(place, ranks, col_arrays, inverses, rows, left_fac, right_fac, capacity, grid_rows, grid_cols)


def shards(diag_tiles, left_fac, right_fac, ranks):
    row_slots, cap = left_fac.shape[0], left_fac.shape[3]
    grid_rows = lax.axis_size("row")
    full = row_slots * cap
    packed = max(cap, full * 5 // 8)
    args = (diag_tiles, left_fac, right_fac, ranks)
    if packed == full:
        return device_program(full, *args)
    tile_ids = jnp.arange(ranks.shape[0], dtype=jnp.int32)[:, None]
    live = jnp.where(tile_ids > jnp.arange(2, dtype=jnp.int32)[None, :], ranks[:, :2], 0)
    widest = jnp.max(sum(live[s * grid_rows : (s + 1) * grid_rows] for s in range(row_slots)))
    return lax.cond(
        widest <= packed,
        functools.partial(device_program, packed),
        functools.partial(device_program, full),
        *args,
    )


def solution(mesh):
    in_specs = (P("row", None, None), P("row", "col", None, None), P("row", "col", None, None), P())
    out_specs = P("row", "col", None, None)
    return jax.shard_map(shards, mesh=mesh, in_specs=in_specs, out_specs=out_specs, check_vma=False)
```

```python
import functools

import jax
import jax.numpy as jnp
from jax import lax
from jax.experimental import pallas as pl
from jax.experimental.pallas import tpu as pltpu
from jax.sharding import PartitionSpec as P

PRECISE = lax.Precision.HIGHEST
AXES = ("row", "col")
BLOCK = 32
GROUP = 8
LANES = 128
NT = (((1,), (1,)), ((), ()))
TN = (((0,), (0,)), ((), ()))
NN = (((1,), (0,)), ((), ()))
ANYWHERE = pl.BlockSpec(memory_space=pl.ANY)
IN_VMEM = pl.BlockSpec(memory_space=pltpu.VMEM)
IN_SMEM = pl.BlockSpec(memory_space=pltpu.SMEM)
IN_HBM = pl.BlockSpec(memory_space=pltpu.HBM)
MEBI = 1024 * 1024


def dot32(lhs, rhs, dims):
    return lax.dot_general(lhs, rhs, dims, precision=PRECISE, preferred_element_type=jnp.float32)


def dot16(lhs, rhs, dims):
    return lax.dot_general(lhs, rhs, dims, preferred_element_type=jnp.float32)


def split2(value):
    high = value.astype(jnp.bfloat16)
    low = (value - high.astype(jnp.float32)).astype(jnp.bfloat16)
    return high, low


def params(mebibytes, **extra):
    return pltpu.CompilerParams(vmem_limit_bytes=mebibytes * MEBI, **extra)


def cost(flops, moved):
    return pl.CostEstimate(flops=int(flops), bytes_accessed=int(moved), transcendentals=0)


def eliminate(tiles):
    tiles, start = tiles
    rows = tiles[0].shape[0]
    done = []
    for first in range(0, rows, GROUP):
        height = rows - first
        row_ids = lax.broadcasted_iota(jnp.int32, (height, LANES), 0)
        heads = [
            jnp.broadcast_to(tiles[0][:, start + first + j : start + first + j + 1], (height, LANES))
            for j in range(GROUP)
        ]
        scale = jnp.zeros((GROUP, LANES), jnp.float32)
        for j in range(GROUP):
            pivot = heads[j][j : j + 1, :]
            factor = jnp.where(row_ids > j, heads[j] * (1.0 / pivot), 0.0)
            for other in range(j + 1, GROUP):
                heads[other] = heads[other] - factor * heads[other][j : j + 1, :]
            tiles = [tile - factor * tile[j : j + 1, :] for tile in tiles]
            root = lax.rsqrt(pivot)
            root = root * (1.5 - 0.5 * pivot * root * root)
            scale = jnp.where(row_ids[:GROUP] == j, root, scale)
        done.append([tile[:GROUP] * scale for tile in tiles])
        tiles = [tile[GROUP:] for tile in tiles]
    return [jnp.concatenate(parts, axis=0) for parts in zip(*done)]


def inverse_factor(source, work, result):
    order = source.shape[0]
    span = order // LANES
    for base in range(0, order, BLOCK):
        low = base // LANES
        row_ids = lax.broadcasted_iota(jnp.int32, (BLOCK, LANES), 0)
        lane_ids = lax.broadcasted_iota(jnp.int32, (BLOCK, LANES), 1)
        unit = jnp.where(lane_ids - base % LANES == row_ids, 1.0, 0.0)
        zero = jnp.zeros((BLOCK, LANES), jnp.float32)
        tiles = [source[base : base + BLOCK, s * LANES : (s + 1) * LANES] for s in range(low, span)]
        tiles += [zero] * low + [unit]
        if base:
            taken = dot32(
                work[0:base, base : base + BLOCK],
                work[0:base, low * LANES : order + (low + 1) * LANES],
                TN,
            )
            tiles = [tile - taken[:, s * LANES : (s + 1) * LANES] for s, tile in enumerate(tiles)]
        tiles = eliminate((tiles, base % LANES))
        for s, tile in enumerate(tiles):
            work[base : base + BLOCK, (low + s) * LANES : (low + s + 1) * LANES] = tile
        for s in range(low + 1, span):
            work[base : base + BLOCK, order + s * LANES : order + (s + 1) * LANES] = zero
    result[...] = work[:, order:]


def fetch(choice, candidates, target, sem):
    for n, candidate in enumerate(candidates):
        copy = pltpu.make_async_copy(candidate, target, sem)
        pl.when(choice == n)(copy.start)
    return pltpu.make_async_copy(candidates[0], target, sem).wait


def first_kernel(place, tile, result, work):
    pl.when(place[0] == 0)(lambda: inverse_factor(tile, work, result))


def first_inverse(place, tile):
    order = tile.shape[1]
    return pl.pallas_call(
        first_kernel,
        out_shape=jax.ShapeDtypeStruct((order, order), jnp.float32),
        in_specs=[IN_SMEM, IN_VMEM],
        out_specs=IN_VMEM,
        scratch_shapes=[pltpu.VMEM((order, 2 * order), jnp.float32)],
        compiler_params=params(8),
        cost_estimate=cost(2**33, 2**20),
        name="first_inverse",
    )(place, tile)


def second_kernel(place, ranks, tile, bases, inverse, weights, shifted, work):
    order = inverse.shape[0]
    cap = bases.shape[0] // 2

    @pl.when(place[0] == 1)
    def _():
        weights[:order, :] = inverse[...]
        live = lax.broadcasted_iota(jnp.int32, (cap, order), 0) < ranks[1, 0]
        left = jnp.where(live, bases[:cap, :], 0.0)
        right = jnp.where(live, bases[cap:, :], 0.0)
        solved = dot32(right, inverse[...], NT)
        dense = dot32(left, solved, TN)
        shifted[...] = tile[...] - dot32(dense, dense, NT)
        inverse_factor(shifted, work, weights.at[pl.ds(2 * order, order)])
        weights[order : 2 * order, :] = -dot32(dot32(weights[2 * order :, :], dense, NN), inverse[...], NN)


def second_inverse(place, ranks, tile, bases, inverse):
    order = inverse.shape[0]
    return pl.pallas_call(
        second_kernel,
        out_shape=jax.ShapeDtypeStruct((3 * order, order), jnp.float32),
        in_specs=[IN_SMEM, IN_SMEM, IN_VMEM, IN_VMEM, IN_VMEM],
        out_specs=IN_VMEM,
        scratch_shapes=[
            pltpu.VMEM((order, order), jnp.float32),
            pltpu.VMEM((order, 2 * order), jnp.float32),
        ],
        compiler_params=params(8),
        cost_estimate=cost(2**10, 2**10),
        name="second_inverse",
    )(place, ranks, tile, bases, inverse)


def segment(ranks, panel, group, slot, slots, grid_rows):
    start, count = jnp.int32(0), jnp.int32(0)
    for s in range(slots):
        tile_row = s * grid_rows + group
        rank = jnp.where(tile_row > panel, ranks[tile_row, panel], 0)
        start = start + jnp.where(s < slot, rank, 0)
        count = count + jnp.where(s == slot, rank, 0)
    return start, count


def pack_kernel(capacity, grid_rows, place, ranks, left, right, packed, pivot, held, sem):
    slots, order, cap = held.shape[1:]
    copies = [
        pltpu.make_async_copy(source.at[:, 0], held.at[k], sem.at[k]) for k, source in enumerate((left, right))
    ]
    for copy in copies:
        copy.start()
    panel = jnp.minimum(place[1], 1)
    spot = lax.broadcasted_iota(jnp.int32, (capacity, cap), 0)
    column = lax.broadcasted_iota(jnp.int32, (capacity, cap), 1)
    chosen = []
    for slot in range(slots):
        start, count = segment(ranks, panel, place[0], slot, slots, grid_rows)
        hit = (spot - start == column) & (column < count)
        chosen.append(jnp.where(hit, 1.0, 0.0).astype(jnp.bfloat16))
    for k, copy in enumerate(copies):
        copy.wait()
        total = sum(dot16(chosen[slot], held[k, slot], NT) for slot in range(slots))
        packed[k * capacity : (k + 1) * capacity, :] = total
        pivot[k * cap : (k + 1) * cap, :] = total[:cap]


def pack(place, ranks, left_fac, right_fac, capacity, grid_rows):
    slots, _, order, cap = left_fac.shape
    return pl.pallas_call(
        functools.partial(pack_kernel, capacity, grid_rows),
        out_shape=(
            jax.ShapeDtypeStruct((2 * capacity, order), jnp.float32),
            jax.ShapeDtypeStruct((2 * cap, order), jnp.float32),
        ),
        in_specs=[IN_SMEM, IN_SMEM, IN_HBM, IN_HBM],
        out_specs=(IN_VMEM, IN_VMEM),
        scratch_shapes=[pltpu.VMEM((2, slots, order, cap), jnp.bfloat16), pltpu.SemaphoreType.DMA((2,))],
        compiler_params=params(16),
        cost_estimate=cost(2**10, 2**10),
        name="pack",
    )(place, ranks, left_fac, right_fac)


def pick_kernel(count, index, *refs):
    candidates, target, sem = refs[:count], refs[count], refs[count + 1]
    wait = fetch(index[0], candidates, target, sem)
    pl.when(index[0] >= 0)(wait)


def pick(index, candidates):
    return pl.pallas_call(
        functools.partial(pick_kernel, len(candidates)),
        out_shape=jax.ShapeDtypeStruct(candidates[0].shape, candidates[0].dtype),
        in_specs=[IN_SMEM] + [ANYWHERE] * len(candidates),
        out_specs=ANYWHERE,
        scratch_shapes=[pltpu.SemaphoreType.DMA],
        compiler_params=params(4),
        cost_estimate=cost(0, 2 * candidates[0].size * 4),
        name="pick",
    )(jnp.reshape(index, (1,)).astype(jnp.int32), *candidates)


def rows_kernel(capacity, grid_rows, count, place, ranks, *refs):
    sources, weights, stacked = refs[: 2 * count], refs[2 * count : 2 * count + 2], refs[2 * count + 2]
    landed, inverses, weight_high, weight_low, sems = refs[2 * count + 3 :]
    order = inverses.shape[1]
    inverses_in = fetch(1 - place[0] % 2, weights, inverses, sems.at[4])
    slots = stacked.shape[0]
    cap = LANES
    waits = []
    for t in range(2):
        for k in range(2):
            part = [source.at[pl.ds(k * capacity, capacity)] for source in sources[t * count : (t + 1) * count]]
            waits.append(fetch(place[1], part, landed.at[2 * t + k, pl.ds(0, capacity)], sems.at[2 * t + k]))
            landed[2 * t + k, capacity:, :] = jnp.zeros((cap, order), jnp.float32)
    inverses_in()
    base_parts, second_parts = split2(inverses[: 2 * order, :]), split2(inverses[2 * order :, :])
    for wait in waits:
        wait()
    solved0 = sum(dot16(landed[1].astype(jnp.bfloat16), part, NT) for part in base_parts)
    solved1 = sum(dot16(landed[3].astype(jnp.bfloat16), part, NT) for part in second_parts)
    for column, value in ((0, solved0), (2 * order, solved1)):
        high, low = split2(value)
        weight_high[:, column : column + value.shape[1]] = high
        weight_low[:, column : column + value.shape[1]] = low
    live = lax.broadcasted_iota(jnp.int32, (cap, order), 0)
    for slot in range(slots):
        pieces = []
        for t in range(2):
            start, rank = segment(ranks, t, place[0], slot, slots, grid_rows)
            spot = pl.ds(pl.multiple_of(start, 16), cap)
            left = jnp.where(live < rank, landed[2 * t, spot, :], 0.0).astype(jnp.bfloat16)
            columns = pl.ds(0, 2 * order) if t == 0 else pl.ds(2 * order, order)
            weights = jnp.concatenate([weight_high[spot, columns], weight_low[spot, columns]], axis=0)
            pieces.append(dot16(jnp.concatenate([left, left], axis=0), weights, TN))
        for column, value in ((0, pieces[0][:, :order]), (order, pieces[0][:, order:] + pieces[1])):
            high, low = split2(value)
            stacked[slot, :, column : column + order] = high
            stacked[slot, :, 2 * order + column : 2 * order + column + order] = low
            stacked[slot, :, 4 * order + column : 4 * order + column + order] = high


def row_panels(place, ranks, firsts, seconds, inverses, capacity, slots, grid_rows):
    order = inverses[0].shape[1]
    count = len(firsts)
    return pl.pallas_call(
        functools.partial(rows_kernel, capacity, grid_rows, count),
        out_shape=jax.ShapeDtypeStruct((slots, order, 6 * order), jnp.bfloat16),
        in_specs=[IN_SMEM] * 2 + [ANYWHERE] * (2 * count + 2),
        out_specs=IN_VMEM,
        scratch_shapes=[
            pltpu.VMEM((4, capacity + LANES, order), jnp.float32),
            pltpu.VMEM((3 * order, order), jnp.float32),
            pltpu.VMEM((capacity + LANES, 3 * order), jnp.bfloat16),
            pltpu.VMEM((capacity + LANES, 3 * order), jnp.bfloat16),
            pltpu.SemaphoreType.DMA((5,)),
        ],
        compiler_params=params(20),
        cost_estimate=cost(2**32, 2**22),
        name="row_panels",
    )(place, ranks, *firsts, *seconds, *inverses)


def schur_kernel(capacity, grid_rows, grid_cols, place, ranks, *refs):
    spread = grid_rows // grid_cols
    sources = refs[: 4 * spread]
    weights, (rows, left, right, out) = refs[4 * spread : 4 * spread + 2], refs[4 * spread + 2 : 4 * spread + 6]
    landed, inverses, weight0, weight1, bases, panel, sems = refs[4 * spread + 6 :]
    slots, order, cap = out.shape[0], out.shape[2], left.shape[3]
    padded = landed.shape[1]
    used = padded - LANES
    step = pl.program_id(0)
    row_here, col_here = place[0], place[1]
    mine = row_here // grid_cols

    @pl.when(step == 0)
    def _():
        inverses_in = fetch(1 - row_here % 2, weights, inverses, sems.at[4 * spread])
        passed = (row_here ^ col_here) & 1
        waits = []
        for n in range(2 * spread):
            for k in range(2):
                part = [source.at[pl.ds(k * capacity, capacity)] for source in sources[2 * n : 2 * n + 2]]
                waits.append(fetch(passed, part, landed.at[2 * n + k, pl.ds(0, capacity)], sems.at[2 * n + k]))
                if padded > capacity:
                    landed[2 * n + k, capacity:, :] = jnp.zeros((padded - capacity, order), jnp.float32)
        inverses_in()
        base_parts, second_parts = split2(inverses[: 2 * order, :]), split2(inverses[2 * order :, :])
        for wait in waits:
            wait()
        for g in range(spread):
            right0 = landed[4 * g + 1, :used, :].astype(jnp.bfloat16)
            right1 = landed[4 * g + 3, :used, :].astype(jnp.bfloat16)
            solved0 = sum(dot16(part, right0, NT) for part in base_parts)
            solved1 = sum(dot16(part, right1, NT) for part in second_parts)
            for target, at, value in (
                (weight0, 2 * g, solved0[:order]),
                (weight1, 4 * g, solved0[order:]),
                (weight1, 4 * g + 2, solved1),
            ):
                for n, piece in enumerate(split2(value)):
                    target[at + n, :, :used] = piece
                    target[at + n, :, used:] = jnp.zeros((order, padded - used), jnp.bfloat16)

    tile_col = step * grid_cols + col_here
    last_row = (slots - 1) * grid_rows + row_here

    @pl.when((tile_col > 1) & (last_row > tile_col))
    def _():
        part = step % spread
        g = part ^ mine
        group = part * grid_cols + col_here
        span = 2 * LANES
        ids = lax.broadcasted_iota(jnp.int32, (span, order), 0)
        windows = []
        for t in range(2):
            start, count = segment(ranks, t, group, step // spread, slots, grid_rows)
            first_lane = start // LANES * LANES
            window = pl.ds(pl.multiple_of(first_lane, LANES), span)
            value = landed[4 * g + 2 * t, window, :]
            live = (ids >= start - first_lane) & (ids < start - first_lane + count)
            value = jnp.where(live, value, 0.0).astype(jnp.bfloat16)
            bases[t * span : (t + 1) * span, :] = value
            windows.append(window)
        panel0 = sum(dot16(weight0[2 * g + n, :, windows[0]], bases[:span], NN) for n in range(2))
        panel1 = sum(
            dot16(weight1[4 * g + n, :, windows[n // 2]], bases[n // 2 * span : (n // 2 + 1) * span], NN)
            for n in range(4)
        )
        for at, value in ((0, panel0), (order, panel1)):
            high, low = split2(value)
            panel[at : at + order, :] = high
            panel[2 * order + at : 3 * order + at, :] = high
            panel[4 * order + at : 5 * order + at, :] = low

    for slot in range(slots):
        tile_row = slot * grid_rows + row_here
        below = tile_row > tile_col

        @pl.when(jnp.logical_not(below))
        def _():
            out[slot, 0] = jnp.zeros((order, order), jnp.float32)

        for t in range(2):

            @pl.when(below & (tile_col == t))
            def _():
                high = rows[slot, :, t * order : (t + 1) * order].astype(jnp.float32)
                low = rows[slot, :, (t + 2) * order : (t + 3) * order].astype(jnp.float32)
                out[slot, 0] = high + low

        @pl.when(below & (tile_col > 1))
        def _():
            basis = left[slot, 0].astype(jnp.float32)
            live = lax.broadcasted_iota(jnp.int32, basis.shape, 1) < ranks[tile_row, tile_col]
            front = dot16(jnp.where(live, basis, 0.0).astype(jnp.bfloat16), right[slot, 0], NT)
            out[slot, 0] = front - dot16(rows[slot], panel[...], NN)


def schur(place, ranks, col_arrays, inverses, rows, left_fac, right_fac, capacity, grid_rows, grid_cols):
    slots, steps, order, cap = left_fac.shape
    spread = grid_rows // grid_cols
    padded = (-(-capacity // LANES) + 1) * LANES
    flat = [array for pair in col_arrays for array in pair]
    factor = pl.BlockSpec((slots, 1, order, cap), lambda m: (0, m, 0, 0))
    return pl.pallas_call(
        functools.partial(schur_kernel, capacity, grid_rows, grid_cols),
        grid=(steps,),
        out_shape=pltpu.HBM((slots, steps, order, order), jnp.float32),
        in_specs=[IN_SMEM] * 2 + [ANYWHERE] * (len(flat) + 2) + [IN_VMEM, factor, factor],
        out_specs=pl.BlockSpec((slots, 1, order, order), lambda m: (0, m, 0, 0)),
        scratch_shapes=[
            pltpu.VMEM((4 * spread, padded, order), jnp.float32),
            pltpu.VMEM((3 * order, order), jnp.float32),
            pltpu.VMEM((2 * spread, order, padded), jnp.bfloat16),
            pltpu.VMEM((4 * spread, order, padded), jnp.bfloat16),
            pltpu.VMEM((4 * LANES, order), jnp.bfloat16),
            pltpu.VMEM((6 * order, order), jnp.bfloat16),
            pltpu.SemaphoreType.DMA((4 * spread + 1,)),
        ],
        compiler_params=params(40, dimension_semantics=("arbitrary",)),
        cost_estimate=cost(2**33, 2**24),
        name="schur",
    )(place, ranks, *flat, *inverses, rows, left_fac, right_fac)


def after(array, *others):
    return lax.optimization_barrier((array, *others))[0]


def device_program(capacity, diag_tiles, left_fac, right_fac, ranks):
    grid_rows = lax.axis_size("row")
    grid_cols = lax.axis_size("col")
    row_here = lax.axis_index("row")
    col_here = lax.axis_index("col")
    row_slots, _, order, cap = left_fac.shape
    assert cap == LANES and grid_rows % grid_cols == 0 and grid_cols >= 2
    spread = grid_rows // grid_cols
    row_bits = grid_rows.bit_length() - 1
    low_bits = grid_cols.bit_length() - 1
    assert 1 << row_bits == grid_rows and 1 << low_bits == grid_cols
    every_row = range(grid_rows)
    every_col = range(grid_cols)
    place = jnp.stack([row_here, col_here]).astype(jnp.int32)

    def move(array, pairs):
        flat = [(r * grid_cols + c, s * grid_cols + d) for (r, c), (s, d) in pairs]
        return lax.ppermute(array, AXES, flat)

    def down_column(array, root, fences):
        held = [root]
        stages = []
        for bit in range(1, row_bits):
            step = 1 << bit
            got = move(array, [((r, c), (r ^ step, c)) for r in held for c in every_col])
            got = after(got, back, fences[min(bit, len(fences)) - 1])
            array = jnp.where(row_here >> bit == 1, got, array)
            held = held + [r ^ step for r in held]
            stages.append(array)
        return stages

    def to_other_parity(array, root):
        return move(array, [((r, c), (r ^ 1, c)) for r in every_row if r % 2 == root for c in every_col])

    def chain_step(array, s):
        return move(array, [((r, c - 1), (r, c)) for c in (s, s + 1) if c < grid_cols for r in every_row])

    packed, pivot_bases = pack(place, ranks, left_fac, right_fac, capacity, grid_rows)
    chain = [packed, chain_step(packed, 1)]
    back = move(packed, [((r, 1), (r, 0)) for r in every_row])

    received = [move(pivot_bases, [((1, 0), (1, c))]) for c in every_col if c]
    pivot_bases = jnp.where(col_here == 0, pivot_bases, sum(received))
    inverse0 = first_inverse(place, diag_tiles[0])
    inverse0 = move(inverse0, [((0, c), (1, c)) for c in every_col])
    weights = second_inverse(place, ranks, diag_tiles[0], pivot_bases, inverse0)
    chain[1], weights = lax.optimization_barrier((chain[1], weights))

    for s in range(2, grid_cols):
        chain.append(chain_step(chain[s - 1], s))
    hops = down_column(weights, 1, chain[2:] or chain[1:])
    inverses = [hops[-1], to_other_parity(hops[-1], 1)]

    firsts = list(chain)
    seconds = [back] + chain[:-1]
    offset = (row_here ^ col_here) & (grid_cols - 1)
    held = {c: [c] for c in every_col}

    def hop(array, bit, held):
        step = 1 << bit
        return move(
            array,
            [
                ((r + h * grid_cols, c), ((r + h * grid_cols) ^ step, c))
                for c in every_col
                for r in held[c]
                for h in range(spread)
            ],
        )

    def low_hops(candidates, *fence):
        have = pick(jnp.where(offset == 0, col_here, -1), candidates)
        held = {c: [c] for c in every_col}
        for bit in range(1, low_bits):
            got = hop(have, bit, held)
            got = after(got, *fence) if fence else got
            arrived = (offset >> bit == 1) & (offset & 1 == 0)
            stays = (offset >> bit == 0) & (offset & 1 == 0)
            have = pick(jnp.where(arrived, 1, jnp.where(stays, 0, -1)), [have, got])
            held = {c: held[c] + [r ^ (1 << bit) for r in held[c]] for c in every_col}
        return have

    def high_hops(have):
        held = {c: [r for r in range(grid_cols) if (r ^ c) % 2 == 0] for c in every_col}
        sets = [have]
        for bit in range(low_bits, row_bits):
            sets = sets + [hop(array, bit, held) for array in sets]
        return [[array, hop(array, 0, held)] for array in sets]

    second_have = low_hops(seconds)
    rows = row_panels(place, ranks, firsts, seconds, inverses, capacity, row_slots, grid_rows)
    first_have = low_hops([after(array, second_have) for array in firsts], rows)
    second_sets, first_sets = high_hops(second_have), high_hops(first_have)
    col_arrays = [sets[g] for g in range(spread) for sets in (first_sets, second_sets)]
    return schur(place, ranks, col_arrays, inverses, rows, left_fac, right_fac, capacity, grid_rows, grid_cols)


def shards(diag_tiles, left_fac, right_fac, ranks):
    row_slots, cap = left_fac.shape[0], left_fac.shape[3]
    grid_rows = lax.axis_size("row")
    full = row_slots * cap
    packed = max(cap, full * 5 // 8)
    args = (diag_tiles, left_fac, right_fac, ranks)
    if packed == full:
        return device_program(full, *args)
    tile_ids = jnp.arange(ranks.shape[0], dtype=jnp.int32)[:, None]
    live = jnp.where(tile_ids > jnp.arange(2, dtype=jnp.int32)[None, :], ranks[:, :2], 0)
    widest = jnp.max(sum(live[s * grid_rows : (s + 1) * grid_rows] for s in range(row_slots)))
    return lax.cond(
        widest <= packed,
        functools.partial(device_program, packed),
        functools.partial(device_program, full),
        *args,
    )


def solution(mesh):
    in_specs = (P("row", None, None), P("row", "col", None, None), P("row", "col", None, None), P())
    out_specs = P("row", "col", None, None)
    return jax.shard_map(shards, mesh=mesh, in_specs=in_specs, out_specs=out_specs, check_vma=False)
```

```python
import functools

import jax
import jax.numpy as jnp
from jax import lax
from jax.experimental import pallas as pl
from jax.experimental.pallas import tpu as pltpu
from jax.sharding import PartitionSpec as P

PRECISE = lax.Precision.HIGHEST
AXES = ("row", "col")
BLOCK = 32
GROUP = 8
LANES = 128
NT = (((1,), (1,)), ((), ()))
TN = (((0,), (0,)), ((), ()))
NN = (((1,), (0,)), ((), ()))
ANYWHERE = pl.BlockSpec(memory_space=pl.ANY)
IN_VMEM = pl.BlockSpec(memory_space=pltpu.VMEM)
IN_SMEM = pl.BlockSpec(memory_space=pltpu.SMEM)
IN_HBM = pl.BlockSpec(memory_space=pltpu.HBM)
MEBI = 1024 * 1024


def dot32(lhs, rhs, dims):
    return lax.dot_general(lhs, rhs, dims, precision=PRECISE, preferred_element_type=jnp.float32)


def dot16(lhs, rhs, dims):
    return lax.dot_general(lhs, rhs, dims, preferred_element_type=jnp.float32)


def split2(value):
    high = value.astype(jnp.bfloat16)
    low = (value - high.astype(jnp.float32)).astype(jnp.bfloat16)
    return high, low


def params(mebibytes, **extra):
    return pltpu.CompilerParams(vmem_limit_bytes=mebibytes * MEBI, **extra)


def cost(flops, moved):
    return pl.CostEstimate(flops=int(flops), bytes_accessed=int(moved), transcendentals=0)


def eliminate(tiles):
    tiles, start = tiles
    rows = tiles[0].shape[0]
    done = []
    for first in range(0, rows, GROUP):
        height = rows - first
        row_ids = lax.broadcasted_iota(jnp.int32, (height, LANES), 0)
        heads = [
            jnp.broadcast_to(tiles[0][:, start + first + j : start + first + j + 1], (height, LANES))
            for j in range(GROUP)
        ]
        scale = jnp.zeros((GROUP, LANES), jnp.float32)
        for j in range(GROUP):
            pivot = heads[j][j : j + 1, :]
            factor = jnp.where(row_ids > j, heads[j] * (1.0 / pivot), 0.0)
            for other in range(j + 1, GROUP):
                heads[other] = heads[other] - factor * heads[other][j : j + 1, :]
            tiles = [tile - factor * tile[j : j + 1, :] for tile in tiles]
            root = lax.rsqrt(pivot)
            root = root * (1.5 - 0.5 * pivot * root * root)
            scale = jnp.where(row_ids[:GROUP] == j, root, scale)
        done.append([tile[:GROUP] * scale for tile in tiles])
        tiles = [tile[GROUP:] for tile in tiles]
    return [jnp.concatenate(parts, axis=0) for parts in zip(*done)]


def inverse_factor(source, work, result):
    order = source.shape[0]
    span = order // LANES
    for base in range(0, order, BLOCK):
        low = base // LANES
        row_ids = lax.broadcasted_iota(jnp.int32, (BLOCK, LANES), 0)
        lane_ids = lax.broadcasted_iota(jnp.int32, (BLOCK, LANES), 1)
        unit = jnp.where(lane_ids - base % LANES == row_ids, 1.0, 0.0)
        zero = jnp.zeros((BLOCK, LANES), jnp.float32)
        tiles = [source[base : base + BLOCK, s * LANES : (s + 1) * LANES] for s in range(low, span)]
        tiles += [zero] * low + [unit]
        if base:
            taken = dot32(
                work[0:base, base : base + BLOCK],
                work[0:base, low * LANES : order + (low + 1) * LANES],
                TN,
            )
            tiles = [tile - taken[:, s * LANES : (s + 1) * LANES] for s, tile in enumerate(tiles)]
        tiles = eliminate((tiles, base % LANES))
        for s, tile in enumerate(tiles):
            work[base : base + BLOCK, (low + s) * LANES : (low + s + 1) * LANES] = tile
        for s in range(low + 1, span):
            work[base : base + BLOCK, order + s * LANES : order + (s + 1) * LANES] = zero
    result[...] = work[:, order:]


def fetch(choice, candidates, target, sem):
    for n, candidate in enumerate(candidates):
        copy = pltpu.make_async_copy(candidate, target, sem)
        pl.when(choice == n)(copy.start)
    return pltpu.make_async_copy(candidates[0], target, sem).wait


def first_kernel(place, tiles, result, tile, work, sem):
    @pl.when(place[0] == 0)
    def _():
        copy = pltpu.make_async_copy(tiles.at[0], tile, sem)
        copy.start()
        copy.wait()
        inverse_factor(tile, work, result)


def first_inverse(place, tiles):
    order = tiles.shape[2]
    return pl.pallas_call(
        first_kernel,
        out_shape=jax.ShapeDtypeStruct((order, order), jnp.float32),
        in_specs=[IN_SMEM, ANYWHERE],
        out_specs=IN_VMEM,
        scratch_shapes=[
            pltpu.VMEM((order, order), jnp.float32),
            pltpu.VMEM((order, 2 * order), jnp.float32),
            pltpu.SemaphoreType.DMA,
        ],
        compiler_params=params(8),
        cost_estimate=cost(2**10, 2**10),
        name="first_inverse",
    )(place, tiles)


def second_kernel(place, ranks, tiles, bases, inverse, weights, shifted, work, sem):
    order = inverse.shape[0]
    cap = bases.shape[0] // 2

    @pl.when(place[0] == 1)
    def _():
        copy = pltpu.make_async_copy(tiles.at[0], shifted, sem)
        copy.start()
        weights[:order, :] = inverse[...]
        live = lax.broadcasted_iota(jnp.int32, (cap, order), 0) < ranks[1, 0]
        left = jnp.where(live, bases[:cap, :], 0.0)
        right = jnp.where(live, bases[cap:, :], 0.0)
        solved = dot32(right, inverse[...], NT)
        dense = dot32(left, solved, TN)
        copy.wait()
        shifted[...] = shifted[...] - dot32(dense, dense, NT)
        inverse_factor(shifted, work, weights.at[pl.ds(2 * order, order)])
        weights[order : 2 * order, :] = -dot32(dot32(weights[2 * order :, :], dense, NN), inverse[...], NN)


def second_inverse(place, ranks, tiles, bases, inverse):
    order = inverse.shape[0]
    return pl.pallas_call(
        second_kernel,
        out_shape=jax.ShapeDtypeStruct((3 * order, order), jnp.float32),
        in_specs=[IN_SMEM, IN_SMEM, ANYWHERE, IN_VMEM, IN_VMEM],
        out_specs=IN_VMEM,
        scratch_shapes=[
            pltpu.VMEM((order, order), jnp.float32),
            pltpu.VMEM((order, 2 * order), jnp.float32),
            pltpu.SemaphoreType.DMA,
        ],
        compiler_params=params(8),
        cost_estimate=cost(2**10, 2**10),
        name="second_inverse",
    )(place, ranks, tiles, bases, inverse)


def segment(ranks, panel, group, slot, slots, grid_rows):
    start, count = jnp.int32(0), jnp.int32(0)
    for s in range(slots):
        tile_row = s * grid_rows + group
        rank = jnp.where(tile_row > panel, ranks[tile_row, panel], 0)
        start = start + jnp.where(s < slot, rank, 0)
        count = count + jnp.where(s == slot, rank, 0)
    return start, count


def pack_kernel(capacity, grid_rows, place, ranks, left, right, packed, pivot, held, sem):
    slots, order, cap = held.shape[1:]
    copies = [
        pltpu.make_async_copy(source.at[:, 0], held.at[k], sem.at[k]) for k, source in enumerate((left, right))
    ]
    for copy in copies:
        copy.start()
    panel = jnp.minimum(place[1], 1)
    spot = lax.broadcasted_iota(jnp.int32, (capacity, cap), 0)
    column = lax.broadcasted_iota(jnp.int32, (capacity, cap), 1)
    chosen = []
    for slot in range(slots):
        start, count = segment(ranks, panel, place[0], slot, slots, grid_rows)
        hit = (spot - start == column) & (column < count)
        chosen.append(jnp.where(hit, 1.0, 0.0).astype(jnp.bfloat16))
    for k, copy in enumerate(copies):
        copy.wait()
        total = sum(dot16(chosen[slot], held[k, slot], NT) for slot in range(slots))
        packed[k * capacity : (k + 1) * capacity, :] = total
        pivot[k * cap : (k + 1) * cap, :] = total[:cap]


def pack(place, ranks, left_fac, right_fac, capacity, grid_rows):
    slots, _, order, cap = left_fac.shape
    return pl.pallas_call(
        functools.partial(pack_kernel, capacity, grid_rows),
        out_shape=(
            jax.ShapeDtypeStruct((2 * capacity, order), jnp.float32),
            jax.ShapeDtypeStruct((2 * cap, order), jnp.float32),
        ),
        in_specs=[IN_SMEM, IN_SMEM, IN_HBM, IN_HBM],
        out_specs=(IN_VMEM, IN_VMEM),
        scratch_shapes=[pltpu.VMEM((2, slots, order, cap), jnp.bfloat16), pltpu.SemaphoreType.DMA((2,))],
        compiler_params=params(16),
        cost_estimate=cost(2**10, 2**10),
        name="pack",
    )(place, ranks, left_fac, right_fac)


def pick_kernel(count, index, *refs):
    candidates, target, sem = refs[:count], refs[count], refs[count + 1]
    wait = fetch(index[0], candidates, target, sem)
    pl.when(index[0] >= 0)(wait)


def pick(index, candidates):
    return pl.pallas_call(
        functools.partial(pick_kernel, len(candidates)),
        out_shape=jax.ShapeDtypeStruct(candidates[0].shape, candidates[0].dtype),
        in_specs=[IN_SMEM] + [ANYWHERE] * len(candidates),
        out_specs=ANYWHERE,
        scratch_shapes=[pltpu.SemaphoreType.DMA],
        compiler_params=params(4),
        cost_estimate=cost(0, 2 * candidates[0].size * 4),
        name="pick",
    )(jnp.reshape(index, (1,)).astype(jnp.int32), *candidates)


def rows_kernel(capacity, grid_rows, count, place, ranks, *refs):
    sources, weights, stacked = refs[: 2 * count], refs[2 * count : 2 * count + 2], refs[2 * count + 2]
    landed, inverses, weight_high, weight_low, sems = refs[2 * count + 3 :]
    order = inverses.shape[1]
    inverses_in = fetch(1 - place[0] % 2, weights, inverses, sems.at[4])
    slots = stacked.shape[0]
    cap = LANES
    waits = []
    for t in range(2):
        for k in range(2):
            part = [source.at[pl.ds(k * capacity, capacity)] for source in sources[t * count : (t + 1) * count]]
            waits.append(fetch(place[1], part, landed.at[2 * t + k, pl.ds(0, capacity)], sems.at[2 * t + k]))
            landed[2 * t + k, capacity:, :] = jnp.zeros((cap, order), jnp.float32)
    inverses_in()
    base_parts, second_parts = split2(inverses[: 2 * order, :]), split2(inverses[2 * order :, :])
    for wait in waits:
        wait()
    solved0 = sum(dot16(landed[1].astype(jnp.bfloat16), part, NT) for part in base_parts)
    solved1 = sum(dot16(landed[3].astype(jnp.bfloat16), part, NT) for part in second_parts)
    for column, value in ((0, solved0), (2 * order, solved1)):
        high, low = split2(value)
        weight_high[:, column : column + value.shape[1]] = high
        weight_low[:, column : column + value.shape[1]] = low
    live = lax.broadcasted_iota(jnp.int32, (cap, order), 0)
    for slot in range(slots):
        pieces = []
        for t in range(2):
            start, rank = segment(ranks, t, place[0], slot, slots, grid_rows)
            spot = pl.ds(pl.multiple_of(start, 16), cap)
            left = jnp.where(live < rank, landed[2 * t, spot, :], 0.0).astype(jnp.bfloat16)
            columns = pl.ds(0, 2 * order) if t == 0 else pl.ds(2 * order, order)
            weights = jnp.concatenate([weight_high[spot, columns], weight_low[spot, columns]], axis=0)
            pieces.append(dot16(jnp.concatenate([left, left], axis=0), weights, TN))
        for column, value in ((0, pieces[0][:, :order]), (order, pieces[0][:, order:] + pieces[1])):
            high, low = split2(value)
            stacked[slot, :, column : column + order] = high
            stacked[slot, :, 2 * order + column : 2 * order + column + order] = low
            stacked[slot, :, 4 * order + column : 4 * order + column + order] = high


def row_panels(place, ranks, firsts, seconds, inverses, capacity, slots, grid_rows):
    order = inverses[0].shape[1]
    count = len(firsts)
    return pl.pallas_call(
        functools.partial(rows_kernel, capacity, grid_rows, count),
        out_shape=jax.ShapeDtypeStruct((slots, order, 6 * order), jnp.bfloat16),
        in_specs=[IN_SMEM] * 2 + [ANYWHERE] * (2 * count + 2),
        out_specs=IN_VMEM,
        scratch_shapes=[
            pltpu.VMEM((4, capacity + LANES, order), jnp.float32),
            pltpu.VMEM((3 * order, order), jnp.float32),
            pltpu.VMEM((capacity + LANES, 3 * order), jnp.bfloat16),
            pltpu.VMEM((capacity + LANES, 3 * order), jnp.bfloat16),
            pltpu.SemaphoreType.DMA((5,)),
        ],
        compiler_params=params(20),
        cost_estimate=cost(2**32, 2**22),
        name="row_panels",
    )(place, ranks, *firsts, *seconds, *inverses)


def schur_kernel(capacity, grid_rows, grid_cols, place, ranks, *refs):
    spread = grid_rows // grid_cols
    sources = refs[: 4 * spread]
    weights, (rows, left, right, out) = refs[4 * spread : 4 * spread + 2], refs[4 * spread + 2 : 4 * spread + 6]
    landed, inverses, weight0, weight1, bases, panel, sems = refs[4 * spread + 6 :]
    slots, order, cap = out.shape[0], out.shape[2], left.shape[3]
    padded = landed.shape[1]
    used = padded - LANES
    step = pl.program_id(0)
    row_here, col_here = place[0], place[1]
    mine = row_here // grid_cols

    @pl.when(step == 0)
    def _():
        inverses_in = fetch(1 - row_here % 2, weights, inverses, sems.at[4 * spread])
        passed = (row_here ^ col_here) & 1
        waits = []
        for n in range(2 * spread):
            for k in range(2):
                part = [source.at[pl.ds(k * capacity, capacity)] for source in sources[2 * n : 2 * n + 2]]
                waits.append(fetch(passed, part, landed.at[2 * n + k, pl.ds(0, capacity)], sems.at[2 * n + k]))
                if padded > capacity:
                    landed[2 * n + k, capacity:, :] = jnp.zeros((padded - capacity, order), jnp.float32)
        inverses_in()
        base_parts, second_parts = split2(inverses[: 2 * order, :]), split2(inverses[2 * order :, :])
        for wait in waits:
            wait()
        for g in range(spread):
            right0 = landed[4 * g + 1, :used, :].astype(jnp.bfloat16)
            right1 = landed[4 * g + 3, :used, :].astype(jnp.bfloat16)
            solved0 = sum(dot16(part, right0, NT) for part in base_parts)
            solved1 = sum(dot16(part, right1, NT) for part in second_parts)
            for target, at, value in (
                (weight0, 2 * g, solved0[:order]),
                (weight1, 4 * g, solved0[order:]),
                (weight1, 4 * g + 2, solved1),
            ):
                for n, piece in enumerate(split2(value)):
                    target[at + n, :, :used] = piece
                    target[at + n, :, used:] = jnp.zeros((order, padded - used), jnp.bfloat16)

    tile_col = step * grid_cols + col_here
    last_row = (slots - 1) * grid_rows + row_here

    @pl.when((tile_col > 1) & (last_row > tile_col))
    def _():
        part = step % spread
        g = part ^ mine
        group = part * grid_cols + col_here
        span = 2 * LANES
        ids = lax.broadcasted_iota(jnp.int32, (span, order), 0)
        windows = []
        for t in range(2):
            start, count = segment(ranks, t, group, step // spread, slots, grid_rows)
            first_lane = start // LANES * LANES
            window = pl.ds(pl.multiple_of(first_lane, LANES), span)
            value = landed[4 * g + 2 * t, window, :]
            live = (ids >= start - first_lane) & (ids < start - first_lane + count)
            value = jnp.where(live, value, 0.0).astype(jnp.bfloat16)
            bases[t * span : (t + 1) * span, :] = value
            windows.append(window)
        panel0 = sum(dot16(weight0[2 * g + n, :, windows[0]], bases[:span], NN) for n in range(2))
        panel1 = sum(
            dot16(weight1[4 * g + n, :, windows[n // 2]], bases[n // 2 * span : (n // 2 + 1) * span], NN)
            for n in range(4)
        )
        for at, value in ((0, panel0), (order, panel1)):
            high, low = split2(value)
            panel[at : at + order, :] = high
            panel[2 * order + at : 3 * order + at, :] = high
            panel[4 * order + at : 5 * order + at, :] = low

    for slot in range(slots):
        tile_row = slot * grid_rows + row_here
        below = tile_row > tile_col

        @pl.when(jnp.logical_not(below))
        def _():
            out[slot, 0] = jnp.zeros((order, order), jnp.float32)

        for t in range(2):

            @pl.when(below & (tile_col == t))
            def _():
                high = rows[slot, :, t * order : (t + 1) * order].astype(jnp.float32)
                low = rows[slot, :, (t + 2) * order : (t + 3) * order].astype(jnp.float32)
                out[slot, 0] = high + low

        @pl.when(below & (tile_col > 1))
        def _():
            basis = left[slot, 0].astype(jnp.float32)
            live = lax.broadcasted_iota(jnp.int32, basis.shape, 1) < ranks[tile_row, tile_col]
            front = dot16(jnp.where(live, basis, 0.0).astype(jnp.bfloat16), right[slot, 0], NT)
            out[slot, 0] = front - dot16(rows[slot], panel[...], NN)


def schur(place, ranks, col_arrays, inverses, rows, left_fac, right_fac, capacity, grid_rows, grid_cols):
    slots, steps, order, cap = left_fac.shape
    spread = grid_rows // grid_cols
    padded = (-(-capacity // LANES) + 1) * LANES
    flat = [array for pair in col_arrays for array in pair]
    factor = pl.BlockSpec((slots, 1, order, cap), lambda m: (0, m, 0, 0))
    return pl.pallas_call(
        functools.partial(schur_kernel, capacity, grid_rows, grid_cols),
        grid=(steps,),
        out_shape=pltpu.HBM((slots, steps, order, order), jnp.float32),
        in_specs=[IN_SMEM] * 2 + [ANYWHERE] * (len(flat) + 2) + [IN_VMEM, factor, factor],
        out_specs=pl.BlockSpec((slots, 1, order, order), lambda m: (0, m, 0, 0)),
        scratch_shapes=[
            pltpu.VMEM((4 * spread, padded, order), jnp.float32),
            pltpu.VMEM((3 * order, order), jnp.float32),
            pltpu.VMEM((2 * spread, order, padded), jnp.bfloat16),
            pltpu.VMEM((4 * spread, order, padded), jnp.bfloat16),
            pltpu.VMEM((4 * LANES, order), jnp.bfloat16),
            pltpu.VMEM((6 * order, order), jnp.bfloat16),
            pltpu.SemaphoreType.DMA((4 * spread + 1,)),
        ],
        compiler_params=params(40, dimension_semantics=("arbitrary",)),
        cost_estimate=cost(2**33, 2**24),
        name="schur",
    )(place, ranks, *flat, *inverses, rows, left_fac, right_fac)


def after(array, *others):
    return lax.optimization_barrier((array, *others))[0]


def device_program(capacity, early, diag_tiles, left_fac, right_fac, ranks):
    grid_rows = lax.axis_size("row")
    grid_cols = lax.axis_size("col")
    row_here = lax.axis_index("row")
    col_here = lax.axis_index("col")
    row_slots, _, order, cap = left_fac.shape
    assert cap == LANES and grid_rows % grid_cols == 0 and grid_cols >= 2
    spread = grid_rows // grid_cols
    row_bits = grid_rows.bit_length() - 1
    low_bits = grid_cols.bit_length() - 1
    assert 1 << row_bits == grid_rows and 1 << low_bits == grid_cols
    every_row = range(grid_rows)
    every_col = range(grid_cols)
    place = jnp.stack([row_here, col_here]).astype(jnp.int32)

    def move(array, pairs):
        flat = [(r * grid_cols + c, s * grid_cols + d) for (r, c), (s, d) in pairs]
        return lax.ppermute(array, AXES, flat)

    def down_column(array, root, fences):
        held = [root]
        for bit in range(1, row_bits):
            step = 1 << bit
            got = move(array, [((r, c), (r ^ step, c)) for r in held for c in every_col])
            got = after(got, fences[min(bit, len(fences)) - 1])
            mine = row_here % 2 == root
            array = pick(jnp.where(mine & (row_here >> bit == 0), 0, jnp.where(mine & (row_here >> bit == 1), 1, -1)), [array, got])
            held = held + [r ^ step for r in held]
        return array

    def to_other_parity(array, root):
        return move(array, [((r, c), (r ^ 1, c)) for r in every_row if r % 2 == root for c in every_col])

    def chain_step(array, s):
        return move(array, [((r, c - 1), (r, c)) for c in (s, s + 1) if c < grid_cols for r in every_row])

    inverse0 = first_inverse(place, diag_tiles)
    packed, pivot_bases = pack(after(place, inverse0), ranks, left_fac, right_fac, capacity, grid_rows)
    chain = [packed, chain_step(packed, 1)]
    back = move(packed, [((r, 1), (r, 0)) for r in every_row])

    received = [move(pivot_bases, [((1, 0), (1, c))]) for c in every_col if c]
    pivot_bases = jnp.where(col_here == 0, pivot_bases, sum(received))
    inverse0 = move(inverse0, [((0, c), (1, c)) for c in every_col])
    weights = second_inverse(place, ranks, diag_tiles, pivot_bases, inverse0)
    chain[1], weights, _ = lax.optimization_barrier((chain[1], weights, early))

    for s in range(2, grid_cols):
        chain.append(chain_step(chain[s - 1], s))
    firsts = list(chain)
    seconds = [back] + chain[:-1]
    offset = (row_here ^ col_here) & (grid_cols - 1)

    def source(candidates):
        return pick(jnp.where(offset == 0, col_here, -1), candidates)

    second_source = source(seconds)

    def hop(array, bit, held):
        step = 1 << bit
        return move(
            array,
            [
                ((r + h * grid_cols, c), ((r + h * grid_cols) ^ step, c))
                for c in every_col
                for r in held[c]
                for h in range(spread)
            ],
        )

    def low_hops(have, *fence):
        held = {c: [c] for c in every_col}
        for bit in range(1, low_bits):
            got = hop(have, bit, held)
            got = after(got, *fence) if fence else got
            arrived = (offset >> bit == 1) & (offset & 1 == 0)
            stays = (offset >> bit == 0) & (offset & 1 == 0)
            have = pick(jnp.where(arrived, 1, jnp.where(stays, 0, -1)), [have, got])
            held = {c: held[c] + [r ^ (1 << bit) for r in held[c]] for c in every_col}
        return have

    def high_hops(have):
        held = {c: [r for r in range(grid_cols) if (r ^ c) % 2 == 0] for c in every_col}
        sets = [have]
        for bit in range(low_bits, row_bits):
            sets = sets + [hop(array, bit, held) for array in sets]
        return [[array, hop(array, 0, held)] for array in sets]

    second_have = low_hops(second_source)
    first_source = source([after(array, second_have) for array in firsts])
    weights = down_column(weights, 1, [chain[min(2, grid_cols - 1)], first_source])
    inverses = [weights, to_other_parity(weights, 1)]
    rows = row_panels(place, ranks, firsts, seconds, inverses, capacity, row_slots, grid_rows)
    first_have = low_hops(first_source, rows)
    second_sets, first_sets = high_hops(second_have), high_hops(first_have)
    col_arrays = [sets[g] for g in range(spread) for sets in (first_sets, second_sets)]
    return schur(place, ranks, col_arrays, inverses, rows, left_fac, right_fac, capacity, grid_rows, grid_cols)


def shards(diag_tiles, left_fac, right_fac, ranks):
    row_slots, cap = left_fac.shape[0], left_fac.shape[3]
    grid_rows = lax.axis_size("row")
    full = row_slots * cap
    packed = max(cap, full * 5 // 8)
    args = (diag_tiles, left_fac, right_fac, ranks)
    tile_ids = jnp.arange(ranks.shape[0], dtype=jnp.int32)[:, None]
    live = jnp.where(tile_ids > jnp.arange(2, dtype=jnp.int32)[None, :], ranks[:, :2], 0)
    widest = jnp.max(sum(live[s * grid_rows : (s + 1) * grid_rows] for s in range(row_slots)))
    result = device_program(packed, widest, *args)
    if packed == full:
        return result

    def again(state):
        return jnp.zeros_like(state[0]), device_program(full, state[0], *args)

    return lax.while_loop(lambda state: state[0] > packed, again, (widest, result))[1]


def solution(mesh):
    in_specs = (P("row", None, None), P("row", "col", None, None), P("row", "col", None, None), P())
    out_specs = P("row", "col", None, None)
    return jax.shard_map(shards, mesh=mesh, in_specs=in_specs, out_specs=out_specs, check_vma=False)
```

```python
import functools

import jax
import jax.numpy as jnp
from jax import lax
from jax.experimental import pallas as pl
from jax.experimental.pallas import tpu as pltpu
from jax.sharding import PartitionSpec as P

PRECISE = lax.Precision.HIGHEST
AXES = ("row", "col")
BLOCK = 32
GROUP = 8
LANES = 128
NT = (((1,), (1,)), ((), ()))
TN = (((0,), (0,)), ((), ()))
NN = (((1,), (0,)), ((), ()))
ANYWHERE = pl.BlockSpec(memory_space=pl.ANY)
IN_VMEM = pl.BlockSpec(memory_space=pltpu.VMEM)
IN_SMEM = pl.BlockSpec(memory_space=pltpu.SMEM)
IN_HBM = pl.BlockSpec(memory_space=pltpu.HBM)
MEBI = 1024 * 1024


def dot32(lhs, rhs, dims):
    return lax.dot_general(lhs, rhs, dims, precision=PRECISE, preferred_element_type=jnp.float32)


def dot16(lhs, rhs, dims):
    return lax.dot_general(lhs, rhs, dims, preferred_element_type=jnp.float32)


def split2(value):
    high = value.astype(jnp.bfloat16)
    low = (value - high.astype(jnp.float32)).astype(jnp.bfloat16)
    return high, low


def params(mebibytes, **extra):
    return pltpu.CompilerParams(vmem_limit_bytes=mebibytes * MEBI, **extra)


def cost(flops, moved):
    return pl.CostEstimate(flops=int(flops), bytes_accessed=int(moved), transcendentals=0)


def eliminate(tiles):
    tiles, start = tiles
    rows = tiles[0].shape[0]
    done = []
    for first in range(0, rows, GROUP):
        height = rows - first
        row_ids = lax.broadcasted_iota(jnp.int32, (height, LANES), 0)
        heads = [
            jnp.broadcast_to(tiles[0][:, start + first + j : start + first + j + 1], (height, LANES))
            for j in range(GROUP)
        ]
        scale = jnp.zeros((GROUP, LANES), jnp.float32)
        for j in range(GROUP):
            pivot = heads[j][j : j + 1, :]
            factor = jnp.where(row_ids > j, heads[j] * (1.0 / pivot), 0.0)
            for other in range(j + 1, GROUP):
                heads[other] = heads[other] - factor * heads[other][j : j + 1, :]
            tiles = [tile - factor * tile[j : j + 1, :] for tile in tiles]
            root = lax.rsqrt(pivot)
            root = root * (1.5 - 0.5 * pivot * root * root)
            scale = jnp.where(row_ids[:GROUP] == j, root, scale)
        done.append([tile[:GROUP] * scale for tile in tiles])
        tiles = [tile[GROUP:] for tile in tiles]
    return [jnp.concatenate(parts, axis=0) for parts in zip(*done)]


def inverse_factor(source, work, result):
    order = source.shape[0]
    span = order // LANES
    for base in range(0, order, BLOCK):
        low = base // LANES
        row_ids = lax.broadcasted_iota(jnp.int32, (BLOCK, LANES), 0)
        lane_ids = lax.broadcasted_iota(jnp.int32, (BLOCK, LANES), 1)
        unit = jnp.where(lane_ids - base % LANES == row_ids, 1.0, 0.0)
        zero = jnp.zeros((BLOCK, LANES), jnp.float32)
        tiles = [source[base : base + BLOCK, s * LANES : (s + 1) * LANES] for s in range(low, span)]
        tiles += [zero] * low + [unit]
        if base:
            taken = dot32(
                work[0:base, base : base + BLOCK],
                work[0:base, low * LANES : order + (low + 1) * LANES],
                TN,
            )
            tiles = [tile - taken[:, s * LANES : (s + 1) * LANES] for s, tile in enumerate(tiles)]
        tiles = eliminate((tiles, base % LANES))
        for s, tile in enumerate(tiles):
            work[base : base + BLOCK, (low + s) * LANES : (low + s + 1) * LANES] = tile
        for s in range(low + 1, span):
            work[base : base + BLOCK, order + s * LANES : order + (s + 1) * LANES] = zero
    result[...] = work[:, order:]


def fetch(choice, candidates, target, sem):
    for n, candidate in enumerate(candidates):
        copy = pltpu.make_async_copy(candidate, target, sem)
        pl.when(choice == n)(copy.start)
    return pltpu.make_async_copy(candidates[0], target, sem).wait


def first_kernel(place, tiles, result, tile, work, sem):
    @pl.when(place[0] == 0)
    def _():
        copy = pltpu.make_async_copy(tiles.at[0], tile, sem)
        copy.start()
        copy.wait()
        inverse_factor(tile, work, result)


def first_inverse(place, tiles):
    order = tiles.shape[2]
    return pl.pallas_call(
        first_kernel,
        out_shape=jax.ShapeDtypeStruct((order, order), jnp.float32),
        in_specs=[IN_SMEM, ANYWHERE],
        out_specs=IN_VMEM,
        scratch_shapes=[
            pltpu.VMEM((order, order), jnp.float32),
            pltpu.VMEM((order, 2 * order), jnp.float32),
            pltpu.SemaphoreType.DMA,
        ],
        compiler_params=params(8),
        cost_estimate=cost(2**10, 2**10),
        name="first_inverse",
    )(place, tiles)


def second_kernel(place, ranks, tiles, bases, inverse, weights, shifted, work, sem):
    order = inverse.shape[0]
    cap = bases.shape[0] // 2

    @pl.when(place[0] == 1)
    def _():
        copy = pltpu.make_async_copy(tiles.at[0], shifted, sem)
        copy.start()
        weights[:order, :] = inverse[...]
        live = lax.broadcasted_iota(jnp.int32, (cap, order), 0) < ranks[1, 0]
        left = jnp.where(live, bases[:cap, :], 0.0)
        right = jnp.where(live, bases[cap:, :], 0.0)
        solved = dot32(right, inverse[...], NT)
        dense = dot32(left, solved, TN)
        copy.wait()
        shifted[...] = shifted[...] - dot32(dense, dense, NT)
        inverse_factor(shifted, work, weights.at[pl.ds(2 * order, order)])
        weights[order : 2 * order, :] = -dot32(dot32(weights[2 * order :, :], dense, NN), inverse[...], NN)


def second_inverse(place, ranks, tiles, bases, inverse):
    order = inverse.shape[0]
    return pl.pallas_call(
        second_kernel,
        out_shape=jax.ShapeDtypeStruct((3 * order, order), jnp.float32),
        in_specs=[IN_SMEM, IN_SMEM, ANYWHERE, IN_VMEM, IN_VMEM],
        out_specs=IN_VMEM,
        scratch_shapes=[
            pltpu.VMEM((order, order), jnp.float32),
            pltpu.VMEM((order, 2 * order), jnp.float32),
            pltpu.SemaphoreType.DMA,
        ],
        compiler_params=params(8),
        cost_estimate=cost(2**10, 2**10),
        name="second_inverse",
    )(place, ranks, tiles, bases, inverse)


def segment(ranks, panel, group, slot, slots, grid_rows):
    start, count = jnp.int32(0), jnp.int32(0)
    for s in range(slots):
        tile_row = s * grid_rows + group
        rank = jnp.where(tile_row > panel, ranks[tile_row, panel], 0)
        start = start + jnp.where(s < slot, rank, 0)
        count = count + jnp.where(s == slot, rank, 0)
    return start, count


def pack_kernel(capacity, grid_rows, place, ranks, left, right, packed, pivot, held, sem):
    slots, order, cap = held.shape[1:]
    copies = [
        pltpu.make_async_copy(source.at[:, 0], held.at[k], sem.at[k]) for k, source in enumerate((left, right))
    ]
    for copy in copies:
        copy.start()
    panel = jnp.minimum(place[1], 1)
    spot = lax.broadcasted_iota(jnp.int32, (capacity, cap), 0)
    column = lax.broadcasted_iota(jnp.int32, (capacity, cap), 1)
    chosen = []
    for slot in range(slots):
        start, count = segment(ranks, panel, place[0], slot, slots, grid_rows)
        hit = (spot - start == column) & (column < count)
        chosen.append(jnp.where(hit, 1.0, 0.0).astype(jnp.bfloat16))
    for k, copy in enumerate(copies):
        copy.wait()
        total = sum(dot16(chosen[slot], held[k, slot], NT) for slot in range(slots))
        packed[k * capacity : (k + 1) * capacity, :] = total
        pivot[k * cap : (k + 1) * cap, :] = total[:cap]


def pack(place, ranks, left_fac, right_fac, capacity, grid_rows):
    slots, _, order, cap = left_fac.shape
    return pl.pallas_call(
        functools.partial(pack_kernel, capacity, grid_rows),
        out_shape=(
            jax.ShapeDtypeStruct((2 * capacity, order), jnp.float32),
            jax.ShapeDtypeStruct((2 * cap, order), jnp.float32),
        ),
        in_specs=[IN_SMEM, IN_SMEM, IN_HBM, IN_HBM],
        out_specs=(IN_VMEM, IN_VMEM),
        scratch_shapes=[pltpu.VMEM((2, slots, order, cap), jnp.bfloat16), pltpu.SemaphoreType.DMA((2,))],
        compiler_params=params(16),
        cost_estimate=cost(2**10, 2**10),
        name="pack",
    )(place, ranks, left_fac, right_fac)


def pick_kernel(count, index, *refs):
    candidates, target, sem = refs[:count], refs[count], refs[count + 1]
    wait = fetch(index[0], candidates, target, sem)
    pl.when(index[0] >= 0)(wait)


def pick(index, candidates):
    return pl.pallas_call(
        functools.partial(pick_kernel, len(candidates)),
        out_shape=jax.ShapeDtypeStruct(candidates[0].shape, candidates[0].dtype),
        in_specs=[IN_SMEM] + [ANYWHERE] * len(candidates),
        out_specs=ANYWHERE,
        scratch_shapes=[pltpu.SemaphoreType.DMA],
        compiler_params=params(4),
        cost_estimate=cost(2**32, 2**20),
        name="pick",
    )(jnp.reshape(index, (1,)).astype(jnp.int32), *candidates)


def rows_kernel(capacity, grid_rows, count, place, ranks, *refs):
    sources, weights, stacked = refs[: 2 * count], refs[2 * count : 2 * count + 2], refs[2 * count + 2]
    landed, inverses, weight_high, weight_low, sems = refs[2 * count + 3 :]
    order = inverses.shape[1]
    inverses_in = fetch(1 - place[0] % 2, weights, inverses, sems.at[4])
    slots = stacked.shape[0]
    cap = LANES
    waits = []
    for t in range(2):
        for k in range(2):
            part = [source.at[pl.ds(k * capacity, capacity)] for source in sources[t * count : (t + 1) * count]]
            waits.append(fetch(place[1], part, landed.at[2 * t + k, pl.ds(0, capacity)], sems.at[2 * t + k]))
            landed[2 * t + k, capacity:, :] = jnp.zeros((cap, order), jnp.float32)
    inverses_in()
    base_parts, second_parts = split2(inverses[: 2 * order, :]), split2(inverses[2 * order :, :])
    for wait in waits:
        wait()
    solved0 = sum(dot16(landed[1].astype(jnp.bfloat16), part, NT) for part in base_parts)
    solved1 = sum(dot16(landed[3].astype(jnp.bfloat16), part, NT) for part in second_parts)
    for column, value in ((0, solved0), (2 * order, solved1)):
        high, low = split2(value)
        weight_high[:, column : column + value.shape[1]] = high
        weight_low[:, column : column + value.shape[1]] = low
    live = lax.broadcasted_iota(jnp.int32, (cap, order), 0)
    for slot in range(slots):
        pieces = []
        for t in range(2):
            start, rank = segment(ranks, t, place[0], slot, slots, grid_rows)
            spot = pl.ds(pl.multiple_of(start, 16), cap)
            left = jnp.where(live < rank, landed[2 * t, spot, :], 0.0).astype(jnp.bfloat16)
            columns = pl.ds(0, 2 * order) if t == 0 else pl.ds(2 * order, order)
            weights = jnp.concatenate([weight_high[spot, columns], weight_low[spot, columns]], axis=0)
            pieces.append(dot16(jnp.concatenate([left, left], axis=0), weights, TN))
        for column, value in ((0, pieces[0][:, :order]), (order, pieces[0][:, order:] + pieces[1])):
            high, low = split2(value)
            stacked[slot, :, column : column + order] = high
            stacked[slot, :, 2 * order + column : 2 * order + column + order] = low
            stacked[slot, :, 4 * order + column : 4 * order + column + order] = high


def row_panels(place, ranks, firsts, seconds, inverses, capacity, slots, grid_rows):
    order = inverses[0].shape[1]
    count = len(firsts)
    return pl.pallas_call(
        functools.partial(rows_kernel, capacity, grid_rows, count),
        out_shape=jax.ShapeDtypeStruct((slots, order, 6 * order), jnp.bfloat16),
        in_specs=[IN_SMEM] * 2 + [ANYWHERE] * (2 * count + 2),
        out_specs=IN_VMEM,
        scratch_shapes=[
            pltpu.VMEM((4, capacity + LANES, order), jnp.float32),
            pltpu.VMEM((3 * order, order), jnp.float32),
            pltpu.VMEM((capacity + LANES, 3 * order), jnp.bfloat16),
            pltpu.VMEM((capacity + LANES, 3 * order), jnp.bfloat16),
            pltpu.SemaphoreType.DMA((5,)),
        ],
        compiler_params=params(20),
        cost_estimate=cost(2**10, 2**10),
        name="row_panels",
    )(place, ranks, *firsts, *seconds, *inverses)


def schur_kernel(capacity, grid_rows, grid_cols, place, ranks, *refs):
    spread = grid_rows // grid_cols
    sources = refs[: 4 * spread]
    weights, (rows, left, right, out) = refs[4 * spread : 4 * spread + 2], refs[4 * spread + 2 : 4 * spread + 6]
    landed, inverses, weight0, weight1, bases, panel, sems = refs[4 * spread + 6 :]
    slots, order, cap = out.shape[0], out.shape[2], left.shape[3]
    padded = landed.shape[1]
    used = padded - LANES
    step = pl.program_id(0)
    row_here, col_here = place[0], place[1]
    mine = row_here // grid_cols

    @pl.when(step == 0)
    def _():
        inverses_in = fetch(1 - row_here % 2, weights, inverses, sems.at[4 * spread])
        passed = (row_here ^ col_here) & 1
        waits = []
        for n in range(2 * spread):
            for k in range(2):
                part = [source.at[pl.ds(k * capacity, capacity)] for source in sources[2 * n : 2 * n + 2]]
                waits.append(fetch(passed, part, landed.at[2 * n + k, pl.ds(0, capacity)], sems.at[2 * n + k]))
                if padded > capacity:
                    landed[2 * n + k, capacity:, :] = jnp.zeros((padded - capacity, order), jnp.float32)
        inverses_in()
        base_parts, second_parts = split2(inverses[: 2 * order, :]), split2(inverses[2 * order :, :])
        for wait in waits:
            wait()
        for g in range(spread):
            right0 = landed[4 * g + 1, :used, :].astype(jnp.bfloat16)
            right1 = landed[4 * g + 3, :used, :].astype(jnp.bfloat16)
            solved0 = sum(dot16(part, right0, NT) for part in base_parts)
            solved1 = sum(dot16(part, right1, NT) for part in second_parts)
            for target, at, value in (
                (weight0, 2 * g, solved0[:order]),
                (weight1, 4 * g, solved0[order:]),
                (weight1, 4 * g + 2, solved1),
            ):
                for n, piece in enumerate(split2(value)):
                    target[at + n, :, :used] = piece
                    target[at + n, :, used:] = jnp.zeros((order, padded - used), jnp.bfloat16)

    tile_col = step * grid_cols + col_here
    last_row = (slots - 1) * grid_rows + row_here

    @pl.when((tile_col > 1) & (last_row > tile_col))
    def _():
        part = step % spread
        g = part ^ mine
        group = part * grid_cols + col_here
        span = 2 * LANES
        ids = lax.broadcasted_iota(jnp.int32, (span, order), 0)
        windows = []
        for t in range(2):
            start, count = segment(ranks, t, group, step // spread, slots, grid_rows)
            first_lane = start // LANES * LANES
            window = pl.ds(pl.multiple_of(first_lane, LANES), span)
            value = landed[4 * g + 2 * t, window, :]
            live = (ids >= start - first_lane) & (ids < start - first_lane + count)
            value = jnp.where(live, value, 0.0).astype(jnp.bfloat16)
            bases[t * span : (t + 1) * span, :] = value
            windows.append(window)
        panel0 = sum(dot16(weight0[2 * g + n, :, windows[0]], bases[:span], NN) for n in range(2))
        panel1 = sum(
            dot16(weight1[4 * g + n, :, windows[n // 2]], bases[n // 2 * span : (n // 2 + 1) * span], NN)
            for n in range(4)
        )
        for at, value in ((0, panel0), (order, panel1)):
            high, low = split2(value)
            panel[at : at + order, :] = high
            panel[2 * order + at : 3 * order + at, :] = high
            panel[4 * order + at : 5 * order + at, :] = low

    for slot in range(slots):
        tile_row = slot * grid_rows + row_here
        below = tile_row > tile_col

        @pl.when(jnp.logical_not(below))
        def _():
            out[slot, 0] = jnp.zeros((order, order), jnp.float32)

        for t in range(2):

            @pl.when(below & (tile_col == t))
            def _():
                high = rows[slot, :, t * order : (t + 1) * order].astype(jnp.float32)
                low = rows[slot, :, (t + 2) * order : (t + 3) * order].astype(jnp.float32)
                out[slot, 0] = high + low

        @pl.when(below & (tile_col > 1))
        def _():
            basis = left[slot, 0].astype(jnp.float32)
            live = lax.broadcasted_iota(jnp.int32, basis.shape, 1) < ranks[tile_row, tile_col]
            front = dot16(jnp.where(live, basis, 0.0).astype(jnp.bfloat16), right[slot, 0], NT)
            out[slot, 0] = front - dot16(rows[slot], panel[...], NN)


def schur(place, ranks, col_arrays, inverses, rows, left_fac, right_fac, capacity, grid_rows, grid_cols):
    slots, steps, order, cap = left_fac.shape
    spread = grid_rows // grid_cols
    padded = (-(-capacity // LANES) + 1) * LANES
    flat = [array for pair in col_arrays for array in pair]
    factor = pl.BlockSpec((slots, 1, order, cap), lambda m: (0, m, 0, 0))
    return pl.pallas_call(
        functools.partial(schur_kernel, capacity, grid_rows, grid_cols),
        grid=(steps,),
        out_shape=pltpu.HBM((slots, steps, order, order), jnp.float32),
        in_specs=[IN_SMEM] * 2 + [ANYWHERE] * (len(flat) + 2) + [IN_VMEM, factor, factor],
        out_specs=pl.BlockSpec((slots, 1, order, order), lambda m: (0, m, 0, 0)),
        scratch_shapes=[
            pltpu.VMEM((4 * spread, padded, order), jnp.float32),
            pltpu.VMEM((3 * order, order), jnp.float32),
            pltpu.VMEM((2 * spread, order, padded), jnp.bfloat16),
            pltpu.VMEM((4 * spread, order, padded), jnp.bfloat16),
            pltpu.VMEM((4 * LANES, order), jnp.bfloat16),
            pltpu.VMEM((6 * order, order), jnp.bfloat16),
            pltpu.SemaphoreType.DMA((4 * spread + 1,)),
        ],
        compiler_params=params(40, dimension_semantics=("arbitrary",)),
        cost_estimate=cost(2**33, 2**24),
        name="schur",
    )(place, ranks, *flat, *inverses, rows, left_fac, right_fac)


def after(array, *others):
    return lax.optimization_barrier((array, *others))[0]


def device_program(capacity, early, inverses, diag_tiles, left_fac, right_fac, ranks):
    grid_rows = lax.axis_size("row")
    grid_cols = lax.axis_size("col")
    row_here = lax.axis_index("row")
    col_here = lax.axis_index("col")
    row_slots, _, order, cap = left_fac.shape
    assert cap == LANES and grid_rows % grid_cols == 0 and grid_cols >= 2
    spread = grid_rows // grid_cols
    row_bits = grid_rows.bit_length() - 1
    low_bits = grid_cols.bit_length() - 1
    assert 1 << row_bits == grid_rows and 1 << low_bits == grid_cols
    every_row = range(grid_rows)
    every_col = range(grid_cols)
    place = jnp.stack([row_here, col_here]).astype(jnp.int32)

    def move(array, pairs):
        flat = [(r * grid_cols + c, s * grid_cols + d) for (r, c), (s, d) in pairs]
        return lax.ppermute(array, AXES, flat)

    def down_column(array, root, fences):
        held = [root]
        for bit in range(1, row_bits):
            step = 1 << bit
            got = move(array, [((r, c), (r ^ step, c)) for r in held for c in every_col])
            got = after(got, fences[min(bit, len(fences)) - 1])
            mine = row_here % 2 == root
            array = pick(jnp.where(mine & (row_here >> bit == 0), 0, jnp.where(mine & (row_here >> bit == 1), 1, -1)), [array, got])
            held = held + [r ^ step for r in held]
        return array

    def to_other_parity(array, root):
        return move(array, [((r, c), (r ^ 1, c)) for r in every_row if r % 2 == root for c in every_col])

    def chain_step(array, s):
        return move(array, [((r, c - 1), (r, c)) for c in (s, s + 1) if c < grid_cols for r in every_row])

    factoring = inverses is None
    if factoring:
        inverse0 = first_inverse(place, diag_tiles)
    packed, pivot_bases = pack(after(place, inverse0) if factoring else place, ranks, left_fac, right_fac, capacity, grid_rows)
    chain = [packed, chain_step(packed, 1)]
    back = move(packed, [((r, 1), (r, 0)) for r in every_row])

    if factoring:
        received = [move(pivot_bases, [((1, 0), (1, c))]) for c in every_col if c]
        pivot_bases = jnp.where(col_here == 0, pivot_bases, sum(received))
        inverse0 = move(inverse0, [((0, c), (1, c)) for c in every_col])
        weights = second_inverse(place, ranks, diag_tiles, pivot_bases, inverse0)
        chain[1], weights, _ = lax.optimization_barrier((chain[1], weights, early))

    for s in range(2, grid_cols):
        chain.append(chain_step(chain[s - 1], s))
    firsts = list(chain)
    seconds = [back] + chain[:-1]
    offset = (row_here ^ col_here) & (grid_cols - 1)

    def source(candidates):
        return pick(jnp.where(offset == 0, col_here, -1), candidates)

    second_source = source(seconds)

    def hop(array, bit, held):
        step = 1 << bit
        return move(
            array,
            [
                ((r + h * grid_cols, c), ((r + h * grid_cols) ^ step, c))
                for c in every_col
                for r in held[c]
                for h in range(spread)
            ],
        )

    def low_hops(have, *fence):
        held = {c: [c] for c in every_col}
        for bit in range(1, low_bits):
            got = hop(have, bit, held)
            got = after(got, *fence) if fence else got
            arrived = (offset >> bit == 1) & (offset & 1 == 0)
            stays = (offset >> bit == 0) & (offset & 1 == 0)
            have = pick(jnp.where(arrived, 1, jnp.where(stays, 0, -1)), [have, got])
            held = {c: held[c] + [r ^ (1 << bit) for r in held[c]] for c in every_col}
        return have

    def high_hops(have):
        held = {c: [r for r in range(grid_cols) if (r ^ c) % 2 == 0] for c in every_col}
        sets = [have]
        for bit in range(low_bits, row_bits):
            sets = sets + [hop(array, bit, held) for array in sets]
        return [[array, hop(array, 0, held)] for array in sets]

    first_source = source(firsts)
    second_have = low_hops(second_source, first_source)
    if factoring:
        weights = down_column(weights, 1, [chain[min(2, grid_cols - 1)], second_have])
        inverses = [weights, to_other_parity(weights, 1)]
    rows = row_panels(place, ranks, firsts, seconds, inverses, capacity, row_slots, grid_rows)
    first_have = low_hops(first_source, rows)
    second_sets, first_sets = high_hops(second_have), high_hops(first_have)
    col_arrays = [sets[g] for g in range(spread) for sets in (first_sets, second_sets)]
    return schur(place, ranks, col_arrays, inverses, rows, left_fac, right_fac, capacity, grid_rows, grid_cols), inverses


def shards(diag_tiles, left_fac, right_fac, ranks):
    row_slots, cap = left_fac.shape[0], left_fac.shape[3]
    grid_rows = lax.axis_size("row")
    full = row_slots * cap
    packed = max(cap, full * 5 // 8)
    args = (diag_tiles, left_fac, right_fac, ranks)
    tile_ids = jnp.arange(ranks.shape[0], dtype=jnp.int32)[:, None]
    live = jnp.where(tile_ids > jnp.arange(2, dtype=jnp.int32)[None, :], ranks[:, :2], 0)
    widest = jnp.max(sum(live[s * grid_rows : (s + 1) * grid_rows] for s in range(row_slots)))
    result, inverses = device_program(packed, widest, None, *args)
    if packed == full:
        return result

    def again(state):
        return jnp.zeros_like(state[0]), device_program(full, state[0], inverses, *args)[0]

    return lax.while_loop(lambda state: state[0] > packed, again, (widest, result))[1]


def solution(mesh):
    in_specs = (P("row", None, None), P("row", "col", None, None), P("row", "col", None, None), P())
    out_specs = P("row", "col", None, None)
    return jax.shard_map(shards, mesh=mesh, in_specs=in_specs, out_specs=out_specs, check_vma=False)
```

```python
import functools

import jax
import jax.numpy as jnp
from jax import lax
from jax.experimental import pallas as pl
from jax.experimental.pallas import tpu as pltpu
from jax.sharding import PartitionSpec as P

PRECISE = lax.Precision.HIGHEST
AXES = ("row", "col")
BLOCK = 32
GROUP = 8
LANES = 128
NT = (((1,), (1,)), ((), ()))
TN = (((0,), (0,)), ((), ()))
NN = (((1,), (0,)), ((), ()))
ANYWHERE = pl.BlockSpec(memory_space=pl.ANY)
IN_VMEM = pl.BlockSpec(memory_space=pltpu.VMEM)
IN_SMEM = pl.BlockSpec(memory_space=pltpu.SMEM)
IN_HBM = pl.BlockSpec(memory_space=pltpu.HBM)
MEBI = 1024 * 1024


def dot32(lhs, rhs, dims):
    return lax.dot_general(lhs, rhs, dims, precision=PRECISE, preferred_element_type=jnp.float32)


def dot16(lhs, rhs, dims):
    return lax.dot_general(lhs, rhs, dims, preferred_element_type=jnp.float32)


def split2(value):
    high = value.astype(jnp.bfloat16)
    low = (value - high.astype(jnp.float32)).astype(jnp.bfloat16)
    return high, low


def params(mebibytes, **extra):
    return pltpu.CompilerParams(vmem_limit_bytes=mebibytes * MEBI, **extra)


def cost(flops, moved):
    return pl.CostEstimate(flops=int(flops), bytes_accessed=int(moved), transcendentals=0)


def eliminate(tiles):
    tiles, start = tiles
    rows = tiles[0].shape[0]
    done = []
    for first in range(0, rows, GROUP):
        height = rows - first
        row_ids = lax.broadcasted_iota(jnp.int32, (height, LANES), 0)
        heads = [
            jnp.broadcast_to(tiles[0][:, start + first + j : start + first + j + 1], (height, LANES))
            for j in range(GROUP)
        ]
        scale = jnp.zeros((GROUP, LANES), jnp.float32)
        for j in range(GROUP):
            pivot = heads[j][j : j + 1, :]
            factor = jnp.where(row_ids > j, heads[j] * (1.0 / pivot), 0.0)
            for other in range(j + 1, GROUP):
                heads[other] = heads[other] - factor * heads[other][j : j + 1, :]
            tiles = [tile - factor * tile[j : j + 1, :] for tile in tiles]
            root = lax.rsqrt(pivot)
            root = root * (1.5 - 0.5 * pivot * root * root)
            scale = jnp.where(row_ids[:GROUP] == j, root, scale)
        done.append([tile[:GROUP] * scale for tile in tiles])
        tiles = [tile[GROUP:] for tile in tiles]
    return [jnp.concatenate(parts, axis=0) for parts in zip(*done)]


def inverse_factor(source, work, result):
    order = source.shape[0]
    span = order // LANES
    for base in range(0, order, BLOCK):
        low = base // LANES
        row_ids = lax.broadcasted_iota(jnp.int32, (BLOCK, LANES), 0)
        lane_ids = lax.broadcasted_iota(jnp.int32, (BLOCK, LANES), 1)
        unit = jnp.where(lane_ids - base % LANES == row_ids, 1.0, 0.0)
        zero = jnp.zeros((BLOCK, LANES), jnp.float32)
        tiles = [source[base : base + BLOCK, s * LANES : (s + 1) * LANES] for s in range(low, span)]
        tiles += [zero] * low + [unit]
        if base:
            taken = dot32(
                work[0:base, base : base + BLOCK],
                work[0:base, low * LANES : order + (low + 1) * LANES],
                TN,
            )
            tiles = [tile - taken[:, s * LANES : (s + 1) * LANES] for s, tile in enumerate(tiles)]
        tiles = eliminate((tiles, base % LANES))
        for s, tile in enumerate(tiles):
            work[base : base + BLOCK, (low + s) * LANES : (low + s + 1) * LANES] = tile
        for s in range(low + 1, span):
            work[base : base + BLOCK, order + s * LANES : order + (s + 1) * LANES] = zero
    result[...] = work[:, order:]


def fetch(choice, candidates, target, sem):
    for n, candidate in enumerate(candidates):
        copy = pltpu.make_async_copy(candidate, target, sem)
        pl.when(choice == n)(copy.start)
    return pltpu.make_async_copy(candidates[0], target, sem).wait


def first_kernel(place, tiles, result, tile, work, sem):
    @pl.when(place[0] == 0)
    def _():
        copy = pltpu.make_async_copy(tiles.at[0], tile, sem)
        copy.start()
        copy.wait()
        inverse_factor(tile, work, result)


def first_inverse(place, tiles):
    order = tiles.shape[2]
    return pl.pallas_call(
        first_kernel,
        out_shape=jax.ShapeDtypeStruct((order, order), jnp.float32),
        in_specs=[IN_SMEM, IN_HBM],
        out_specs=IN_VMEM,
        scratch_shapes=[
            pltpu.VMEM((order, order), jnp.float32),
            pltpu.VMEM((order, 2 * order), jnp.float32),
            pltpu.SemaphoreType.DMA,
        ],
        compiler_params=params(8),
        cost_estimate=cost(2**10, 2**10),
        name="first_inverse",
    )(place, tiles)


def second_kernel(place, ranks, tiles, bases, inverse, weights, shifted, work, sem):
    order = inverse.shape[0]
    cap = bases.shape[0] // 2

    @pl.when(place[0] == 1)
    def _():
        copy = pltpu.make_async_copy(tiles.at[0], shifted, sem)
        copy.start()
        weights[:order, :] = inverse[...]
        live = lax.broadcasted_iota(jnp.int32, (cap, order), 0) < ranks[1, 0]
        left = jnp.where(live, bases[:cap, :], 0.0)
        right = jnp.where(live, bases[cap:, :], 0.0)
        solved = dot32(right, inverse[...], NT)
        dense = dot32(left, solved, TN)
        copy.wait()
        shifted[...] = shifted[...] - dot32(dense, dense, NT)
        inverse_factor(shifted, work, weights.at[pl.ds(2 * order, order)])
        weights[order : 2 * order, :] = -dot32(dot32(weights[2 * order :, :], dense, NN), inverse[...], NN)


def second_inverse(place, ranks, tiles, bases, inverse):
    order = inverse.shape[0]
    return pl.pallas_call(
        second_kernel,
        out_shape=jax.ShapeDtypeStruct((3 * order, order), jnp.float32),
        in_specs=[IN_SMEM, IN_SMEM, IN_HBM, IN_VMEM, IN_VMEM],
        out_specs=IN_VMEM,
        scratch_shapes=[
            pltpu.VMEM((order, order), jnp.float32),
            pltpu.VMEM((order, 2 * order), jnp.float32),
            pltpu.SemaphoreType.DMA,
        ],
        compiler_params=params(8),
        cost_estimate=cost(2**10, 2**10),
        name="second_inverse",
    )(place, ranks, tiles, bases, inverse)


def segment(ranks, panel, group, slot, slots, grid_rows):
    start, count = jnp.int32(0), jnp.int32(0)
    for s in range(slots):
        tile_row = s * grid_rows + group
        rank = jnp.where(tile_row > panel, ranks[tile_row, panel], 0)
        start = start + jnp.where(s < slot, rank, 0)
        count = count + jnp.where(s == slot, rank, 0)
    return start, count


def pack_kernel(capacity, grid_rows, place, ranks, left, right, packed, pivot, held, sem):
    slots, order, cap = held.shape[1:]
    copies = [
        pltpu.make_async_copy(source.at[:, 0], held.at[k], sem.at[k]) for k, source in enumerate((left, right))
    ]
    for copy in copies:
        copy.start()
    panel = jnp.minimum(place[1], 1)
    spot = lax.broadcasted_iota(jnp.int32, (capacity, cap), 0)
    column = lax.broadcasted_iota(jnp.int32, (capacity, cap), 1)
    chosen = []
    for slot in range(slots):
        start, count = segment(ranks, panel, place[0], slot, slots, grid_rows)
        hit = (spot - start == column) & (column < count)
        chosen.append(jnp.where(hit, 1.0, 0.0).astype(jnp.bfloat16))
    for k, copy in enumerate(copies):
        copy.wait()
        total = sum(dot16(chosen[slot], held[k, slot], NT) for slot in range(slots))
        packed[k * capacity : (k + 1) * capacity, :] = total
        pivot[k * cap : (k + 1) * cap, :] = total[:cap]


def pack(place, ranks, left_fac, right_fac, capacity, grid_rows):
    slots, _, order, cap = left_fac.shape
    return pl.pallas_call(
        functools.partial(pack_kernel, capacity, grid_rows),
        out_shape=(
            jax.ShapeDtypeStruct((2 * capacity, order), jnp.float32),
            jax.ShapeDtypeStruct((2 * cap, order), jnp.float32),
        ),
        in_specs=[IN_SMEM, IN_SMEM, IN_HBM, IN_HBM],
        out_specs=(IN_VMEM, IN_VMEM),
        scratch_shapes=[pltpu.VMEM((2, slots, order, cap), jnp.bfloat16), pltpu.SemaphoreType.DMA((2,))],
        compiler_params=params(16),
        cost_estimate=cost(2**10, 2**10),
        name="pack",
    )(place, ranks, left_fac, right_fac)


def pick_kernel(count, index, *refs):
    candidates, target, sem = refs[:count], refs[count], refs[count + 1]
    wait = fetch(index[0], candidates, target, sem)
    pl.when(index[0] >= 0)(wait)


def pick(index, candidates):
    return pl.pallas_call(
        functools.partial(pick_kernel, len(candidates)),
        out_shape=jax.ShapeDtypeStruct(candidates[0].shape, candidates[0].dtype),
        in_specs=[IN_SMEM] + [ANYWHERE] * len(candidates),
        out_specs=ANYWHERE,
        scratch_shapes=[pltpu.SemaphoreType.DMA],
        compiler_params=params(4),
        cost_estimate=cost(2**32, 2**20),
        name="pick",
    )(jnp.reshape(index, (1,)).astype(jnp.int32), *candidates)


def rows_kernel(capacity, grid_rows, count, place, ranks, *refs):
    sources, weights, stacked = refs[: 2 * count], refs[2 * count : 2 * count + 2], refs[2 * count + 2]
    landed, inverses, weight_high, weight_low, sems = refs[2 * count + 3 :]
    order = inverses.shape[1]
    inverses_in = fetch(1 - place[0] % 2, weights, inverses, sems.at[4])
    slots = stacked.shape[0]
    cap = LANES
    waits = []
    for t in range(2):
        for k in range(2):
            part = [source.at[pl.ds(k * capacity, capacity)] for source in sources[t * count : (t + 1) * count]]
            waits.append(fetch(place[1], part, landed.at[2 * t + k, pl.ds(0, capacity)], sems.at[2 * t + k]))
            landed[2 * t + k, capacity:, :] = jnp.zeros((cap, order), jnp.float32)
    inverses_in()
    base_parts, second_parts = split2(inverses[: 2 * order, :]), split2(inverses[2 * order :, :])
    for wait in waits:
        wait()
    solved0 = sum(dot16(landed[1].astype(jnp.bfloat16), part, NT) for part in base_parts)
    solved1 = sum(dot16(landed[3].astype(jnp.bfloat16), part, NT) for part in second_parts)
    for column, value in ((0, solved0), (2 * order, solved1)):
        high, low = split2(value)
        weight_high[:, column : column + value.shape[1]] = high
        weight_low[:, column : column + value.shape[1]] = low
    live = lax.broadcasted_iota(jnp.int32, (cap, order), 0)
    for slot in range(slots):
        pieces = []
        for t in range(2):
            start, rank = segment(ranks, t, place[0], slot, slots, grid_rows)
            spot = pl.ds(pl.multiple_of(start, 16), cap)
            left = jnp.where(live < rank, landed[2 * t, spot, :], 0.0).astype(jnp.bfloat16)
            columns = pl.ds(0, 2 * order) if t == 0 else pl.ds(2 * order, order)
            weights = jnp.concatenate([weight_high[spot, columns], weight_low[spot, columns]], axis=0)
            pieces.append(dot16(jnp.concatenate([left, left], axis=0), weights, TN))
        for column, value in ((0, pieces[0][:, :order]), (order, pieces[0][:, order:] + pieces[1])):
            high, low = split2(value)
            stacked[slot, :, column : column + order] = high
            stacked[slot, :, 2 * order + column : 2 * order + column + order] = low
            stacked[slot, :, 4 * order + column : 4 * order + column + order] = high


def row_panels(place, ranks, firsts, seconds, inverses, capacity, slots, grid_rows):
    order = inverses[0].shape[1]
    count = len(firsts)
    return pl.pallas_call(
        functools.partial(rows_kernel, capacity, grid_rows, count),
        out_shape=jax.ShapeDtypeStruct((slots, order, 6 * order), jnp.bfloat16),
        in_specs=[IN_SMEM] * 2 + [ANYWHERE] * (2 * count + 2),
        out_specs=IN_VMEM,
        scratch_shapes=[
            pltpu.VMEM((4, capacity + LANES, order), jnp.float32),
            pltpu.VMEM((3 * order, order), jnp.float32),
            pltpu.VMEM((capacity + LANES, 3 * order), jnp.bfloat16),
            pltpu.VMEM((capacity + LANES, 3 * order), jnp.bfloat16),
            pltpu.SemaphoreType.DMA((5,)),
        ],
        compiler_params=params(20),
        cost_estimate=cost(2**10, 2**10),
        name="row_panels",
    )(place, ranks, *firsts, *seconds, *inverses)


def schur_kernel(capacity, grid_rows, grid_cols, place, ranks, *refs):
    spread = grid_rows // grid_cols
    sources = refs[: 4 * spread]
    weights, (rows, left, right, out) = refs[4 * spread : 4 * spread + 2], refs[4 * spread + 2 : 4 * spread + 6]
    landed, inverses, weight0, weight1, bases, panel, sems = refs[4 * spread + 6 :]
    slots, order, cap = out.shape[0], out.shape[2], left.shape[3]
    padded = landed.shape[1]
    used = padded - LANES
    step = pl.program_id(0)
    row_here, col_here = place[0], place[1]
    mine = row_here // grid_cols

    @pl.when(step == 0)
    def _():
        inverses_in = fetch(1 - row_here % 2, weights, inverses, sems.at[4 * spread])
        passed = (row_here ^ col_here) & 1
        waits = []
        for n in range(2 * spread):
            for k in range(2):
                part = [source.at[pl.ds(k * capacity, capacity)] for source in sources[2 * n : 2 * n + 2]]
                waits.append(fetch(passed, part, landed.at[2 * n + k, pl.ds(0, capacity)], sems.at[2 * n + k]))
                if padded > capacity:
                    landed[2 * n + k, capacity:, :] = jnp.zeros((padded - capacity, order), jnp.float32)
        inverses_in()
        base_parts, second_parts = split2(inverses[: 2 * order, :]), split2(inverses[2 * order :, :])
        for wait in waits:
            wait()
        for g in range(spread):
            right0 = landed[4 * g + 1, :used, :].astype(jnp.bfloat16)
            right1 = landed[4 * g + 3, :used, :].astype(jnp.bfloat16)
            solved0 = sum(dot16(part, right0, NT) for part in base_parts)
            solved1 = sum(dot16(part, right1, NT) for part in second_parts)
            for target, at, value in (
                (weight0, 2 * g, solved0[:order]),
                (weight1, 4 * g, solved0[order:]),
                (weight1, 4 * g + 2, solved1),
            ):
                for n, piece in enumerate(split2(value)):
                    target[at + n, :, :used] = piece
                    target[at + n, :, used:] = jnp.zeros((order, padded - used), jnp.bfloat16)

    tile_col = step * grid_cols + col_here
    last_row = (slots - 1) * grid_rows + row_here

    @pl.when((tile_col > 1) & (last_row > tile_col))
    def _():
        part = step % spread
        g = part ^ mine
        group = part * grid_cols + col_here
        span = 2 * LANES
        ids = lax.broadcasted_iota(jnp.int32, (span, order), 0)
        windows = []
        for t in range(2):
            start, count = segment(ranks, t, group, step // spread, slots, grid_rows)
            first_lane = start // LANES * LANES
            window = pl.ds(pl.multiple_of(first_lane, LANES), span)
            value = landed[4 * g + 2 * t, window, :]
            live = (ids >= start - first_lane) & (ids < start - first_lane + count)
            value = jnp.where(live, value, 0.0).astype(jnp.bfloat16)
            bases[t * span : (t + 1) * span, :] = value
            windows.append(window)
        panel0 = sum(dot16(weight0[2 * g + n, :, windows[0]], bases[:span], NN) for n in range(2))
        panel1 = sum(
            dot16(weight1[4 * g + n, :, windows[n // 2]], bases[n // 2 * span : (n // 2 + 1) * span], NN)
            for n in range(4)
        )
        for at, value in ((0, panel0), (order, panel1)):
            high, low = split2(value)
            panel[at : at + order, :] = high
            panel[2 * order + at : 3 * order + at, :] = high
            panel[4 * order + at : 5 * order + at, :] = low

    for slot in range(slots):
        tile_row = slot * grid_rows + row_here
        below = tile_row > tile_col

        @pl.when(jnp.logical_not(below))
        def _():
            out[slot, 0] = jnp.zeros((order, order), jnp.float32)

        for t in range(2):

            @pl.when(below & (tile_col == t))
            def _():
                high = rows[slot, :, t * order : (t + 1) * order].astype(jnp.float32)
                low = rows[slot, :, (t + 2) * order : (t + 3) * order].astype(jnp.float32)
                out[slot, 0] = high + low

        @pl.when(below & (tile_col > 1))
        def _():
            basis = left[slot, 0].astype(jnp.float32)
            live = lax.broadcasted_iota(jnp.int32, basis.shape, 1) < ranks[tile_row, tile_col]
            front = dot16(jnp.where(live, basis, 0.0).astype(jnp.bfloat16), right[slot, 0], NT)
            out[slot, 0] = front - dot16(rows[slot], panel[...], NN)


def schur(place, ranks, col_arrays, inverses, rows, left_fac, right_fac, capacity, grid_rows, grid_cols):
    slots, steps, order, cap = left_fac.shape
    spread = grid_rows // grid_cols
    padded = (-(-capacity // LANES) + 1) * LANES
    flat = [array for pair in col_arrays for array in pair]
    factor = pl.BlockSpec((slots, 1, order, cap), lambda m: (0, m, 0, 0))
    return pl.pallas_call(
        functools.partial(schur_kernel, capacity, grid_rows, grid_cols),
        grid=(steps,),
        out_shape=pltpu.HBM((slots, steps, order, order), jnp.float32),
        in_specs=[IN_SMEM] * 2 + [ANYWHERE] * (len(flat) + 2) + [IN_VMEM, factor, factor],
        out_specs=pl.BlockSpec((slots, 1, order, order), lambda m: (0, m, 0, 0)),
        scratch_shapes=[
            pltpu.VMEM((4 * spread, padded, order), jnp.float32),
            pltpu.VMEM((3 * order, order), jnp.float32),
            pltpu.VMEM((2 * spread, order, padded), jnp.bfloat16),
            pltpu.VMEM((4 * spread, order, padded), jnp.bfloat16),
            pltpu.VMEM((4 * LANES, order), jnp.bfloat16),
            pltpu.VMEM((6 * order, order), jnp.bfloat16),
            pltpu.SemaphoreType.DMA((4 * spread + 1,)),
        ],
        compiler_params=params(40, dimension_semantics=("arbitrary",)),
        cost_estimate=cost(2**33, 2**24),
        name="schur",
    )(place, ranks, *flat, *inverses, rows, left_fac, right_fac)


def after(array, *others):
    return lax.optimization_barrier((array, *others))[0]


def device_program(capacity, early, inverses, diag_tiles, left_fac, right_fac, ranks):
    grid_rows = lax.axis_size("row")
    grid_cols = lax.axis_size("col")
    row_here = lax.axis_index("row")
    col_here = lax.axis_index("col")
    row_slots, _, order, cap = left_fac.shape
    assert cap == LANES and grid_rows % grid_cols == 0 and grid_cols >= 2
    spread = grid_rows // grid_cols
    row_bits = grid_rows.bit_length() - 1
    low_bits = grid_cols.bit_length() - 1
    assert 1 << row_bits == grid_rows and 1 << low_bits == grid_cols
    every_row = range(grid_rows)
    every_col = range(grid_cols)
    place = jnp.stack([row_here, col_here]).astype(jnp.int32)

    def move(array, pairs):
        flat = [(r * grid_cols + c, s * grid_cols + d) for (r, c), (s, d) in pairs]
        return lax.ppermute(array, AXES, flat)

    def down_column(array, root, fences):
        held = [root]
        for bit in range(1, row_bits):
            step = 1 << bit
            got = move(array, [((r, c), (r ^ step, c)) for r in held for c in every_col])
            got = after(got, fences[min(bit, len(fences)) - 1])
            mine = row_here % 2 == root
            array = pick(jnp.where(mine & (row_here >> bit == 0), 0, jnp.where(mine & (row_here >> bit == 1), 1, -1)), [array, got])
            held = held + [r ^ step for r in held]
        return array

    def to_other_parity(array, root):
        return move(array, [((r, c), (r ^ 1, c)) for r in every_row if r % 2 == root for c in every_col])

    def chain_step(array, s):
        return move(array, [((r, c - 1), (r, c)) for c in (s, s + 1) if c < grid_cols for r in every_row])

    factoring = inverses is None
    if factoring:
        inverse0 = first_inverse(place, diag_tiles)
        passed = move(inverse0, [((0, c), (1, c)) for c in every_col])
    packed, pivot_bases = pack(after(place, inverse0) if factoring else place, ranks, left_fac, right_fac, capacity, grid_rows)
    back = move(packed, [((r, 1), (r, 0)) for r in every_row])
    chain = [packed]
    if factoring:
        received = [move(pivot_bases, [((1, 0), (1, c))]) for c in every_col if c]
        pivot_bases = jnp.where(col_here == 0, pivot_bases, sum(received))
        chain.append(chain_step(after(packed, passed, pivot_bases), 1))
        weights = second_inverse(place, ranks, diag_tiles, pivot_bases, passed)
        chain[1], weights = lax.optimization_barrier((chain[1], weights))
    else:
        chain.append(chain_step(packed, 1))

    for s in range(2, grid_cols):
        chain.append(chain_step(chain[s - 1], s))
    firsts = list(chain)
    seconds = [back] + chain[:-1]
    offset = (row_here ^ col_here) & (grid_cols - 1)

    def source(candidates):
        return pick(jnp.where(offset == 0, col_here, -1), candidates)

    second_source = source(seconds)

    def hop(array, bit, held):
        step = 1 << bit
        return move(
            array,
            [
                ((r + h * grid_cols, c), ((r + h * grid_cols) ^ step, c))
                for c in every_col
                for r in held[c]
                for h in range(spread)
            ],
        )

    def low_hops(have, *fence):
        held = {c: [c] for c in every_col}
        for bit in range(1, low_bits):
            got = hop(have, bit, held)
            got = after(got, *fence) if fence else got
            arrived = (offset >> bit == 1) & (offset & 1 == 0)
            stays = (offset >> bit == 0) & (offset & 1 == 0)
            have = pick(jnp.where(arrived, 1, jnp.where(stays, 0, -1)), [have, got])
            held = {c: held[c] + [r ^ (1 << bit) for r in held[c]] for c in every_col}
        return have

    def high_hops(have, *fence):
        held = {c: [r for r in range(grid_cols) if (r ^ c) % 2 == 0] for c in every_col}
        sets = [have]
        for bit in range(low_bits, row_bits):
            sets = sets + [hop(array, bit, held) for array in sets]
        sets = [after(array, *fence) if fence else array for array in sets]
        return [[array, hop(array, 0, held)] for array in sets]

    first_source = source(firsts)
    second_have = low_hops(second_source, first_source)
    if factoring:
        weights = down_column(weights, 1, [chain[min(2, grid_cols - 1)], second_have])
        inverses = [weights, to_other_parity(weights, 1)]
    rows = row_panels(place, ranks, firsts, seconds, inverses, capacity, row_slots, grid_rows)
    first_have = low_hops(first_source, rows)
    second_sets, first_sets = high_hops(second_have, early), high_hops(first_have)
    col_arrays = [sets[g] for g in range(spread) for sets in (first_sets, second_sets)]
    return schur(place, ranks, col_arrays, inverses, rows, left_fac, right_fac, capacity, grid_rows, grid_cols), inverses


def shards(diag_tiles, left_fac, right_fac, ranks):
    row_slots, cap = left_fac.shape[0], left_fac.shape[3]
    grid_rows = lax.axis_size("row")
    full = row_slots * cap
    packed = max(cap, full * 5 // 8)
    args = (diag_tiles, left_fac, right_fac, ranks)
    tile_ids = jnp.arange(ranks.shape[0], dtype=jnp.int32)[:, None]
    live = jnp.where(tile_ids > jnp.arange(2, dtype=jnp.int32)[None, :], ranks[:, :2], 0)
    widest = jnp.max(sum(live[s * grid_rows : (s + 1) * grid_rows] for s in range(row_slots)))
    result, inverses = device_program(packed, widest, None, *args)
    if packed == full:
        return result

    def again(state):
        return jnp.zeros_like(state[0]), device_program(full, state[0], inverses, *args)[0]

    return lax.while_loop(lambda state: state[0] > packed, again, (widest, result))[1]


def solution(mesh):
    in_specs = (P("row", None, None), P("row", "col", None, None), P("row", "col", None, None), P())
    out_specs = P("row", "col", None, None)
    return jax.shard_map(shards, mesh=mesh, in_specs=in_specs, out_specs=out_specs, check_vma=False)
```

```python
import functools

import jax
import jax.numpy as jnp
from jax import lax
from jax.experimental import pallas as pl
from jax.experimental.pallas import tpu as pltpu
from jax.sharding import PartitionSpec as P

PRECISE = lax.Precision.HIGHEST
AXES = ("row", "col")
BLOCK = 32
GROUP = 8
LANES = 128
NT = (((1,), (1,)), ((), ()))
TN = (((0,), (0,)), ((), ()))
NN = (((1,), (0,)), ((), ()))
ANYWHERE = pl.BlockSpec(memory_space=pl.ANY)
IN_VMEM = pl.BlockSpec(memory_space=pltpu.VMEM)
IN_SMEM = pl.BlockSpec(memory_space=pltpu.SMEM)
IN_HBM = pl.BlockSpec(memory_space=pltpu.HBM)
MEBI = 1024 * 1024


def dot32(lhs, rhs, dims):
    return lax.dot_general(lhs, rhs, dims, precision=PRECISE, preferred_element_type=jnp.float32)


def dot16(lhs, rhs, dims):
    return lax.dot_general(lhs, rhs, dims, preferred_element_type=jnp.float32)


def split2(value):
    high = value.astype(jnp.bfloat16)
    low = (value - high.astype(jnp.float32)).astype(jnp.bfloat16)
    return high, low


def params(mebibytes, **extra):
    return pltpu.CompilerParams(vmem_limit_bytes=mebibytes * MEBI, **extra)


def cost(flops, moved):
    return pl.CostEstimate(flops=int(flops), bytes_accessed=int(moved), transcendentals=0)


def eliminate(tiles):
    tiles, start = tiles
    rows = tiles[0].shape[0]
    done = []
    for first in range(0, rows, GROUP):
        height = rows - first
        row_ids = lax.broadcasted_iota(jnp.int32, (height, LANES), 0)
        heads = [
            jnp.broadcast_to(tiles[0][:, start + first + j : start + first + j + 1], (height, LANES))
            for j in range(GROUP)
        ]
        scale = jnp.zeros((GROUP, LANES), jnp.float32)
        for j in range(GROUP):
            pivot = heads[j][j : j + 1, :]
            factor = jnp.where(row_ids > j, heads[j] * (1.0 / pivot), 0.0)
            for other in range(j + 1, GROUP):
                heads[other] = heads[other] - factor * heads[other][j : j + 1, :]
            tiles = [tile - factor * tile[j : j + 1, :] for tile in tiles]
            root = lax.rsqrt(pivot)
            root = root * (1.5 - 0.5 * pivot * root * root)
            scale = jnp.where(row_ids[:GROUP] == j, root, scale)
        done.append([tile[:GROUP] * scale for tile in tiles])
        tiles = [tile[GROUP:] for tile in tiles]
    return [jnp.concatenate(parts, axis=0) for parts in zip(*done)]


def inverse_factor(source, work, result):
    order = source.shape[0]
    span = order // LANES
    for base in range(0, order, BLOCK):
        low = base // LANES
        row_ids = lax.broadcasted_iota(jnp.int32, (BLOCK, LANES), 0)
        lane_ids = lax.broadcasted_iota(jnp.int32, (BLOCK, LANES), 1)
        unit = jnp.where(lane_ids - base % LANES == row_ids, 1.0, 0.0)
        zero = jnp.zeros((BLOCK, LANES), jnp.float32)
        tiles = [source[base : base + BLOCK, s * LANES : (s + 1) * LANES] for s in range(low, span)]
        tiles += [zero] * low + [unit]
        if base:
            taken = dot32(
                work[0:base, base : base + BLOCK],
                work[0:base, low * LANES : order + (low + 1) * LANES],
                TN,
            )
            tiles = [tile - taken[:, s * LANES : (s + 1) * LANES] for s, tile in enumerate(tiles)]
        tiles = eliminate((tiles, base % LANES))
        for s, tile in enumerate(tiles):
            work[base : base + BLOCK, (low + s) * LANES : (low + s + 1) * LANES] = tile
        for s in range(low + 1, span):
            work[base : base + BLOCK, order + s * LANES : order + (s + 1) * LANES] = zero
    result[...] = work[:, order:]


def fetch(choice, candidates, target, sem):
    for n, candidate in enumerate(candidates):
        copy = pltpu.make_async_copy(candidate, target, sem)
        pl.when(choice == n)(copy.start)
    return pltpu.make_async_copy(candidates[0], target, sem).wait


def first_kernel(place, tiles, result, tile, work, sem):
    @pl.when(place[0] == 0)
    def _():
        copy = pltpu.make_async_copy(tiles.at[0], tile, sem)
        copy.start()
        copy.wait()
        inverse_factor(tile, work, result)


def first_inverse(place, tiles):
    order = tiles.shape[2]
    return pl.pallas_call(
        first_kernel,
        out_shape=jax.ShapeDtypeStruct((order, order), jnp.float32),
        in_specs=[IN_SMEM, IN_HBM],
        out_specs=IN_VMEM,
        scratch_shapes=[
            pltpu.VMEM((order, order), jnp.float32),
            pltpu.VMEM((order, 2 * order), jnp.float32),
            pltpu.SemaphoreType.DMA,
        ],
        compiler_params=params(8),
        cost_estimate=cost(2**33, 2**20),
        name="first_inverse",
    )(place, tiles)


def second_kernel(place, ranks, tiles, bases, inverse, weights, shifted, work, sem):
    order = inverse.shape[0]
    cap = bases.shape[0] // 2

    @pl.when(place[0] == 1)
    def _():
        copy = pltpu.make_async_copy(tiles.at[0], shifted, sem)
        copy.start()
        weights[:order, :] = inverse[...]
        live = lax.broadcasted_iota(jnp.int32, (cap, order), 0) < ranks[1, 0]
        left = jnp.where(live, bases[:cap, :], 0.0)
        right = jnp.where(live, bases[cap:, :], 0.0)
        solved = dot32(right, inverse[...], NT)
        dense = dot32(left, solved, TN)
        copy.wait()
        shifted[...] = shifted[...] - dot32(dense, dense, NT)
        inverse_factor(shifted, work, weights.at[pl.ds(2 * order, order)])
        weights[order : 2 * order, :] = -dot32(dot32(weights[2 * order :, :], dense, NN), inverse[...], NN)


def second_inverse(place, ranks, tiles, bases, inverse):
    order = inverse.shape[0]
    return pl.pallas_call(
        second_kernel,
        out_shape=jax.ShapeDtypeStruct((3 * order, order), jnp.float32),
        in_specs=[IN_SMEM, IN_SMEM, IN_HBM, IN_VMEM, IN_VMEM],
        out_specs=IN_VMEM,
        scratch_shapes=[
            pltpu.VMEM((order, order), jnp.float32),
            pltpu.VMEM((order, 2 * order), jnp.float32),
            pltpu.SemaphoreType.DMA,
        ],
        compiler_params=params(8),
        cost_estimate=cost(2**10, 2**10),
        name="second_inverse",
    )(place, ranks, tiles, bases, inverse)


def segment(ranks, panel, group, slot, slots, grid_rows):
    start, count = jnp.int32(0), jnp.int32(0)
    for s in range(slots):
        tile_row = s * grid_rows + group
        rank = jnp.where(tile_row > panel, ranks[tile_row, panel], 0)
        start = start + jnp.where(s < slot, rank, 0)
        count = count + jnp.where(s == slot, rank, 0)
    return start, count


def pack_kernel(capacity, grid_rows, place, ranks, left, right, packed, pivot, held, sem):
    slots, order, cap = held.shape[1:]
    copies = [
        pltpu.make_async_copy(source.at[:, 0], held.at[k], sem.at[k]) for k, source in enumerate((left, right))
    ]
    for copy in copies:
        copy.start()
    panel = jnp.minimum(place[1], 1)
    spot = lax.broadcasted_iota(jnp.int32, (capacity, cap), 0)
    column = lax.broadcasted_iota(jnp.int32, (capacity, cap), 1)
    chosen = []
    for slot in range(slots):
        start, count = segment(ranks, panel, place[0], slot, slots, grid_rows)
        hit = (spot - start == column) & (column < count)
        chosen.append(jnp.where(hit, 1.0, 0.0).astype(jnp.bfloat16))
    for k, copy in enumerate(copies):
        copy.wait()
        total = sum(dot16(chosen[slot], held[k, slot], NT) for slot in range(slots))
        packed[k * capacity : (k + 1) * capacity, :] = total
        pivot[k * cap : (k + 1) * cap, :] = total[:cap]


def pack(place, ranks, left_fac, right_fac, capacity, grid_rows):
    slots, _, order, cap = left_fac.shape
    return pl.pallas_call(
        functools.partial(pack_kernel, capacity, grid_rows),
        out_shape=(
            jax.ShapeDtypeStruct((2 * capacity, order), jnp.float32),
            jax.ShapeDtypeStruct((2 * cap, order), jnp.float32),
        ),
        in_specs=[IN_SMEM, IN_SMEM, IN_HBM, IN_HBM],
        out_specs=(IN_VMEM, IN_VMEM),
        scratch_shapes=[pltpu.VMEM((2, slots, order, cap), jnp.bfloat16), pltpu.SemaphoreType.DMA((2,))],
        compiler_params=params(16),
        cost_estimate=cost(2**10, 2**10),
        name="pack",
    )(place, ranks, left_fac, right_fac)


def pick_kernel(count, index, *refs):
    candidates, target, sem = refs[:count], refs[count], refs[count + 1]
    wait = fetch(index[0], candidates, target, sem)
    pl.when(index[0] >= 0)(wait)


def pick(index, candidates):
    return pl.pallas_call(
        functools.partial(pick_kernel, len(candidates)),
        out_shape=jax.ShapeDtypeStruct(candidates[0].shape, candidates[0].dtype),
        in_specs=[IN_SMEM] + [ANYWHERE] * len(candidates),
        out_specs=ANYWHERE,
        scratch_shapes=[pltpu.SemaphoreType.DMA],
        compiler_params=params(4),
        cost_estimate=cost(2**32, 2**20),
        name="pick",
    )(jnp.reshape(index, (1,)).astype(jnp.int32), *candidates)


def rows_kernel(capacity, grid_rows, count, place, ranks, *refs):
    sources, weights, stacked = refs[: 2 * count], refs[2 * count : 2 * count + 2], refs[2 * count + 2]
    landed, inverses, weight_high, weight_low, sems = refs[2 * count + 3 :]
    order = inverses.shape[1]
    inverses_in = fetch(1 - place[0] % 2, weights, inverses, sems.at[4])
    slots = stacked.shape[0]
    cap = LANES
    waits = []
    for t in range(2):
        for k in range(2):
            part = [source.at[pl.ds(k * capacity, capacity)] for source in sources[t * count : (t + 1) * count]]
            waits.append(fetch(place[1], part, landed.at[2 * t + k, pl.ds(0, capacity)], sems.at[2 * t + k]))
            landed[2 * t + k, capacity:, :] = jnp.zeros((cap, order), jnp.float32)
    inverses_in()
    base_parts, second_parts = split2(inverses[: 2 * order, :]), split2(inverses[2 * order :, :])
    for wait in waits:
        wait()
    solved0 = sum(dot16(landed[1].astype(jnp.bfloat16), part, NT) for part in base_parts)
    solved1 = sum(dot16(landed[3].astype(jnp.bfloat16), part, NT) for part in second_parts)
    for column, value in ((0, solved0), (2 * order, solved1)):
        high, low = split2(value)
        weight_high[:, column : column + value.shape[1]] = high
        weight_low[:, column : column + value.shape[1]] = low
    live = lax.broadcasted_iota(jnp.int32, (cap, order), 0)
    for slot in range(slots):
        pieces = []
        for t in range(2):
            start, rank = segment(ranks, t, place[0], slot, slots, grid_rows)
            spot = pl.ds(pl.multiple_of(start, 16), cap)
            left = jnp.where(live < rank, landed[2 * t, spot, :], 0.0).astype(jnp.bfloat16)
            columns = pl.ds(0, 2 * order) if t == 0 else pl.ds(2 * order, order)
            weights = jnp.concatenate([weight_high[spot, columns], weight_low[spot, columns]], axis=0)
            pieces.append(dot16(jnp.concatenate([left, left], axis=0), weights, TN))
        for column, value in ((0, pieces[0][:, :order]), (order, pieces[0][:, order:] + pieces[1])):
            high, low = split2(value)
            stacked[slot, :, column : column + order] = high
            stacked[slot, :, 2 * order + column : 2 * order + column + order] = low
            stacked[slot, :, 4 * order + column : 4 * order + column + order] = high


def row_panels(place, ranks, firsts, seconds, inverses, capacity, slots, grid_rows):
    order = inverses[0].shape[1]
    count = len(firsts)
    return pl.pallas_call(
        functools.partial(rows_kernel, capacity, grid_rows, count),
        out_shape=jax.ShapeDtypeStruct((slots, order, 6 * order), jnp.bfloat16),
        in_specs=[IN_SMEM] * 2 + [ANYWHERE] * (2 * count + 2),
        out_specs=IN_VMEM,
        scratch_shapes=[
            pltpu.VMEM((4, capacity + LANES, order), jnp.float32),
            pltpu.VMEM((3 * order, order), jnp.float32),
            pltpu.VMEM((capacity + LANES, 3 * order), jnp.bfloat16),
            pltpu.VMEM((capacity + LANES, 3 * order), jnp.bfloat16),
            pltpu.SemaphoreType.DMA((5,)),
        ],
        compiler_params=params(20),
        cost_estimate=cost(2**10, 2**10),
        name="row_panels",
    )(place, ranks, *firsts, *seconds, *inverses)


def schur_kernel(capacity, grid_rows, grid_cols, place, ranks, *refs):
    spread = grid_rows // grid_cols
    sources = refs[: 4 * spread]
    weights, (rows, left, right, out) = refs[4 * spread : 4 * spread + 2], refs[4 * spread + 2 : 4 * spread + 6]
    landed, inverses, weight0, weight1, bases, panel, sems = refs[4 * spread + 6 :]
    slots, order, cap = out.shape[0], out.shape[2], left.shape[3]
    padded = landed.shape[1]
    used = padded - LANES
    step = pl.program_id(0)
    row_here, col_here = place[0], place[1]
    mine = row_here // grid_cols

    @pl.when(step == 0)
    def _():
        inverses_in = fetch(1 - row_here % 2, weights, inverses, sems.at[4 * spread])
        passed = (row_here ^ col_here) & 1
        waits = []
        for n in range(2 * spread):
            for k in range(2):
                part = [source.at[pl.ds(k * capacity, capacity)] for source in sources[2 * n : 2 * n + 2]]
                waits.append(fetch(passed, part, landed.at[2 * n + k, pl.ds(0, capacity)], sems.at[2 * n + k]))
                if padded > capacity:
                    landed[2 * n + k, capacity:, :] = jnp.zeros((padded - capacity, order), jnp.float32)
        inverses_in()
        base_parts, second_parts = split2(inverses[: 2 * order, :]), split2(inverses[2 * order :, :])
        for wait in waits:
            wait()
        for g in range(spread):
            right0 = landed[4 * g + 1, :used, :].astype(jnp.bfloat16)
            right1 = landed[4 * g + 3, :used, :].astype(jnp.bfloat16)
            solved0 = sum(dot16(part, right0, NT) for part in base_parts)
            solved1 = sum(dot16(part, right1, NT) for part in second_parts)
            for target, at, value in (
                (weight0, 2 * g, solved0[:order]),
                (weight1, 4 * g, solved0[order:]),
                (weight1, 4 * g + 2, solved1),
            ):
                for n, piece in enumerate(split2(value)):
                    target[at + n, :, :used] = piece
                    target[at + n, :, used:] = jnp.zeros((order, padded - used), jnp.bfloat16)

    tile_col = step * grid_cols + col_here
    last_row = (slots - 1) * grid_rows + row_here

    @pl.when((tile_col > 1) & (last_row > tile_col))
    def _():
        part = step % spread
        g = part ^ mine
        group = part * grid_cols + col_here
        span = 2 * LANES
        ids = lax.broadcasted_iota(jnp.int32, (span, order), 0)
        windows = []
        for t in range(2):
            start, count = segment(ranks, t, group, step // spread, slots, grid_rows)
            first_lane = start // LANES * LANES
            window = pl.ds(pl.multiple_of(first_lane, LANES), span)
            value = landed[4 * g + 2 * t, window, :]
            live = (ids >= start - first_lane) & (ids < start - first_lane + count)
            value = jnp.where(live, value, 0.0).astype(jnp.bfloat16)
            bases[t * span : (t + 1) * span, :] = value
            windows.append(window)
        panel0 = sum(dot16(weight0[2 * g + n, :, windows[0]], bases[:span], NN) for n in range(2))
        panel1 = sum(
            dot16(weight1[4 * g + n, :, windows[n // 2]], bases[n // 2 * span : (n // 2 + 1) * span], NN)
            for n in range(4)
        )
        for at, value in ((0, panel0), (order, panel1)):
            high, low = split2(value)
            panel[at : at + order, :] = high
            panel[2 * order + at : 3 * order + at, :] = high
            panel[4 * order + at : 5 * order + at, :] = low

    for slot in range(slots):
        tile_row = slot * grid_rows + row_here
        below = tile_row > tile_col

        @pl.when(jnp.logical_not(below))
        def _():
            out[slot, 0] = jnp.zeros((order, order), jnp.float32)

        for t in range(2):

            @pl.when(below & (tile_col == t))
            def _():
                high = rows[slot, :, t * order : (t + 1) * order].astype(jnp.float32)
                low = rows[slot, :, (t + 2) * order : (t + 3) * order].astype(jnp.float32)
                out[slot, 0] = high + low

        @pl.when(below & (tile_col > 1))
        def _():
            basis = left[slot, 0].astype(jnp.float32)
            live = lax.broadcasted_iota(jnp.int32, basis.shape, 1) < ranks[tile_row, tile_col]
            front = dot16(jnp.where(live, basis, 0.0).astype(jnp.bfloat16), right[slot, 0], NT)
            out[slot, 0] = front - dot16(rows[slot], panel[...], NN)


def schur(place, ranks, col_arrays, inverses, rows, left_fac, right_fac, capacity, grid_rows, grid_cols):
    slots, steps, order, cap = left_fac.shape
    spread = grid_rows // grid_cols
    padded = (-(-capacity // LANES) + 1) * LANES
    flat = [array for pair in col_arrays for array in pair]
    factor = pl.BlockSpec((slots, 1, order, cap), lambda m: (0, m, 0, 0))
    return pl.pallas_call(
        functools.partial(schur_kernel, capacity, grid_rows, grid_cols),
        grid=(steps,),
        out_shape=pltpu.HBM((slots, steps, order, order), jnp.float32),
        in_specs=[IN_SMEM] * 2 + [ANYWHERE] * (len(flat) + 2) + [IN_VMEM, factor, factor],
        out_specs=pl.BlockSpec((slots, 1, order, order), lambda m: (0, m, 0, 0)),
        scratch_shapes=[
            pltpu.VMEM((4 * spread, padded, order), jnp.float32),
            pltpu.VMEM((3 * order, order), jnp.float32),
            pltpu.VMEM((2 * spread, order, padded), jnp.bfloat16),
            pltpu.VMEM((4 * spread, order, padded), jnp.bfloat16),
            pltpu.VMEM((4 * LANES, order), jnp.bfloat16),
            pltpu.VMEM((6 * order, order), jnp.bfloat16),
            pltpu.SemaphoreType.DMA((4 * spread + 1,)),
        ],
        compiler_params=params(40, dimension_semantics=("arbitrary",)),
        cost_estimate=cost(2**33, 2**24),
        name="schur",
    )(place, ranks, *flat, *inverses, rows, left_fac, right_fac)


def after(array, *others):
    return lax.optimization_barrier((array, *others))[0]


def device_program(capacity, early, inverses, diag_tiles, left_fac, right_fac, ranks):
    grid_rows = lax.axis_size("row")
    grid_cols = lax.axis_size("col")
    row_here = lax.axis_index("row")
    col_here = lax.axis_index("col")
    row_slots, _, order, cap = left_fac.shape
    assert cap == LANES and grid_rows % grid_cols == 0 and grid_cols >= 2
    spread = grid_rows // grid_cols
    row_bits = grid_rows.bit_length() - 1
    low_bits = grid_cols.bit_length() - 1
    assert 1 << row_bits == grid_rows and 1 << low_bits == grid_cols
    every_row = range(grid_rows)
    every_col = range(grid_cols)
    place = jnp.stack([row_here, col_here]).astype(jnp.int32)

    def move(array, pairs):
        flat = [(r * grid_cols + c, s * grid_cols + d) for (r, c), (s, d) in pairs]
        return lax.ppermute(array, AXES, flat)

    def down_column(array, root, fences):
        held = [root]
        for bit in range(1, row_bits):
            step = 1 << bit
            got = move(array, [((r, c), (r ^ step, c)) for r in held for c in every_col])
            got = after(got, fences[min(bit, len(fences)) - 1])
            mine = row_here % 2 == root
            array = pick(jnp.where(mine & (row_here >> bit == 0), 0, jnp.where(mine & (row_here >> bit == 1), 1, -1)), [array, got])
            held = held + [r ^ step for r in held]
        return array

    def to_other_parity(array, root):
        return move(array, [((r, c), (r ^ 1, c)) for r in every_row if r % 2 == root for c in every_col])

    def chain_step(array, s):
        return move(array, [((r, c - 1), (r, c)) for c in (s, s + 1) if c < grid_cols for r in every_row])

    factoring = inverses is None
    if factoring:
        inverse0 = first_inverse(place, diag_tiles)
        passed = move(inverse0, [((0, c), (1, c)) for c in every_col])
    packed, pivot_bases = pack(place, ranks, left_fac, right_fac, capacity, grid_rows)
    back = move(packed, [((r, 1), (r, 0)) for r in every_row])
    chain = [packed]
    if factoring:
        received = [move(pivot_bases, [((1, 0), (1, c))]) for c in every_col if c]
        pivot_bases = jnp.where(col_here == 0, pivot_bases, sum(received))
        chain.append(chain_step(packed, 1))
        weights = second_inverse(place, ranks, diag_tiles, pivot_bases, passed)
        chain[1], weights = lax.optimization_barrier((chain[1], weights))
    else:
        chain.append(chain_step(packed, 1))

    for s in range(2, grid_cols):
        chain.append(chain_step(chain[s - 1], s))
    firsts = list(chain)
    seconds = [back] + chain[:-1]
    offset = (row_here ^ col_here) & (grid_cols - 1)

    def source(candidates):
        return pick(jnp.where(offset == 0, col_here, -1), candidates)

    second_source = source(seconds)

    def hop(array, bit, held):
        step = 1 << bit
        return move(
            array,
            [
                ((r + h * grid_cols, c), ((r + h * grid_cols) ^ step, c))
                for c in every_col
                for r in held[c]
                for h in range(spread)
            ],
        )

    def low_hops(have, *fence):
        held = {c: [c] for c in every_col}
        for bit in range(1, low_bits):
            got = hop(have, bit, held)
            got = after(got, *fence) if fence else got
            arrived = (offset >> bit == 1) & (offset & 1 == 0)
            stays = (offset >> bit == 0) & (offset & 1 == 0)
            have = pick(jnp.where(arrived, 1, jnp.where(stays, 0, -1)), [have, got])
            held = {c: held[c] + [r ^ (1 << bit) for r in held[c]] for c in every_col}
        return have

    def high_hops(have, *fence):
        held = {c: [r for r in range(grid_cols) if (r ^ c) % 2 == 0] for c in every_col}
        sets = [have]
        for bit in range(low_bits, row_bits):
            sets = sets + [hop(array, bit, held) for array in sets]
        sets = [after(array, *fence) if fence else array for array in sets]
        return [[array, hop(array, 0, held)] for array in sets]

    first_source = source(firsts)
    second_have = low_hops(second_source, first_source)
    if factoring:
        weights = down_column(weights, 1, [chain[min(2, grid_cols - 1)], second_have])
        inverses = [weights, to_other_parity(weights, 1)]
    rows = row_panels(place, ranks, firsts, seconds, inverses, capacity, row_slots, grid_rows)
    first_have = low_hops(first_source, rows)
    second_sets, first_sets = high_hops(second_have, early), high_hops(first_have)
    col_arrays = [sets[g] for g in range(spread) for sets in (first_sets, second_sets)]
    return schur(place, ranks, col_arrays, inverses, rows, left_fac, right_fac, capacity, grid_rows, grid_cols), inverses


def shards(diag_tiles, left_fac, right_fac, ranks):
    row_slots, cap = left_fac.shape[0], left_fac.shape[3]
    grid_rows = lax.axis_size("row")
    full = row_slots * cap
    packed = max(cap, full * 5 // 8)
    args = (diag_tiles, left_fac, right_fac, ranks)
    tile_ids = jnp.arange(ranks.shape[0], dtype=jnp.int32)[:, None]
    live = jnp.where(tile_ids > jnp.arange(2, dtype=jnp.int32)[None, :], ranks[:, :2], 0)
    widest = jnp.max(sum(live[s * grid_rows : (s + 1) * grid_rows] for s in range(row_slots)))
    result, inverses = device_program(packed, widest, None, *args)
    if packed == full:
        return result

    def again(state):
        return jnp.zeros_like(state[0]), device_program(full, state[0], inverses, *args)[0]

    return lax.while_loop(lambda state: state[0] > packed, again, (widest, result))[1]


def solution(mesh):
    in_specs = (P("row", None, None), P("row", "col", None, None), P("row", "col", None, None), P())
    out_specs = P("row", "col", None, None)
    return jax.shard_map(shards, mesh=mesh, in_specs=in_specs, out_specs=out_specs, check_vma=False)
```

```python
import functools

import jax
import jax.numpy as jnp
from jax import lax
from jax.experimental import pallas as pl
from jax.experimental.pallas import tpu as pltpu
from jax.sharding import PartitionSpec as P

PRECISE = lax.Precision.HIGHEST
AXES = ("row", "col")
BLOCK = 32
GROUP = 8
LANES = 128
NT = (((1,), (1,)), ((), ()))
TN = (((0,), (0,)), ((), ()))
NN = (((1,), (0,)), ((), ()))
ANYWHERE = pl.BlockSpec(memory_space=pl.ANY)
IN_VMEM = pl.BlockSpec(memory_space=pltpu.VMEM)
IN_SMEM = pl.BlockSpec(memory_space=pltpu.SMEM)
IN_HBM = pl.BlockSpec(memory_space=pltpu.HBM)
MEBI = 1024 * 1024


def dot32(lhs, rhs, dims):
    return lax.dot_general(lhs, rhs, dims, precision=PRECISE, preferred_element_type=jnp.float32)


def dot16(lhs, rhs, dims):
    return lax.dot_general(lhs, rhs, dims, preferred_element_type=jnp.float32)


def split2(value):
    high = value.astype(jnp.bfloat16)
    low = (value - high.astype(jnp.float32)).astype(jnp.bfloat16)
    return high, low


def params(mebibytes, **extra):
    return pltpu.CompilerParams(vmem_limit_bytes=mebibytes * MEBI, **extra)


def cost(flops, moved):
    return pl.CostEstimate(flops=int(flops), bytes_accessed=int(moved), transcendentals=0)


def eliminate(tiles):
    tiles, start = tiles
    rows = tiles[0].shape[0]
    done = []
    for first in range(0, rows, GROUP):
        height = rows - first
        row_ids = lax.broadcasted_iota(jnp.int32, (height, LANES), 0)
        heads = [
            jnp.broadcast_to(tiles[0][:, start + first + j : start + first + j + 1], (height, LANES))
            for j in range(GROUP)
        ]
        scale = jnp.zeros((GROUP, LANES), jnp.float32)
        for j in range(GROUP):
            pivot = heads[j][j : j + 1, :]
            factor = jnp.where(row_ids > j, heads[j] * (1.0 / pivot), 0.0)
            for other in range(j + 1, GROUP):
                heads[other] = heads[other] - factor * heads[other][j : j + 1, :]
            tiles = [tile - factor * tile[j : j + 1, :] for tile in tiles]
            root = lax.rsqrt(pivot)
            root = root * (1.5 - 0.5 * pivot * root * root)
            scale = jnp.where(row_ids[:GROUP] == j, root, scale)
        done.append([tile[:GROUP] * scale for tile in tiles])
        tiles = [tile[GROUP:] for tile in tiles]
    return [jnp.concatenate(parts, axis=0) for parts in zip(*done)]


def inverse_factor(source, work, result):
    order = source.shape[0]
    span = order // LANES
    for base in range(0, order, BLOCK):
        low = base // LANES
        row_ids = lax.broadcasted_iota(jnp.int32, (BLOCK, LANES), 0)
        lane_ids = lax.broadcasted_iota(jnp.int32, (BLOCK, LANES), 1)
        unit = jnp.where(lane_ids - base % LANES == row_ids, 1.0, 0.0)
        zero = jnp.zeros((BLOCK, LANES), jnp.float32)
        tiles = [source[base : base + BLOCK, s * LANES : (s + 1) * LANES] for s in range(low, span)]
        tiles += [zero] * low + [unit]
        if base:
            taken = dot32(
                work[0:base, base : base + BLOCK],
                work[0:base, low * LANES : order + (low + 1) * LANES],
                TN,
            )
            tiles = [tile - taken[:, s * LANES : (s + 1) * LANES] for s, tile in enumerate(tiles)]
        tiles = eliminate((tiles, base % LANES))
        for s, tile in enumerate(tiles):
            work[base : base + BLOCK, (low + s) * LANES : (low + s + 1) * LANES] = tile
        for s in range(low + 1, span):
            work[base : base + BLOCK, order + s * LANES : order + (s + 1) * LANES] = zero
    result[...] = work[:, order:]


def fetch(choice, candidates, target, sem):
    for n, candidate in enumerate(candidates):
        copy = pltpu.make_async_copy(candidate, target, sem)
        pl.when(choice == n)(copy.start)
    return pltpu.make_async_copy(candidates[0], target, sem).wait


def first_kernel(place, tiles, result, tile, work, sem):
    @pl.when(place[0] == 0)
    def _():
        copy = pltpu.make_async_copy(tiles.at[0], tile, sem)
        copy.start()
        copy.wait()
        inverse_factor(tile, work, result)


def first_inverse(place, tiles):
    order = tiles.shape[2]
    return pl.pallas_call(
        first_kernel,
        out_shape=jax.ShapeDtypeStruct((order, order), jnp.float32),
        in_specs=[IN_SMEM, IN_HBM],
        out_specs=IN_VMEM,
        scratch_shapes=[
            pltpu.VMEM((order, order), jnp.float32),
            pltpu.VMEM((order, 2 * order), jnp.float32),
            pltpu.SemaphoreType.DMA,
        ],
        compiler_params=params(8),
        cost_estimate=cost(2**33, 2**20),
        name="first_inverse",
    )(place, tiles)


def second_kernel(place, ranks, tiles, bases, inverse, weights, shifted, work, sem):
    order = inverse.shape[0]
    cap = bases.shape[0] // 2

    @pl.when(place[0] == 1)
    def _():
        copy = pltpu.make_async_copy(tiles.at[0], shifted, sem)
        copy.start()
        weights[:order, :] = inverse[...]
        live = lax.broadcasted_iota(jnp.int32, (cap, order), 0) < ranks[1, 0]
        left = jnp.where(live, bases[:cap, :], 0.0)
        right = jnp.where(live, bases[cap:, :], 0.0)
        solved = dot32(right, inverse[...], NT)
        dense = dot32(left, solved, TN)
        copy.wait()
        shifted[...] = shifted[...] - dot32(dense, dense, NT)
        inverse_factor(shifted, work, weights.at[pl.ds(2 * order, order)])
        weights[order : 2 * order, :] = -dot32(dot32(weights[2 * order :, :], dense, NN), inverse[...], NN)


def second_inverse(place, ranks, tiles, bases, inverse):
    order = inverse.shape[0]
    return pl.pallas_call(
        second_kernel,
        out_shape=jax.ShapeDtypeStruct((3 * order, order), jnp.float32),
        in_specs=[IN_SMEM, IN_SMEM, IN_HBM, IN_VMEM, IN_VMEM],
        out_specs=IN_VMEM,
        scratch_shapes=[
            pltpu.VMEM((order, order), jnp.float32),
            pltpu.VMEM((order, 2 * order), jnp.float32),
            pltpu.SemaphoreType.DMA,
        ],
        compiler_params=params(8),
        cost_estimate=cost(2**10, 2**10),
        name="second_inverse",
    )(place, ranks, tiles, bases, inverse)


def segment(ranks, panel, group, slot, slots, grid_rows):
    start, count = jnp.int32(0), jnp.int32(0)
    for s in range(slots):
        tile_row = s * grid_rows + group
        rank = jnp.where(tile_row > panel, ranks[tile_row, panel], 0)
        start = start + jnp.where(s < slot, rank, 0)
        count = count + jnp.where(s == slot, rank, 0)
    return start, count


def pack_kernel(capacity, grid_rows, place, ranks, left, right, packed, pivot, held, sem):
    slots, order, cap = held.shape[1:]
    copies = [
        pltpu.make_async_copy(source.at[:, 0], held.at[k], sem.at[k]) for k, source in enumerate((left, right))
    ]
    for copy in copies:
        copy.start()
    panel = jnp.minimum(place[1], 1)
    spot = lax.broadcasted_iota(jnp.int32, (capacity, cap), 0)
    column = lax.broadcasted_iota(jnp.int32, (capacity, cap), 1)
    chosen = []
    for slot in range(slots):
        start, count = segment(ranks, panel, place[0], slot, slots, grid_rows)
        hit = (spot - start == column) & (column < count)
        chosen.append(jnp.where(hit, 1.0, 0.0).astype(jnp.bfloat16))
    for k, copy in enumerate(copies):
        copy.wait()
        total = sum(dot16(chosen[slot], held[k, slot], NT) for slot in range(slots))
        packed[k * capacity : (k + 1) * capacity, :] = total
        pivot[k * cap : (k + 1) * cap, :] = total[:cap]


def pack(place, ranks, left_fac, right_fac, capacity, grid_rows):
    slots, _, order, cap = left_fac.shape
    return pl.pallas_call(
        functools.partial(pack_kernel, capacity, grid_rows),
        out_shape=(
            jax.ShapeDtypeStruct((2 * capacity, order), jnp.float32),
            jax.ShapeDtypeStruct((2 * cap, order), jnp.float32),
        ),
        in_specs=[IN_SMEM, IN_SMEM, IN_HBM, IN_HBM],
        out_specs=(IN_VMEM, IN_VMEM),
        scratch_shapes=[pltpu.VMEM((2, slots, order, cap), jnp.bfloat16), pltpu.SemaphoreType.DMA((2,))],
        compiler_params=params(16),
        cost_estimate=cost(2**10, 2**10),
        name="pack",
    )(place, ranks, left_fac, right_fac)


def pick_kernel(count, index, *refs):
    candidates, target, sem = refs[:count], refs[count], refs[count + 1]
    wait = fetch(index[0], candidates, target, sem)
    pl.when(index[0] >= 0)(wait)


def pick(index, candidates):
    return pl.pallas_call(
        functools.partial(pick_kernel, len(candidates)),
        out_shape=jax.ShapeDtypeStruct(candidates[0].shape, candidates[0].dtype),
        in_specs=[IN_SMEM] + [ANYWHERE] * len(candidates),
        out_specs=ANYWHERE,
        scratch_shapes=[pltpu.SemaphoreType.DMA],
        compiler_params=params(4),
        cost_estimate=cost(2**32, 2**20),
        name="pick",
    )(jnp.reshape(index, (1,)).astype(jnp.int32), *candidates)


def rows_kernel(capacity, grid_rows, count, place, ranks, *refs):
    sources, weights, stacked = refs[: 2 * count], refs[2 * count : 2 * count + 2], refs[2 * count + 2]
    landed, inverses, weight_high, weight_low, sems = refs[2 * count + 3 :]
    order = inverses.shape[1]
    inverses_in = fetch(1 - place[0] % 2, weights, inverses, sems.at[4])
    slots = stacked.shape[0]
    cap = LANES
    waits = []
    for t in range(2):
        for k in range(2):
            part = [source.at[pl.ds(k * capacity, capacity)] for source in sources[t * count : (t + 1) * count]]
            waits.append(fetch(place[1], part, landed.at[2 * t + k, pl.ds(0, capacity)], sems.at[2 * t + k]))
            landed[2 * t + k, capacity:, :] = jnp.zeros((cap, order), jnp.float32)
    inverses_in()
    base_parts, second_parts = split2(inverses[: 2 * order, :]), split2(inverses[2 * order :, :])
    for wait in waits:
        wait()
    solved0 = sum(dot16(landed[1].astype(jnp.bfloat16), part, NT) for part in base_parts)
    solved1 = sum(dot16(landed[3].astype(jnp.bfloat16), part, NT) for part in second_parts)
    for column, value in ((0, solved0), (2 * order, solved1)):
        high, low = split2(value)
        weight_high[:, column : column + value.shape[1]] = high
        weight_low[:, column : column + value.shape[1]] = low
    live = lax.broadcasted_iota(jnp.int32, (cap, order), 0)
    for slot in range(slots):
        pieces = []
        for t in range(2):
            start, rank = segment(ranks, t, place[0], slot, slots, grid_rows)
            spot = pl.ds(pl.multiple_of(start, 16), cap)
            left = jnp.where(live < rank, landed[2 * t, spot, :], 0.0).astype(jnp.bfloat16)
            columns = pl.ds(0, 2 * order) if t == 0 else pl.ds(2 * order, order)
            weights = jnp.concatenate([weight_high[spot, columns], weight_low[spot, columns]], axis=0)
            pieces.append(dot16(jnp.concatenate([left, left], axis=0), weights, TN))
        for column, value in ((0, pieces[0][:, :order]), (order, pieces[0][:, order:] + pieces[1])):
            high, low = split2(value)
            stacked[slot, :, column : column + order] = high
            stacked[slot, :, 2 * order + column : 2 * order + column + order] = low
            stacked[slot, :, 4 * order + column : 4 * order + column + order] = high


def row_panels(place, ranks, firsts, seconds, inverses, capacity, slots, grid_rows):
    order = inverses[0].shape[1]
    count = len(firsts)
    return pl.pallas_call(
        functools.partial(rows_kernel, capacity, grid_rows, count),
        out_shape=jax.ShapeDtypeStruct((slots, order, 6 * order), jnp.bfloat16),
        in_specs=[IN_SMEM] * 2 + [ANYWHERE] * (2 * count + 2),
        out_specs=IN_VMEM,
        scratch_shapes=[
            pltpu.VMEM((4, capacity + LANES, order), jnp.float32),
            pltpu.VMEM((3 * order, order), jnp.float32),
            pltpu.VMEM((capacity + LANES, 3 * order), jnp.bfloat16),
            pltpu.VMEM((capacity + LANES, 3 * order), jnp.bfloat16),
            pltpu.SemaphoreType.DMA((5,)),
        ],
        compiler_params=params(20),
        cost_estimate=cost(2**10, 2**10),
        name="row_panels",
    )(place, ranks, *firsts, *seconds, *inverses)


def schur_kernel(capacity, grid_rows, grid_cols, place, ranks, *refs):
    spread = grid_rows // grid_cols
    sources = refs[: 4 * spread]
    weights, (rows, left, right, out) = refs[4 * spread : 4 * spread + 2], refs[4 * spread + 2 : 4 * spread + 6]
    landed, inverses, weight0, weight1, bases, panel, sems = refs[4 * spread + 6 :]
    slots, order, cap = out.shape[0], out.shape[2], left.shape[3]
    padded = landed.shape[1]
    used = padded - LANES
    step = pl.program_id(0)
    row_here, col_here = place[0], place[1]
    mine = row_here // grid_cols

    @pl.when(step == 0)
    def _():
        inverses_in = fetch(1 - row_here % 2, weights, inverses, sems.at[4 * spread])
        passed = (row_here ^ col_here) & 1
        waits = []
        for n in range(2 * spread):
            for k in range(2):
                part = [source.at[pl.ds(k * capacity, capacity)] for source in sources[2 * n : 2 * n + 2]]
                waits.append(fetch(passed, part, landed.at[2 * n + k, pl.ds(0, capacity)], sems.at[2 * n + k]))
                if padded > capacity:
                    landed[2 * n + k, capacity:, :] = jnp.zeros((padded - capacity, order), jnp.float32)
        inverses_in()
        base_parts, second_parts = split2(inverses[: 2 * order, :]), split2(inverses[2 * order :, :])
        for wait in waits:
            wait()
        for g in range(spread):
            right0 = landed[4 * g + 1, :used, :].astype(jnp.bfloat16)
            right1 = landed[4 * g + 3, :used, :].astype(jnp.bfloat16)
            solved0 = sum(dot16(part, right0, NT) for part in base_parts)
            solved1 = sum(dot16(part, right1, NT) for part in second_parts)
            for target, at, value in (
                (weight0, 2 * g, solved0[:order]),
                (weight1, 4 * g, solved0[order:]),
                (weight1, 4 * g + 2, solved1),
            ):
                for n, piece in enumerate(split2(value)):
                    target[at + n, :, :used] = piece
                    target[at + n, :, used:] = jnp.zeros((order, padded - used), jnp.bfloat16)

    tile_col = step * grid_cols + col_here
    last_row = (slots - 1) * grid_rows + row_here

    @pl.when((tile_col > 1) & (last_row > tile_col))
    def _():
        part = step % spread
        g = part ^ mine
        group = part * grid_cols + col_here
        span = 2 * LANES
        ids = lax.broadcasted_iota(jnp.int32, (span, order), 0)
        windows = []
        for t in range(2):
            start, count = segment(ranks, t, group, step // spread, slots, grid_rows)
            first_lane = start // LANES * LANES
            window = pl.ds(pl.multiple_of(first_lane, LANES), span)
            value = landed[4 * g + 2 * t, window, :]
            live = (ids >= start - first_lane) & (ids < start - first_lane + count)
            value = jnp.where(live, value, 0.0).astype(jnp.bfloat16)
            bases[t * span : (t + 1) * span, :] = value
            windows.append(window)
        panel0 = sum(dot16(weight0[2 * g + n, :, windows[0]], bases[:span], NN) for n in range(2))
        panel1 = sum(
            dot16(weight1[4 * g + n, :, windows[n // 2]], bases[n // 2 * span : (n // 2 + 1) * span], NN)
            for n in range(4)
        )
        for at, value in ((0, panel0), (order, panel1)):
            high, low = split2(value)
            panel[at : at + order, :] = high
            panel[2 * order + at : 3 * order + at, :] = high
            panel[4 * order + at : 5 * order + at, :] = low

    for slot in range(slots):
        tile_row = slot * grid_rows + row_here
        below = tile_row > tile_col

        @pl.when(jnp.logical_not(below))
        def _():
            out[slot, 0] = jnp.zeros((order, order), jnp.float32)

        for t in range(2):

            @pl.when(below & (tile_col == t))
            def _():
                high = rows[slot, :, t * order : (t + 1) * order].astype(jnp.float32)
                low = rows[slot, :, (t + 2) * order : (t + 3) * order].astype(jnp.float32)
                out[slot, 0] = high + low

        @pl.when(below & (tile_col > 1))
        def _():
            basis = left[slot, 0].astype(jnp.float32)
            live = lax.broadcasted_iota(jnp.int32, basis.shape, 1) < ranks[tile_row, tile_col]
            front = dot16(jnp.where(live, basis, 0.0).astype(jnp.bfloat16), right[slot, 0], NT)
            out[slot, 0] = front - dot16(rows[slot], panel[...], NN)


def schur(place, ranks, col_arrays, inverses, rows, left_fac, right_fac, capacity, grid_rows, grid_cols):
    slots, steps, order, cap = left_fac.shape
    spread = grid_rows // grid_cols
    padded = (-(-capacity // LANES) + 1) * LANES
    flat = [array for pair in col_arrays for array in pair]
    factor = pl.BlockSpec((slots, 1, order, cap), lambda m: (0, m, 0, 0))
    return pl.pallas_call(
        functools.partial(schur_kernel, capacity, grid_rows, grid_cols),
        grid=(steps,),
        out_shape=pltpu.HBM((slots, steps, order, order), jnp.float32),
        in_specs=[IN_SMEM] * 2 + [ANYWHERE] * (len(flat) + 2) + [IN_VMEM, factor, factor],
        out_specs=pl.BlockSpec((slots, 1, order, order), lambda m: (0, m, 0, 0)),
        scratch_shapes=[
            pltpu.VMEM((4 * spread, padded, order), jnp.float32),
            pltpu.VMEM((3 * order, order), jnp.float32),
            pltpu.VMEM((2 * spread, order, padded), jnp.bfloat16),
            pltpu.VMEM((4 * spread, order, padded), jnp.bfloat16),
            pltpu.VMEM((4 * LANES, order), jnp.bfloat16),
            pltpu.VMEM((6 * order, order), jnp.bfloat16),
            pltpu.SemaphoreType.DMA((4 * spread + 1,)),
        ],
        compiler_params=params(40, dimension_semantics=("arbitrary",)),
        cost_estimate=cost(2**33, 2**24),
        name="schur",
    )(place, ranks, *flat, *inverses, rows, left_fac, right_fac)


def after(array, *others):
    return lax.optimization_barrier((array, *others))[0]


def device_program(capacity, early, inverses, diag_tiles, left_fac, right_fac, ranks):
    grid_rows = lax.axis_size("row")
    grid_cols = lax.axis_size("col")
    row_here = lax.axis_index("row")
    col_here = lax.axis_index("col")
    row_slots, _, order, cap = left_fac.shape
    assert cap == LANES and grid_rows % grid_cols == 0 and grid_cols >= 2
    spread = grid_rows // grid_cols
    row_bits = grid_rows.bit_length() - 1
    low_bits = grid_cols.bit_length() - 1
    assert 1 << row_bits == grid_rows and 1 << low_bits == grid_cols
    every_row = range(grid_rows)
    every_col = range(grid_cols)
    place = jnp.stack([row_here, col_here]).astype(jnp.int32)

    def move(array, pairs):
        flat = [(r * grid_cols + c, s * grid_cols + d) for (r, c), (s, d) in pairs]
        return lax.ppermute(array, AXES, flat)

    def down_column(array, root, fences):
        held = [root]
        stages = []
        for bit in range(1, row_bits):
            step = 1 << bit
            got = move(array, [((r, c), (r ^ step, c)) for r in held for c in every_col])
            got = after(got, fences[min(bit, len(fences)) - 1])
            mine = row_here % 2 == root
            array = pick(jnp.where(mine & (row_here >> bit == 0), 0, jnp.where(mine & (row_here >> bit == 1), 1, -1)), [array, got])
            held = held + [r ^ step for r in held]
            stages.append(array)
        return stages

    def to_other_parity(array, root):
        return move(array, [((r, c), (r ^ 1, c)) for r in every_row if r % 2 == root for c in every_col])

    def chain_step(array, s):
        return move(array, [((r, c - 1), (r, c)) for c in (s, s + 1) if c < grid_cols for r in every_row])

    factoring = inverses is None
    if factoring:
        inverse0 = first_inverse(place, diag_tiles)
        passed = move(inverse0, [((0, c), (1, c)) for c in every_col])
    packed, pivot_bases = pack(place, ranks, left_fac, right_fac, capacity, grid_rows)
    back = move(packed, [((r, 1), (r, 0)) for r in every_row])
    chain = [packed]
    if factoring:
        received = [move(pivot_bases, [((1, 0), (1, c))]) for c in every_col if c]
        pivot_bases = jnp.where(col_here == 0, pivot_bases, sum(received))
        chain.append(chain_step(packed, 1))
        weights = second_inverse(place, ranks, diag_tiles, pivot_bases, passed)
        chain[1], weights = lax.optimization_barrier((chain[1], weights))
    else:
        chain.append(chain_step(packed, 1))

    for s in range(2, grid_cols):
        chain.append(chain_step(chain[s - 1], s))
    firsts = list(chain)
    seconds = [back] + chain[:-1]
    offset = (row_here ^ col_here) & (grid_cols - 1)

    def source(candidates):
        return pick(jnp.where(offset == 0, col_here, -1), candidates)

    second_source = source(seconds)

    def hop(array, bit, held):
        step = 1 << bit
        return move(
            array,
            [
                ((r + h * grid_cols, c), ((r + h * grid_cols) ^ step, c))
                for c in every_col
                for r in held[c]
                for h in range(spread)
            ],
        )

    def low_hops(have, *fence):
        held = {c: [c] for c in every_col}
        for bit in range(1, low_bits):
            got = hop(have, bit, held)
            got = after(got, *fence) if fence else got
            arrived = (offset >> bit == 1) & (offset & 1 == 0)
            stays = (offset >> bit == 0) & (offset & 1 == 0)
            have = pick(jnp.where(arrived, 1, jnp.where(stays, 0, -1)), [have, got])
            held = {c: held[c] + [r ^ (1 << bit) for r in held[c]] for c in every_col}
        return have

    def high_hops(have, *fence):
        held = {c: [r for r in range(grid_cols) if (r ^ c) % 2 == 0] for c in every_col}
        sets = [have]
        for bit in range(low_bits, row_bits):
            sets = sets + [hop(array, bit, held) for array in sets]
        sets = [after(array, *fence) if fence else array for array in sets]
        return [[array, hop(array, 0, held)] for array in sets]

    if factoring:
        stages = down_column(weights, 1, [chain[min(2, grid_cols - 1)], second_source])
        weights = stages[-1]
        inverses = [weights, to_other_parity(weights, 1)]
        firsts = [firsts[0], *[after(array, stages[0]) for array in firsts[1:]]]
    first_source = source(firsts)
    second_have = low_hops(second_source, first_source)
    first_have = low_hops(first_source)
    rows = row_panels(place, ranks, firsts, seconds, inverses, capacity, row_slots, grid_rows)
    second_sets, first_sets = high_hops(second_have, early), high_hops(first_have, rows)
    col_arrays = [sets[g] for g in range(spread) for sets in (first_sets, second_sets)]
    return schur(place, ranks, col_arrays, inverses, rows, left_fac, right_fac, capacity, grid_rows, grid_cols), inverses


def shards(diag_tiles, left_fac, right_fac, ranks):
    row_slots, cap = left_fac.shape[0], left_fac.shape[3]
    grid_rows = lax.axis_size("row")
    full = row_slots * cap
    packed = max(cap, full * 5 // 8)
    args = (diag_tiles, left_fac, right_fac, ranks)
    tile_ids = jnp.arange(ranks.shape[0], dtype=jnp.int32)[:, None]
    live = jnp.where(tile_ids > jnp.arange(2, dtype=jnp.int32)[None, :], ranks[:, :2], 0)
    widest = jnp.max(sum(live[s * grid_rows : (s + 1) * grid_rows] for s in range(row_slots)))
    result, inverses = device_program(packed, widest, None, *args)
    if packed == full:
        return result

    def again(state):
        return jnp.zeros_like(state[0]), device_program(full, state[0], inverses, *args)[0]

    return lax.while_loop(lambda state: state[0] > packed, again, (widest, result))[1]


def solution(mesh):
    in_specs = (P("row", None, None), P("row", "col", None, None), P("row", "col", None, None), P())
    out_specs = P("row", "col", None, None)
    return jax.shard_map(shards, mesh=mesh, in_specs=in_specs, out_specs=out_specs, check_vma=False)
```

```python
import functools

import jax
import jax.numpy as jnp
from jax import lax
from jax.experimental import pallas as pl
from jax.experimental.pallas import tpu as pltpu
from jax.sharding import PartitionSpec as P

PRECISE = lax.Precision.HIGHEST
AXES = ("row", "col")
BLOCK = 32
GROUP = 8
LANES = 128
NT = (((1,), (1,)), ((), ()))
TN = (((0,), (0,)), ((), ()))
NN = (((1,), (0,)), ((), ()))
ANYWHERE = pl.BlockSpec(memory_space=pl.ANY)
IN_VMEM = pl.BlockSpec(memory_space=pltpu.VMEM)
IN_SMEM = pl.BlockSpec(memory_space=pltpu.SMEM)
IN_HBM = pl.BlockSpec(memory_space=pltpu.HBM)
MEBI = 1024 * 1024


def dot32(lhs, rhs, dims):
    return lax.dot_general(lhs, rhs, dims, precision=PRECISE, preferred_element_type=jnp.float32)


def dot16(lhs, rhs, dims):
    return lax.dot_general(lhs, rhs, dims, preferred_element_type=jnp.float32)


def split2(value):
    high = value.astype(jnp.bfloat16)
    low = (value - high.astype(jnp.float32)).astype(jnp.bfloat16)
    return high, low


def params(mebibytes, **extra):
    return pltpu.CompilerParams(vmem_limit_bytes=mebibytes * MEBI, **extra)


def cost(flops, moved):
    return pl.CostEstimate(flops=int(flops), bytes_accessed=int(moved), transcendentals=0)


def eliminate(tiles):
    tiles, start = tiles
    rows = tiles[0].shape[0]
    done = []
    for first in range(0, rows, GROUP):
        height = rows - first
        row_ids = lax.broadcasted_iota(jnp.int32, (height, LANES), 0)
        heads = [
            jnp.broadcast_to(tiles[0][:, start + first + j : start + first + j + 1], (height, LANES))
            for j in range(GROUP)
        ]
        scale = jnp.zeros((GROUP, LANES), jnp.float32)
        for j in range(GROUP):
            pivot = heads[j][j : j + 1, :]
            factor = jnp.where(row_ids > j, heads[j] * (1.0 / pivot), 0.0)
            for other in range(j + 1, GROUP):
                heads[other] = heads[other] - factor * heads[other][j : j + 1, :]
            tiles = [tile - factor * tile[j : j + 1, :] for tile in tiles]
            root = lax.rsqrt(pivot)
            root = root * (1.5 - 0.5 * pivot * root * root)
            scale = jnp.where(row_ids[:GROUP] == j, root, scale)
        done.append([tile[:GROUP] * scale for tile in tiles])
        tiles = [tile[GROUP:] for tile in tiles]
    return [jnp.concatenate(parts, axis=0) for parts in zip(*done)]


def inverse_factor(source, work, result):
    order = source.shape[0]
    span = order // LANES
    for base in range(0, order, BLOCK):
        low = base // LANES
        row_ids = lax.broadcasted_iota(jnp.int32, (BLOCK, LANES), 0)
        lane_ids = lax.broadcasted_iota(jnp.int32, (BLOCK, LANES), 1)
        unit = jnp.where(lane_ids - base % LANES == row_ids, 1.0, 0.0)
        zero = jnp.zeros((BLOCK, LANES), jnp.float32)
        tiles = [source[base : base + BLOCK, s * LANES : (s + 1) * LANES] for s in range(low, span)]
        tiles += [zero] * low + [unit]
        if base:
            taken = dot32(
                work[0:base, base : base + BLOCK],
                work[0:base, low * LANES : order + (low + 1) * LANES],
                TN,
            )
            tiles = [tile - taken[:, s * LANES : (s + 1) * LANES] for s, tile in enumerate(tiles)]
        tiles = eliminate((tiles, base % LANES))
        for s, tile in enumerate(tiles):
            work[base : base + BLOCK, (low + s) * LANES : (low + s + 1) * LANES] = tile
        for s in range(low + 1, span):
            work[base : base + BLOCK, order + s * LANES : order + (s + 1) * LANES] = zero
    result[...] = work[:, order:]


def fetch(choice, candidates, target, sem):
    for n, candidate in enumerate(candidates):
        copy = pltpu.make_async_copy(candidate, target, sem)
        pl.when(choice == n)(copy.start)
    return pltpu.make_async_copy(candidates[0], target, sem).wait


def first_kernel(place, tiles, result, tile, work, sem):
    @pl.when(place[0] == 0)
    def _():
        copy = pltpu.make_async_copy(tiles.at[0], tile, sem)
        copy.start()
        copy.wait()
        inverse_factor(tile, work, result)


def first_inverse(place, tiles):
    order = tiles.shape[2]
    return pl.pallas_call(
        first_kernel,
        out_shape=jax.ShapeDtypeStruct((order, order), jnp.float32),
        in_specs=[IN_SMEM, IN_HBM],
        out_specs=IN_VMEM,
        scratch_shapes=[
            pltpu.VMEM((order, order), jnp.float32),
            pltpu.VMEM((order, 2 * order), jnp.float32),
            pltpu.SemaphoreType.DMA,
        ],
        compiler_params=params(8),
        cost_estimate=cost(2**33, 2**20),
        name="first_inverse",
    )(place, tiles)


def second_kernel(place, ranks, tiles, bases, inverse, weights, shifted, work, sem):
    order = inverse.shape[0]
    cap = bases.shape[0] // 2

    @pl.when(place[0] == 1)
    def _():
        copy = pltpu.make_async_copy(tiles.at[0], shifted, sem)
        copy.start()
        weights[:order, :] = inverse[...]
        live = lax.broadcasted_iota(jnp.int32, (cap, order), 0) < ranks[1, 0]
        left = jnp.where(live, bases[:cap, :], 0.0)
        right = jnp.where(live, bases[cap:, :], 0.0)
        solved = dot32(right, inverse[...], NT)
        dense = dot32(left, solved, TN)
        copy.wait()
        shifted[...] = shifted[...] - dot32(dense, dense, NT)
        inverse_factor(shifted, work, weights.at[pl.ds(2 * order, order)])
        weights[order : 2 * order, :] = -dot32(dot32(weights[2 * order :, :], dense, NN), inverse[...], NN)


def second_inverse(place, ranks, tiles, bases, inverse):
    order = inverse.shape[0]
    return pl.pallas_call(
        second_kernel,
        out_shape=jax.ShapeDtypeStruct((3 * order, order), jnp.float32),
        in_specs=[IN_SMEM, IN_SMEM, IN_HBM, IN_VMEM, IN_VMEM],
        out_specs=IN_VMEM,
        scratch_shapes=[
            pltpu.VMEM((order, order), jnp.float32),
            pltpu.VMEM((order, 2 * order), jnp.float32),
            pltpu.SemaphoreType.DMA,
        ],
        compiler_params=params(8),
        cost_estimate=cost(2**10, 2**10),
        name="second_inverse",
    )(place, ranks, tiles, bases, inverse)


def segment(ranks, panel, group, slot, slots, grid_rows):
    start, count = jnp.int32(0), jnp.int32(0)
    for s in range(slots):
        tile_row = s * grid_rows + group
        rank = jnp.where(tile_row > panel, ranks[tile_row, panel], 0)
        start = start + jnp.where(s < slot, rank, 0)
        count = count + jnp.where(s == slot, rank, 0)
    return start, count


def pack_kernel(capacity, grid_rows, place, ranks, left, right, packed, pivot, held, sem):
    slots, order, cap = held.shape[1:]
    copies = [
        pltpu.make_async_copy(source.at[:, 0], held.at[k], sem.at[k]) for k, source in enumerate((left, right))
    ]
    for copy in copies:
        copy.start()
    panel = jnp.minimum(place[1], 1)
    spot = lax.broadcasted_iota(jnp.int32, (capacity, cap), 0)
    column = lax.broadcasted_iota(jnp.int32, (capacity, cap), 1)
    chosen = []
    for slot in range(slots):
        start, count = segment(ranks, panel, place[0], slot, slots, grid_rows)
        hit = (spot - start == column) & (column < count)
        chosen.append(jnp.where(hit, 1.0, 0.0).astype(jnp.bfloat16))
    for k, copy in enumerate(copies):
        copy.wait()
        total = sum(dot16(chosen[slot], held[k, slot], NT) for slot in range(slots))
        packed[k * capacity : (k + 1) * capacity, :] = total
        pivot[k * cap : (k + 1) * cap, :] = total[:cap]


def pack(place, ranks, left_fac, right_fac, capacity, grid_rows):
    slots, _, order, cap = left_fac.shape
    return pl.pallas_call(
        functools.partial(pack_kernel, capacity, grid_rows),
        out_shape=(
            jax.ShapeDtypeStruct((2 * capacity, order), jnp.float32),
            jax.ShapeDtypeStruct((2 * cap, order), jnp.float32),
        ),
        in_specs=[IN_SMEM, IN_SMEM, IN_HBM, IN_HBM],
        out_specs=(IN_VMEM, IN_VMEM),
        scratch_shapes=[pltpu.VMEM((2, slots, order, cap), jnp.bfloat16), pltpu.SemaphoreType.DMA((2,))],
        compiler_params=params(16),
        cost_estimate=cost(2**10, 2**10),
        name="pack",
    )(place, ranks, left_fac, right_fac)


def pick_kernel(count, index, *refs):
    candidates, target, sem = refs[:count], refs[count], refs[count + 1]
    wait = fetch(index[0], candidates, target, sem)
    pl.when(index[0] >= 0)(wait)


def pick(index, candidates):
    return pl.pallas_call(
        functools.partial(pick_kernel, len(candidates)),
        out_shape=jax.ShapeDtypeStruct(candidates[0].shape, candidates[0].dtype),
        in_specs=[IN_SMEM] + [ANYWHERE] * len(candidates),
        out_specs=ANYWHERE,
        scratch_shapes=[pltpu.SemaphoreType.DMA],
        compiler_params=params(4),
        cost_estimate=cost(2**32, 2**20),
        name="pick",
    )(jnp.reshape(index, (1,)).astype(jnp.int32), *candidates)


def rows_kernel(capacity, grid_rows, count, place, ranks, *refs):
    sources, weights, stacked = refs[: 2 * count], refs[2 * count : 2 * count + 2], refs[2 * count + 2]
    landed, inverses, weight_high, weight_low, sems = refs[2 * count + 3 :]
    order = inverses.shape[1]
    inverses_in = fetch(1 - place[0] % 2, weights, inverses, sems.at[4])
    slots = stacked.shape[0]
    cap = LANES
    waits = []
    for t in range(2):
        for k in range(2):
            part = [source.at[pl.ds(k * capacity, capacity)] for source in sources[t * count : (t + 1) * count]]
            waits.append(fetch(place[1], part, landed.at[2 * t + k, pl.ds(0, capacity)], sems.at[2 * t + k]))
            landed[2 * t + k, capacity:, :] = jnp.zeros((cap, order), jnp.float32)
    inverses_in()
    base_parts, second_parts = split2(inverses[: 2 * order, :]), split2(inverses[2 * order :, :])
    for wait in waits:
        wait()
    solved0 = sum(dot16(landed[1].astype(jnp.bfloat16), part, NT) for part in base_parts)
    solved1 = sum(dot16(landed[3].astype(jnp.bfloat16), part, NT) for part in second_parts)
    for column, value in ((0, solved0), (2 * order, solved1)):
        high, low = split2(value)
        weight_high[:, column : column + value.shape[1]] = high
        weight_low[:, column : column + value.shape[1]] = low
    live = lax.broadcasted_iota(jnp.int32, (cap, order), 0)
    for slot in range(slots):
        pieces = []
        for t in range(2):
            start, rank = segment(ranks, t, place[0], slot, slots, grid_rows)
            spot = pl.ds(pl.multiple_of(start, 16), cap)
            left = jnp.where(live < rank, landed[2 * t, spot, :], 0.0).astype(jnp.bfloat16)
            columns = pl.ds(0, 2 * order) if t == 0 else pl.ds(2 * order, order)
            weights = jnp.concatenate([weight_high[spot, columns], weight_low[spot, columns]], axis=0)
            pieces.append(dot16(jnp.concatenate([left, left], axis=0), weights, TN))
        for column, value in ((0, pieces[0][:, :order]), (order, pieces[0][:, order:] + pieces[1])):
            high, low = split2(value)
            stacked[slot, :, column : column + order] = high
            stacked[slot, :, 2 * order + column : 2 * order + column + order] = low
            stacked[slot, :, 4 * order + column : 4 * order + column + order] = high


def row_panels(place, ranks, firsts, seconds, inverses, capacity, slots, grid_rows):
    order = inverses[0].shape[1]
    count = len(firsts)
    return pl.pallas_call(
        functools.partial(rows_kernel, capacity, grid_rows, count),
        out_shape=jax.ShapeDtypeStruct((slots, order, 6 * order), jnp.bfloat16),
        in_specs=[IN_SMEM] * 2 + [ANYWHERE] * (2 * count + 2),
        out_specs=IN_VMEM,
        scratch_shapes=[
            pltpu.VMEM((4, capacity + LANES, order), jnp.float32),
            pltpu.VMEM((3 * order, order), jnp.float32),
            pltpu.VMEM((capacity + LANES, 3 * order), jnp.bfloat16),
            pltpu.VMEM((capacity + LANES, 3 * order), jnp.bfloat16),
            pltpu.SemaphoreType.DMA((5,)),
        ],
        compiler_params=params(20),
        cost_estimate=cost(2**10, 2**10),
        name="row_panels",
    )(place, ranks, *firsts, *seconds, *inverses)


def schur_kernel(capacity, grid_rows, grid_cols, place, ranks, *refs):
    spread = grid_rows // grid_cols
    sources = refs[: 4 * spread]
    weights, (rows, left, right, out) = refs[4 * spread : 4 * spread + 2], refs[4 * spread + 2 : 4 * spread + 6]
    landed, inverses, weight0, weight1, bases, panel, sems = refs[4 * spread + 6 :]
    slots, order, cap = out.shape[0], out.shape[2], left.shape[3]
    padded = landed.shape[1]
    used = padded - LANES
    step = pl.program_id(0)
    row_here, col_here = place[0], place[1]
    mine = row_here // grid_cols

    @pl.when(step == 0)
    def _():
        inverses_in = fetch(1 - row_here % 2, weights, inverses, sems.at[4 * spread])
        passed = (row_here ^ col_here) & 1
        waits = []
        for n in range(2 * spread):
            for k in range(2):
                part = [source.at[pl.ds(k * capacity, capacity)] for source in sources[2 * n : 2 * n + 2]]
                waits.append(fetch(passed, part, landed.at[2 * n + k, pl.ds(0, capacity)], sems.at[2 * n + k]))
                if padded > capacity:
                    landed[2 * n + k, capacity:, :] = jnp.zeros((padded - capacity, order), jnp.float32)
        inverses_in()
        base_parts, second_parts = split2(inverses[: 2 * order, :]), split2(inverses[2 * order :, :])
        for wait in waits:
            wait()
        for g in range(spread):
            right0 = landed[4 * g + 1, :used, :].astype(jnp.bfloat16)
            right1 = landed[4 * g + 3, :used, :].astype(jnp.bfloat16)
            solved0 = sum(dot16(part, right0, NT) for part in base_parts)
            solved1 = sum(dot16(part, right1, NT) for part in second_parts)
            for target, at, value in (
                (weight0, 2 * g, solved0[:order]),
                (weight1, 4 * g, solved0[order:]),
                (weight1, 4 * g + 2, solved1),
            ):
                for n, piece in enumerate(split2(value)):
                    target[at + n, :, :used] = piece
                    target[at + n, :, used:] = jnp.zeros((order, padded - used), jnp.bfloat16)

    tile_col = step * grid_cols + col_here
    last_row = (slots - 1) * grid_rows + row_here

    @pl.when((tile_col > 1) & (last_row > tile_col))
    def _():
        part = step % spread
        g = part ^ mine
        group = part * grid_cols + col_here
        span = 2 * LANES
        ids = lax.broadcasted_iota(jnp.int32, (span, order), 0)
        windows = []
        for t in range(2):
            start, count = segment(ranks, t, group, step // spread, slots, grid_rows)
            first_lane = start // LANES * LANES
            window = pl.ds(pl.multiple_of(first_lane, LANES), span)
            value = landed[4 * g + 2 * t, window, :]
            live = (ids >= start - first_lane) & (ids < start - first_lane + count)
            value = jnp.where(live, value, 0.0).astype(jnp.bfloat16)
            bases[t * span : (t + 1) * span, :] = value
            windows.append(window)
        panel0 = sum(dot16(weight0[2 * g + n, :, windows[0]], bases[:span], NN) for n in range(2))
        panel1 = sum(
            dot16(weight1[4 * g + n, :, windows[n // 2]], bases[n // 2 * span : (n // 2 + 1) * span], NN)
            for n in range(4)
        )
        for at, value in ((0, panel0), (order, panel1)):
            high, low = split2(value)
            panel[at : at + order, :] = high
            panel[2 * order + at : 3 * order + at, :] = high
            panel[4 * order + at : 5 * order + at, :] = low

    for slot in range(slots):
        tile_row = slot * grid_rows + row_here
        below = tile_row > tile_col

        @pl.when(jnp.logical_not(below))
        def _():
            out[slot, 0] = jnp.zeros((order, order), jnp.float32)

        for t in range(2):

            @pl.when(below & (tile_col == t))
            def _():
                high = rows[slot, :, t * order : (t + 1) * order].astype(jnp.float32)
                low = rows[slot, :, (t + 2) * order : (t + 3) * order].astype(jnp.float32)
                out[slot, 0] = high + low

        @pl.when(below & (tile_col > 1))
        def _():
            basis = left[slot, 0].astype(jnp.float32)
            live = lax.broadcasted_iota(jnp.int32, basis.shape, 1) < ranks[tile_row, tile_col]
            front = dot16(jnp.where(live, basis, 0.0).astype(jnp.bfloat16), right[slot, 0], NT)
            out[slot, 0] = front - dot16(rows[slot], panel[...], NN)


def schur(place, ranks, col_arrays, inverses, rows, left_fac, right_fac, capacity, grid_rows, grid_cols):
    slots, steps, order, cap = left_fac.shape
    spread = grid_rows // grid_cols
    padded = (-(-capacity // LANES) + 1) * LANES
    flat = [array for pair in col_arrays for array in pair]
    factor = pl.BlockSpec((slots, 1, order, cap), lambda m: (0, m, 0, 0))
    return pl.pallas_call(
        functools.partial(schur_kernel, capacity, grid_rows, grid_cols),
        grid=(steps,),
        out_shape=pltpu.HBM((slots, steps, order, order), jnp.float32),
        in_specs=[IN_SMEM] * 2 + [ANYWHERE] * (len(flat) + 2) + [IN_VMEM, factor, factor],
        out_specs=pl.BlockSpec((slots, 1, order, order), lambda m: (0, m, 0, 0)),
        scratch_shapes=[
            pltpu.VMEM((4 * spread, padded, order), jnp.float32),
            pltpu.VMEM((3 * order, order), jnp.float32),
            pltpu.VMEM((2 * spread, order, padded), jnp.bfloat16),
            pltpu.VMEM((4 * spread, order, padded), jnp.bfloat16),
            pltpu.VMEM((4 * LANES, order), jnp.bfloat16),
            pltpu.VMEM((6 * order, order), jnp.bfloat16),
            pltpu.SemaphoreType.DMA((4 * spread + 1,)),
        ],
        compiler_params=params(40, dimension_semantics=("arbitrary",)),
        cost_estimate=cost(2**33, 2**24),
        name="schur",
    )(place, ranks, *flat, *inverses, rows, left_fac, right_fac)


def after(array, *others):
    return lax.optimization_barrier((array, *others))[0]


def device_program(capacity, early, inverses, diag_tiles, left_fac, right_fac, ranks):
    grid_rows = lax.axis_size("row")
    grid_cols = lax.axis_size("col")
    row_here = lax.axis_index("row")
    col_here = lax.axis_index("col")
    row_slots, _, order, cap = left_fac.shape
    assert cap == LANES and grid_rows % grid_cols == 0 and grid_cols >= 2
    spread = grid_rows // grid_cols
    row_bits = grid_rows.bit_length() - 1
    low_bits = grid_cols.bit_length() - 1
    assert 1 << row_bits == grid_rows and 1 << low_bits == grid_cols
    every_row = range(grid_rows)
    every_col = range(grid_cols)
    place = jnp.stack([row_here, col_here]).astype(jnp.int32)

    def move(array, pairs):
        flat = [(r * grid_cols + c, s * grid_cols + d) for (r, c), (s, d) in pairs]
        return lax.ppermute(array, AXES, flat)

    def down_column(array, root, fences):
        held = [root]
        stages = []
        for bit in range(1, row_bits):
            step = 1 << bit
            got = move(array, [((r, c), (r ^ step, c)) for r in held for c in every_col])
            got = after(got, fences[min(bit, len(fences)) - 1])
            mine = row_here % 2 == root
            array = pick(jnp.where(mine & (row_here >> bit == 0), 0, jnp.where(mine & (row_here >> bit == 1), 1, -1)), [array, got])
            held = held + [r ^ step for r in held]
            stages.append(array)
        return stages

    def to_other_parity(array, root):
        return move(array, [((r, c), (r ^ 1, c)) for r in every_row if r % 2 == root for c in every_col])

    def chain_step(array, s):
        return move(array, [((r, c - 1), (r, c)) for c in (s, s + 1) if c < grid_cols for r in every_row])

    factoring = inverses is None
    if factoring:
        inverse0 = first_inverse(place, diag_tiles)
        passed = move(inverse0, [((0, c), (1, c)) for c in every_col])
    packed, pivot_bases = pack(place, ranks, left_fac, right_fac, capacity, grid_rows)
    back = move(packed, [((r, 1), (r, 0)) for r in every_row])
    chain = [packed]
    if factoring:
        received = [move(pivot_bases, [((1, 0), (1, c))]) for c in every_col if c]
        pivot_bases = jnp.where(col_here == 0, pivot_bases, sum(received))
        chain.append(chain_step(packed, 1))
        chain[1] = after(chain[1], passed)
        weights = second_inverse(place, ranks, diag_tiles, after(pivot_bases, chain[1]), passed)
    else:
        chain.append(chain_step(packed, 1))

    for s in range(2, grid_cols):
        chain.append(chain_step(chain[s - 1], s))
    firsts = list(chain)
    seconds = [back] + chain[:-1]
    offset = (row_here ^ col_here) & (grid_cols - 1)

    def source(candidates):
        return pick(jnp.where(offset == 0, col_here, -1), candidates)

    second_source = source(seconds)

    def hop(array, bit, held):
        step = 1 << bit
        return move(
            array,
            [
                ((r + h * grid_cols, c), ((r + h * grid_cols) ^ step, c))
                for c in every_col
                for r in held[c]
                for h in range(spread)
            ],
        )

    def low_hops(have, *fence):
        held = {c: [c] for c in every_col}
        for bit in range(1, low_bits):
            got = hop(have, bit, held)
            got = after(got, *fence) if fence else got
            arrived = (offset >> bit == 1) & (offset & 1 == 0)
            stays = (offset >> bit == 0) & (offset & 1 == 0)
            have = pick(jnp.where(arrived, 1, jnp.where(stays, 0, -1)), [have, got])
            held = {c: held[c] + [r ^ (1 << bit) for r in held[c]] for c in every_col}
        return have

    def high_hops(have, *fence):
        held = {c: [r for r in range(grid_cols) if (r ^ c) % 2 == 0] for c in every_col}
        sets = [have]
        for bit in range(low_bits, row_bits):
            sets = sets + [hop(array, bit, held) for array in sets]
        sets = [after(array, *fence) if fence else array for array in sets]
        return [[array, hop(array, 0, held)] for array in sets]

    if factoring:
        stages = down_column(weights, 1, [chain[min(2, grid_cols - 1)], second_source])
        weights = stages[-1]
        inverses = [weights, to_other_parity(weights, 1)]
        firsts = [firsts[0], *[after(array, stages[0]) for array in firsts[1:]]]
    first_source = source(firsts)
    second_have = low_hops(second_source, first_source)
    first_have = low_hops(first_source)
    rows = row_panels(place, ranks, firsts, seconds, inverses, capacity, row_slots, grid_rows)
    second_sets, first_sets = high_hops(second_have, early), high_hops(first_have, rows)
    col_arrays = [sets[g] for g in range(spread) for sets in (first_sets, second_sets)]
    return schur(place, ranks, col_arrays, inverses, rows, left_fac, right_fac, capacity, grid_rows, grid_cols), inverses


def shards(diag_tiles, left_fac, right_fac, ranks):
    row_slots, cap = left_fac.shape[0], left_fac.shape[3]
    grid_rows = lax.axis_size("row")
    full = row_slots * cap
    packed = max(cap, full * 5 // 8)
    args = (diag_tiles, left_fac, right_fac, ranks)
    tile_ids = jnp.arange(ranks.shape[0], dtype=jnp.int32)[:, None]
    live = jnp.where(tile_ids > jnp.arange(2, dtype=jnp.int32)[None, :], ranks[:, :2], 0)
    widest = jnp.max(sum(live[s * grid_rows : (s + 1) * grid_rows] for s in range(row_slots)))
    result, inverses = device_program(packed, widest, None, *args)
    if packed == full:
        return result

    def again(state):
        return jnp.zeros_like(state[0]), device_program(full, state[0], inverses, *args)[0]

    return lax.while_loop(lambda state: state[0] > packed, again, (widest, result))[1]


def solution(mesh):
    in_specs = (P("row", None, None), P("row", "col", None, None), P("row", "col", None, None), P())
    out_specs = P("row", "col", None, None)
    return jax.shard_map(shards, mesh=mesh, in_specs=in_specs, out_specs=out_specs, check_vma=False)
```

```python
import functools

import jax
import jax.numpy as jnp
from jax import lax
from jax.experimental import pallas as pl
from jax.experimental.pallas import tpu as pltpu
from jax.sharding import PartitionSpec as P

PRECISE = lax.Precision.HIGHEST
AXES = ("row", "col")
BLOCK = 32
GROUP = 8
LANES = 128
NT = (((1,), (1,)), ((), ()))
TN = (((0,), (0,)), ((), ()))
NN = (((1,), (0,)), ((), ()))
ANYWHERE = pl.BlockSpec(memory_space=pl.ANY)
IN_VMEM = pl.BlockSpec(memory_space=pltpu.VMEM)
IN_SMEM = pl.BlockSpec(memory_space=pltpu.SMEM)
IN_HBM = pl.BlockSpec(memory_space=pltpu.HBM)
MEBI = 1024 * 1024


def dot32(lhs, rhs, dims):
    return lax.dot_general(lhs, rhs, dims, precision=PRECISE, preferred_element_type=jnp.float32)


def dot16(lhs, rhs, dims):
    return lax.dot_general(lhs, rhs, dims, preferred_element_type=jnp.float32)


def split2(value):
    high = value.astype(jnp.bfloat16)
    low = (value - high.astype(jnp.float32)).astype(jnp.bfloat16)
    return high, low


def params(mebibytes, **extra):
    return pltpu.CompilerParams(vmem_limit_bytes=mebibytes * MEBI, **extra)


def cost(flops, moved):
    return pl.CostEstimate(flops=int(flops), bytes_accessed=int(moved), transcendentals=0)


def eliminate(tiles):
    tiles, start = tiles
    rows = tiles[0].shape[0]
    done = []
    for first in range(0, rows, GROUP):
        height = rows - first
        row_ids = lax.broadcasted_iota(jnp.int32, (height, LANES), 0)
        heads = [
            jnp.broadcast_to(tiles[0][:, start + first + j : start + first + j + 1], (height, LANES))
            for j in range(GROUP)
        ]
        scale = jnp.zeros((GROUP, LANES), jnp.float32)
        for j in range(GROUP):
            pivot = heads[j][j : j + 1, :]
            factor = jnp.where(row_ids > j, heads[j] * (1.0 / pivot), 0.0)
            for other in range(j + 1, GROUP):
                heads[other] = heads[other] - factor * heads[other][j : j + 1, :]
            tiles = [tile - factor * tile[j : j + 1, :] for tile in tiles]
            root = lax.rsqrt(pivot)
            root = root * (1.5 - 0.5 * pivot * root * root)
            scale = jnp.where(row_ids[:GROUP] == j, root, scale)
        done.append([tile[:GROUP] * scale for tile in tiles])
        tiles = [tile[GROUP:] for tile in tiles]
    return [jnp.concatenate(parts, axis=0) for parts in zip(*done)]


def inverse_factor(source, work, result):
    order = source.shape[0]
    span = order // LANES
    for base in range(0, order, BLOCK):
        low = base // LANES
        row_ids = lax.broadcasted_iota(jnp.int32, (BLOCK, LANES), 0)
        lane_ids = lax.broadcasted_iota(jnp.int32, (BLOCK, LANES), 1)
        unit = jnp.where(lane_ids - base % LANES == row_ids, 1.0, 0.0)
        zero = jnp.zeros((BLOCK, LANES), jnp.float32)
        tiles = [source[base : base + BLOCK, s * LANES : (s + 1) * LANES] for s in range(low, span)]
        tiles += [zero] * low + [unit]
        if base:
            taken = dot32(
                work[0:base, base : base + BLOCK],
                work[0:base, low * LANES : order + (low + 1) * LANES],
                TN,
            )
            tiles = [tile - taken[:, s * LANES : (s + 1) * LANES] for s, tile in enumerate(tiles)]
        tiles = eliminate((tiles, base % LANES))
        for s, tile in enumerate(tiles):
            work[base : base + BLOCK, (low + s) * LANES : (low + s + 1) * LANES] = tile
        for s in range(low + 1, span):
            work[base : base + BLOCK, order + s * LANES : order + (s + 1) * LANES] = zero
    result[...] = work[:, order:]


def fetch(choice, candidates, target, sem):
    for n, candidate in enumerate(candidates):
        copy = pltpu.make_async_copy(candidate, target, sem)
        pl.when(choice == n)(copy.start)
    return pltpu.make_async_copy(candidates[0], target, sem).wait


def first_kernel(place, tiles, result, tile, work, sem):
    @pl.when(place[0] == 0)
    def _():
        copy = pltpu.make_async_copy(tiles.at[0], tile, sem)
        copy.start()
        copy.wait()
        inverse_factor(tile, work, result)


def first_inverse(place, tiles):
    order = tiles.shape[2]
    return pl.pallas_call(
        first_kernel,
        out_shape=jax.ShapeDtypeStruct((order, order), jnp.float32),
        in_specs=[IN_SMEM, IN_HBM],
        out_specs=IN_VMEM,
        scratch_shapes=[
            pltpu.VMEM((order, order), jnp.float32),
            pltpu.VMEM((order, 2 * order), jnp.float32),
            pltpu.SemaphoreType.DMA,
        ],
        compiler_params=params(8),
        cost_estimate=cost(2**33, 2**20),
        name="first_inverse",
    )(place, tiles)


def second_kernel(place, ranks, tiles, bases, inverse, weights, shifted, work, sem):
    order = inverse.shape[0]
    cap = bases.shape[0] // 2

    @pl.when(place[0] == 1)
    def _():
        copy = pltpu.make_async_copy(tiles.at[0], shifted, sem)
        copy.start()
        weights[:order, :] = inverse[...]
        live = lax.broadcasted_iota(jnp.int32, (cap, order), 0) < ranks[1, 0]
        left = jnp.where(live, bases[:cap, :], 0.0)
        right = jnp.where(live, bases[cap:, :], 0.0)
        solved = dot32(right, inverse[...], NT)
        dense = dot32(left, solved, TN)
        copy.wait()
        shifted[...] = shifted[...] - dot32(dense, dense, NT)
        inverse_factor(shifted, work, weights.at[pl.ds(2 * order, order)])
        weights[order : 2 * order, :] = -dot32(dot32(weights[2 * order :, :], dense, NN), inverse[...], NN)


def second_inverse(place, ranks, tiles, bases, inverse):
    order = inverse.shape[0]
    return pl.pallas_call(
        second_kernel,
        out_shape=jax.ShapeDtypeStruct((3 * order, order), jnp.float32),
        in_specs=[IN_SMEM, IN_SMEM, IN_HBM, IN_VMEM, IN_VMEM],
        out_specs=IN_VMEM,
        scratch_shapes=[
            pltpu.VMEM((order, order), jnp.float32),
            pltpu.VMEM((order, 2 * order), jnp.float32),
            pltpu.SemaphoreType.DMA,
        ],
        compiler_params=params(8),
        cost_estimate=cost(2**10, 2**10),
        name="second_inverse",
    )(place, ranks, tiles, bases, inverse)


def segment(ranks, panel, group, slot, slots, grid_rows):
    start, count = jnp.int32(0), jnp.int32(0)
    for s in range(slots):
        tile_row = s * grid_rows + group
        rank = jnp.where(tile_row > panel, ranks[tile_row, panel], 0)
        start = start + jnp.where(s < slot, rank, 0)
        count = count + jnp.where(s == slot, rank, 0)
    return start, count


def pack_kernel(capacity, grid_rows, place, ranks, left, right, packed, pivot, held, sem):
    slots, order, cap = held.shape[1:]
    copies = [
        pltpu.make_async_copy(source.at[:, 0], held.at[k], sem.at[k]) for k, source in enumerate((left, right))
    ]
    for copy in copies:
        copy.start()
    panel = jnp.minimum(place[1], 1)
    spot = lax.broadcasted_iota(jnp.int32, (capacity, cap), 0)
    column = lax.broadcasted_iota(jnp.int32, (capacity, cap), 1)
    chosen = []
    for slot in range(slots):
        start, count = segment(ranks, panel, place[0], slot, slots, grid_rows)
        hit = (spot - start == column) & (column < count)
        chosen.append(jnp.where(hit, 1.0, 0.0).astype(jnp.bfloat16))
    for k, copy in enumerate(copies):
        copy.wait()
        total = sum(dot16(chosen[slot], held[k, slot], NT) for slot in range(slots))
        packed[k * capacity : (k + 1) * capacity, :] = total
        pivot[k * cap : (k + 1) * cap, :] = total[:cap]


def pack(place, ranks, left_fac, right_fac, capacity, grid_rows):
    slots, _, order, cap = left_fac.shape
    return pl.pallas_call(
        functools.partial(pack_kernel, capacity, grid_rows),
        out_shape=(
            jax.ShapeDtypeStruct((2 * capacity, order), jnp.float32),
            jax.ShapeDtypeStruct((2 * cap, order), jnp.float32),
        ),
        in_specs=[IN_SMEM, IN_SMEM, IN_HBM, IN_HBM],
        out_specs=(IN_VMEM, IN_VMEM),
        scratch_shapes=[pltpu.VMEM((2, slots, order, cap), jnp.bfloat16), pltpu.SemaphoreType.DMA((2,))],
        compiler_params=params(16),
        cost_estimate=cost(2**10, 2**10),
        name="pack",
    )(place, ranks, left_fac, right_fac)


def pick_kernel(count, index, *refs):
    candidates, target, sem = refs[:count], refs[count], refs[count + 1]
    wait = fetch(index[0], candidates, target, sem)
    pl.when(index[0] >= 0)(wait)


def pick(index, candidates):
    return pl.pallas_call(
        functools.partial(pick_kernel, len(candidates)),
        out_shape=jax.ShapeDtypeStruct(candidates[0].shape, candidates[0].dtype),
        in_specs=[IN_SMEM] + [ANYWHERE] * len(candidates),
        out_specs=ANYWHERE,
        scratch_shapes=[pltpu.SemaphoreType.DMA],
        compiler_params=params(4),
        cost_estimate=cost(2**32, 2**20),
        name="pick",
    )(jnp.reshape(index, (1,)).astype(jnp.int32), *candidates)


def rows_kernel(capacity, grid_rows, count, place, ranks, *refs):
    sources, weights, stacked = refs[: 2 * count], refs[2 * count : 2 * count + 2], refs[2 * count + 2]
    landed, inverses, weight_high, weight_low, sems = refs[2 * count + 3 :]
    order = inverses.shape[1]
    inverses_in = fetch(1 - place[0] % 2, weights, inverses, sems.at[4])
    slots = stacked.shape[0]
    cap = LANES
    waits = []
    for t in range(2):
        for k in range(2):
            part = [source.at[pl.ds(k * capacity, capacity)] for source in sources[t * count : (t + 1) * count]]
            waits.append(fetch(place[1], part, landed.at[2 * t + k, pl.ds(0, capacity)], sems.at[2 * t + k]))
            landed[2 * t + k, capacity:, :] = jnp.zeros((cap, order), jnp.float32)
    inverses_in()
    base_parts, second_parts = split2(inverses[: 2 * order, :]), split2(inverses[2 * order :, :])
    for wait in waits:
        wait()
    solved0 = sum(dot16(landed[1].astype(jnp.bfloat16), part, NT) for part in base_parts)
    solved1 = sum(dot16(landed[3].astype(jnp.bfloat16), part, NT) for part in second_parts)
    for column, value in ((0, solved0), (2 * order, solved1)):
        high, low = split2(value)
        weight_high[:, column : column + value.shape[1]] = high
        weight_low[:, column : column + value.shape[1]] = low
    live = lax.broadcasted_iota(jnp.int32, (cap, order), 0)
    for slot in range(slots):
        pieces = []
        for t in range(2):
            start, rank = segment(ranks, t, place[0], slot, slots, grid_rows)
            spot = pl.ds(pl.multiple_of(start, 16), cap)
            left = jnp.where(live < rank, landed[2 * t, spot, :], 0.0).astype(jnp.bfloat16)
            columns = pl.ds(0, 2 * order) if t == 0 else pl.ds(2 * order, order)
            weights = jnp.concatenate([weight_high[spot, columns], weight_low[spot, columns]], axis=0)
            pieces.append(dot16(jnp.concatenate([left, left], axis=0), weights, TN))
        for column, value in ((0, pieces[0][:, :order]), (order, pieces[0][:, order:] + pieces[1])):
            high, low = split2(value)
            stacked[slot, :, column : column + order] = high
            stacked[slot, :, 2 * order + column : 2 * order + column + order] = low
            stacked[slot, :, 4 * order + column : 4 * order + column + order] = high


def row_panels(place, ranks, firsts, seconds, inverses, capacity, slots, grid_rows):
    order = inverses[0].shape[1]
    count = len(firsts)
    return pl.pallas_call(
        functools.partial(rows_kernel, capacity, grid_rows, count),
        out_shape=jax.ShapeDtypeStruct((slots, order, 6 * order), jnp.bfloat16),
        in_specs=[IN_SMEM] * 2 + [ANYWHERE] * (2 * count + 2),
        out_specs=IN_VMEM,
        scratch_shapes=[
            pltpu.VMEM((4, capacity + LANES, order), jnp.float32),
            pltpu.VMEM((3 * order, order), jnp.float32),
            pltpu.VMEM((capacity + LANES, 3 * order), jnp.bfloat16),
            pltpu.VMEM((capacity + LANES, 3 * order), jnp.bfloat16),
            pltpu.SemaphoreType.DMA((5,)),
        ],
        compiler_params=params(20),
        cost_estimate=cost(2**10, 2**10),
        name="row_panels",
    )(place, ranks, *firsts, *seconds, *inverses)


def schur_kernel(capacity, grid_rows, grid_cols, place, ranks, *refs):
    spread = grid_rows // grid_cols
    sources = refs[: 4 * spread]
    weights, (rows, left, right, out) = refs[4 * spread : 4 * spread + 2], refs[4 * spread + 2 : 4 * spread + 6]
    landed, inverses, weight0, weight1, bases, panel, sems = refs[4 * spread + 6 :]
    slots, order, cap = out.shape[0], out.shape[2], left.shape[3]
    padded = landed.shape[1]
    used = padded - LANES
    step = pl.program_id(0)
    row_here, col_here = place[0], place[1]
    mine = row_here // grid_cols

    @pl.when(step == 0)
    def _():
        inverses_in = fetch(1 - row_here % 2, weights, inverses, sems.at[4 * spread])
        passed = (row_here ^ col_here) & 1
        waits = []
        for n in range(2 * spread):
            for k in range(2):
                part = [source.at[pl.ds(k * capacity, capacity)] for source in sources[2 * n : 2 * n + 2]]
                waits.append(fetch(passed, part, landed.at[2 * n + k, pl.ds(0, capacity)], sems.at[2 * n + k]))
                if padded > capacity:
                    landed[2 * n + k, capacity:, :] = jnp.zeros((padded - capacity, order), jnp.float32)
        inverses_in()
        base_parts, second_parts = split2(inverses[: 2 * order, :]), split2(inverses[2 * order :, :])
        for wait in waits:
            wait()
        for g in range(spread):
            right0 = landed[4 * g + 1, :used, :].astype(jnp.bfloat16)
            right1 = landed[4 * g + 3, :used, :].astype(jnp.bfloat16)
            solved0 = sum(dot16(part, right0, NT) for part in base_parts)
            solved1 = sum(dot16(part, right1, NT) for part in second_parts)
            for target, at, value in (
                (weight0, 2 * g, solved0[:order]),
                (weight1, 4 * g, solved0[order:]),
                (weight1, 4 * g + 2, solved1),
            ):
                for n, piece in enumerate(split2(value)):
                    target[at + n, :, :used] = piece
                    target[at + n, :, used:] = jnp.zeros((order, padded - used), jnp.bfloat16)

    tile_col = step * grid_cols + col_here
    last_row = (slots - 1) * grid_rows + row_here

    @pl.when((tile_col > 1) & (last_row > tile_col))
    def _():
        part = step % spread
        g = part ^ mine
        group = part * grid_cols + col_here
        span = 2 * LANES
        ids = lax.broadcasted_iota(jnp.int32, (span, order), 0)
        windows = []
        for t in range(2):
            start, count = segment(ranks, t, group, step // spread, slots, grid_rows)
            first_lane = start // LANES * LANES
            window = pl.ds(pl.multiple_of(first_lane, LANES), span)
            value = landed[4 * g + 2 * t, window, :]
            live = (ids >= start - first_lane) & (ids < start - first_lane + count)
            value = jnp.where(live, value, 0.0).astype(jnp.bfloat16)
            bases[t * span : (t + 1) * span, :] = value
            windows.append(window)
        panel0 = sum(dot16(weight0[2 * g + n, :, windows[0]], bases[:span], NN) for n in range(2))
        panel1 = sum(
            dot16(weight1[4 * g + n, :, windows[n // 2]], bases[n // 2 * span : (n // 2 + 1) * span], NN)
            for n in range(4)
        )
        for at, value in ((0, panel0), (order, panel1)):
            high, low = split2(value)
            panel[at : at + order, :] = high
            panel[2 * order + at : 3 * order + at, :] = high
            panel[4 * order + at : 5 * order + at, :] = low

    for slot in range(slots):
        tile_row = slot * grid_rows + row_here
        below = tile_row > tile_col

        @pl.when(jnp.logical_not(below))
        def _():
            out[slot, 0] = jnp.zeros((order, order), jnp.float32)

        for t in range(2):

            @pl.when(below & (tile_col == t))
            def _():
                high = rows[slot, :, t * order : (t + 1) * order].astype(jnp.float32)
                low = rows[slot, :, (t + 2) * order : (t + 3) * order].astype(jnp.float32)
                out[slot, 0] = high + low

        @pl.when(below & (tile_col > 1))
        def _():
            basis = left[slot, 0].astype(jnp.float32)
            live = lax.broadcasted_iota(jnp.int32, basis.shape, 1) < ranks[tile_row, tile_col]
            front = dot16(jnp.where(live, basis, 0.0).astype(jnp.bfloat16), right[slot, 0], NT)
            out[slot, 0] = front - dot16(rows[slot], panel[...], NN)


def schur(place, ranks, col_arrays, inverses, rows, left_fac, right_fac, capacity, grid_rows, grid_cols):
    slots, steps, order, cap = left_fac.shape
    spread = grid_rows // grid_cols
    padded = (-(-capacity // LANES) + 1) * LANES
    flat = [array for pair in col_arrays for array in pair]
    factor = pl.BlockSpec((slots, 1, order, cap), lambda m: (0, m, 0, 0))
    return pl.pallas_call(
        functools.partial(schur_kernel, capacity, grid_rows, grid_cols),
        grid=(steps,),
        out_shape=pltpu.HBM((slots, steps, order, order), jnp.float32),
        in_specs=[IN_SMEM] * 2 + [ANYWHERE] * (len(flat) + 2) + [IN_VMEM, factor, factor],
        out_specs=pl.BlockSpec((slots, 1, order, order), lambda m: (0, m, 0, 0)),
        scratch_shapes=[
            pltpu.VMEM((4 * spread, padded, order), jnp.float32),
            pltpu.VMEM((3 * order, order), jnp.float32),
            pltpu.VMEM((2 * spread, order, padded), jnp.bfloat16),
            pltpu.VMEM((4 * spread, order, padded), jnp.bfloat16),
            pltpu.VMEM((4 * LANES, order), jnp.bfloat16),
            pltpu.VMEM((6 * order, order), jnp.bfloat16),
            pltpu.SemaphoreType.DMA((4 * spread + 1,)),
        ],
        compiler_params=params(40, dimension_semantics=("arbitrary",)),
        cost_estimate=cost(2**33, 2**24),
        name="schur",
    )(place, ranks, *flat, *inverses, rows, left_fac, right_fac)


def after(array, *others):
    return lax.optimization_barrier((array, *others))[0]


def device_program(capacity, early, inverses, diag_tiles, left_fac, right_fac, ranks):
    grid_rows = lax.axis_size("row")
    grid_cols = lax.axis_size("col")
    row_here = lax.axis_index("row")
    col_here = lax.axis_index("col")
    row_slots, _, order, cap = left_fac.shape
    assert cap == LANES and grid_rows % grid_cols == 0 and grid_cols >= 2
    spread = grid_rows // grid_cols
    row_bits = grid_rows.bit_length() - 1
    low_bits = grid_cols.bit_length() - 1
    assert 1 << row_bits == grid_rows and 1 << low_bits == grid_cols
    every_row = range(grid_rows)
    every_col = range(grid_cols)
    place = jnp.stack([row_here, col_here]).astype(jnp.int32)

    def move(array, pairs):
        flat = [(r * grid_cols + c, s * grid_cols + d) for (r, c), (s, d) in pairs]
        return lax.ppermute(array, AXES, flat)

    def down_column(array, root, fences):
        held = [root]
        stages = []
        for bit in range(1, row_bits):
            step = 1 << bit
            got = move(array, [((r, c), (r ^ step, c)) for r in held for c in every_col])
            got = after(got, fences[min(bit, len(fences)) - 1])
            mine = row_here % 2 == root
            array = pick(jnp.where(mine & (row_here >> bit == 0), 0, jnp.where(mine & (row_here >> bit == 1), 1, -1)), [array, got])
            held = held + [r ^ step for r in held]
            stages.append(array)
        return stages

    def to_other_parity(array, root):
        return move(array, [((r, c), (r ^ 1, c)) for r in every_row if r % 2 == root for c in every_col])

    def chain_step(array, s):
        return move(array, [((r, c - 1), (r, c)) for c in (s, s + 1) if c < grid_cols for r in every_row])

    factoring = inverses is None
    if factoring:
        inverse0 = first_inverse(place, diag_tiles)
        passed = move(inverse0, [((0, c), (1, c)) for c in every_col])
    packed, pivot_bases = pack(place, ranks, left_fac, right_fac, capacity, grid_rows)
    back = move(packed, [((r, 1), (r, 0)) for r in every_row])
    chain = [packed]
    if factoring:
        received = [move(pivot_bases, [((1, 0), (1, c))]) for c in every_col if c]
        pivot_bases = jnp.where(col_here == 0, pivot_bases, sum(received))
        chain.append(chain_step(packed, 1))
        chain[1] = after(chain[1], passed, pivot_bases)
        weights = second_inverse(place, ranks, diag_tiles, after(pivot_bases, chain[1]), passed)
    else:
        chain.append(chain_step(packed, 1))

    for s in range(2, grid_cols):
        chain.append(chain_step(chain[s - 1], s))
    firsts = list(chain)
    seconds = [back] + chain[:-1]
    offset = (row_here ^ col_here) & (grid_cols - 1)

    def source(candidates):
        return pick(jnp.where(offset == 0, col_here, -1), candidates)

    second_source = source(seconds)

    def hop(array, bit, held):
        step = 1 << bit
        return move(
            array,
            [
                ((r + h * grid_cols, c), ((r + h * grid_cols) ^ step, c))
                for c in every_col
                for r in held[c]
                for h in range(spread)
            ],
        )

    def low_hops(have, *fence):
        held = {c: [c] for c in every_col}
        for bit in range(1, low_bits):
            got = hop(have, bit, held)
            got = after(got, *fence) if fence else got
            arrived = (offset >> bit == 1) & (offset & 1 == 0)
            stays = (offset >> bit == 0) & (offset & 1 == 0)
            have = pick(jnp.where(arrived, 1, jnp.where(stays, 0, -1)), [have, got])
            held = {c: held[c] + [r ^ (1 << bit) for r in held[c]] for c in every_col}
        return have

    def high_hops(have, *fence):
        held = {c: [r for r in range(grid_cols) if (r ^ c) % 2 == 0] for c in every_col}
        sets = [have]
        for bit in range(low_bits, row_bits):
            sets = sets + [hop(array, bit, held) for array in sets]
        sets = [after(array, *fence) if fence else array for array in sets]
        return [[array, hop(array, 0, held)] for array in sets]

    if factoring:
        stages = down_column(weights, 1, [chain[min(2, grid_cols - 1)], second_source])
        weights = stages[-1]
        inverses = [weights, to_other_parity(weights, 1)]
        firsts = [firsts[0], *[after(array, stages[0]) for array in firsts[1:]]]
    first_source = source(firsts)
    second_have = low_hops(second_source, first_source)
    first_have = low_hops(first_source)
    rows = row_panels(place, ranks, firsts, seconds, inverses, capacity, row_slots, grid_rows)
    second_sets, first_sets = high_hops(second_have, early), high_hops(first_have, rows)
    col_arrays = [sets[g] for g in range(spread) for sets in (first_sets, second_sets)]
    return schur(place, ranks, col_arrays, inverses, rows, left_fac, right_fac, capacity, grid_rows, grid_cols), inverses


def shards(diag_tiles, left_fac, right_fac, ranks):
    row_slots, cap = left_fac.shape[0], left_fac.shape[3]
    grid_rows = lax.axis_size("row")
    full = row_slots * cap
    packed = max(cap, full * 5 // 8)
    args = (diag_tiles, left_fac, right_fac, ranks)
    tile_ids = jnp.arange(ranks.shape[0], dtype=jnp.int32)[:, None]
    live = jnp.where(tile_ids > jnp.arange(2, dtype=jnp.int32)[None, :], ranks[:, :2], 0)
    widest = jnp.max(sum(live[s * grid_rows : (s + 1) * grid_rows] for s in range(row_slots)))
    result, inverses = device_program(packed, widest, None, *args)
    if packed == full:
        return result

    def again(state):
        return jnp.zeros_like(state[0]), device_program(full, state[0], inverses, *args)[0]

    return lax.while_loop(lambda state: state[0] > packed, again, (widest, result))[1]


def solution(mesh):
    in_specs = (P("row", None, None), P("row", "col", None, None), P("row", "col", None, None), P())
    out_specs = P("row", "col", None, None)
    return jax.shard_map(shards, mesh=mesh, in_specs=in_specs, out_specs=out_specs, check_vma=False)
```
